256 devices in a mesh: dp: 64 (over z_hi, y, x), tensor: 4 (over z_lo, core).
Axes of the slice: x: 4, y: 4, z: 8 (z_hi: 4, z_lo: 2; z = z_hi * 2 + z_lo), core: 2. Of those that a mesh axis runs over, the one named last changes fastest.
Arguments:
- layer_input: bfloat16 [32768, 4096], P(('dp', 'tensor')), may hold values from -6 to 6
- out_grad: bfloat16 [32768, 4096], P(('dp', 'tensor')), may hold values from -6 to 6
- expert_ids: int32 [32768, 1], P(('dp', 'tensor')), may hold values from 0 to 63; in each aligned block of 128 rows (0 to 127, 128 to 255, ...) at most 3 rows name the same one
- gate_level: int32 [32768, 1], P(('dp', 'tensor')), may hold values from 1 to 8
- w_gate: bfloat16 [64, 4096, 1024], P('dp', None, 'tensor'), may hold values from -0.09375 to 0.09375
- w_up: bfloat16 [64, 4096, 1024], P('dp', None, 'tensor'), may hold values from -0.09375 to 0.09375
- w_down: bfloat16 [64, 1024, 4096], P('dp', 'tensor'), may hold values from -0.1875 to 0.1875
- attn_queries: bfloat16 [8192, 8192], P('dp', 'tensor'), may hold values from -36 to 36
- attn_keys: bfloat16 [8192, 512], P('dp', 'tensor'), may hold values from -12 to 12
- attn_values: bfloat16 [8192, 512], P('dp', 'tensor'), may hold values from -6 to 6
- attn_grad: bfloat16 [8192, 8192], P('dp', 'tensor'), may hold values from -6 to 6
Outputs:
- moe_out: bfloat16 [32768, 4096], P(('dp', 'tensor'))
- grad_x: bfloat16 [32768, 4096], P(('dp', 'tensor'))
- attn_out: bfloat16 [8192, 8192], P('dp', 'tensor')
- grad_q: bfloat16 [8192, 8192], P('dp', 'tensor')
- grad_k: bfloat16 [8192, 512], P('dp', 'tensor')
- grad_v: bfloat16 [8192, 512], P('dp', 'tensor')
The draws below stay inside these ranges and needn't reach their ends.
Inputs may be any that keep to these rules, and one draw needn't show every extreme that they name: `expert_ids`: each row names one expert; among the rows of one device (aligned blocks of 128 rows) no expert is named more than 3 times, a bound that some block reaches.
All inputs are finite; a program needn't handle non-finite values.
Results may differ from the reference program's by a relative error of at most 0.02.
Values may be sent and summed in bfloat16 or wider, within the bound.
No kernel may reach another device: no remote copies, remote signals or barrier semaphores. Data moves between devices by JAX's collectives and lax.ppermute only.
A program may use at most 128 MiB of HBM per device.

```python
import math
import jax
import jax.numpy as jnp
import numpy as np
from jax import lax

D = 4096
FF = 1024
HEADS = 64
KVH = 4
HD = 128
TOPK = 1
ATT_LEN = 128
TOK_SRC = 128
TOKENS = 32768
ATT_TOKENS = 8192
EXPERTS = 64
CAP = 3
N_TENSOR = 4


def shared_keys(key):
    return jnp.clip(jax.random.normal(key, (ATT_TOKENS, KVH * HD), jnp.float32), -4.0, 4.0)


def draw_attn_keys(key, part):
    base = shared_keys(key)
    return base.astype(jnp.bfloat16)


def draw_attn_queries(key, part):
    key = jax.random.fold_in(key, 7)
    fresh = jnp.clip(jax.random.normal(key, (ATT_TOKENS, HEADS * HD), jnp.float32), -4.0, 4.0)
    return fresh.astype(jnp.bfloat16)


def place_ends(values, stream_key, low, top_value):
    shape = values.shape
    spot = [jax.random.randint(jax.random.fold_in(stream_key, axis), (), 0, shape[axis]) for axis in range(len(shape))]
    values = values.at[tuple(spot)].set(low)
    longest = shape.index(max(shape))
    spot[longest] = (spot[longest] + 1) % shape[longest]
    return values.at[tuple(spot)].set(top_value)


def level_of(key, extent, pieces, least, largest):
    def one(dim, blocks):
        draws = jax.random.uniform(jax.random.fold_in(jax.random.fold_in(key, 6), dim), (blocks,), jnp.float32, least / len(pieces), largest / len(pieces))
        return jnp.repeat(jnp.exp(draws), extent[dim] // blocks).reshape((-1,) + (1,) * (len(extent) - dim - 1))

    level = one(*pieces[0])
    for cut in pieces[1:]:
        level = level * one(*cut)
    return level


def shared_out(rng, own, number, rows, amount, top, bound, lean):
    order = jax.random.permutation(rng, amount)
    packed, common = portions_of(amount, rows * top, bound, lean, True), portions_of(amount, rows * top, bound, lean, False)
    places = jnp.arange(amount)

    def named(lengths, turn):
        used = int((lengths > 0).sum())
        fixed = max(1, used // 4)
        shifted = fixed + (places - fixed + turn * (used - fixed)) % max(1, amount - fixed)
        return jnp.zeros((amount,), jnp.int32).at[order[jnp.where(places < fixed, places, shifted)]].set(jnp.asarray(lengths, jnp.int32))

    lengths = jnp.where(number % 4 == 0, named(packed, number // 4), named(common, number - number // 4 - 1))
    mixed = jax.random.permutation(jax.random.fold_in(own, 3), amount)
    source_of, sink = mixed[0:amount // 2 * 2:2], mixed[1:amount // 2 * 2:2]
    margin = jnp.minimum(lengths[source_of] - 1, bound - lengths[sink]) // 2
    margin = jnp.where((source_of == order[0]) | (sink == order[0]) | (lengths[sink] == 0), 0, jnp.maximum(margin, 0))
    shifted = jax.random.randint(jax.random.fold_in(own, 4), (amount // 2,), 0, 1 << 20) % (margin + 1)
    lengths = lengths.at[source_of].add(-shifted).at[sink].add(shifted)
    labels = jnp.searchsorted(jnp.cumsum(lengths), jnp.arange(rows * top), side="right").astype(jnp.int32)
    listing = labels.reshape(top, rows).T
    listing = listing[jax.random.permutation(jax.random.fold_in(own, 1), rows)]
    turn = jax.random.randint(jax.random.fold_in(own, 2), (rows, 1), 0, top)
    return jnp.take_along_axis(listing, (jnp.arange(top)[None, :] + turn) % top, axis=1)


def portions_of(number_of, total, bound, skew, full):
    weights = [(1 << 20) // math.isqrt(rank ** skew) + 1 for rank in range(1, number_of + 1)]
    largest = bound if full else min(bound, max(-(-total // number_of), total * weights[0] // sum(weights)))
    least = 1 if total - largest >= number_of - 1 else 0
    holding, rest = [largest] + [least] * (number_of - 1), total - largest - least * (number_of - 1)
    while rest > 0:
        movable = [i for i in range(1, number_of) if holding[i] < largest] or [i for i in range(1, number_of) if holding[i] < bound]
        mass, remaining = sum([weights[i] for i in movable]), rest
        for i in movable:
            more = min(bound - holding[i], max(1, remaining * weights[i] // mass), rest)
            holding[i] = holding[i] + more
            rest = rest - more
    return np.array(holding)


def scatter_about(stream_key, extent, scale, limit, pieces=(), kind=jnp.bfloat16):
    entries = jax.random.normal(stream_key, extent, jnp.float32) * scale
    if len(pieces) > 0:
        entries = level_of(stream_key, extent, pieces, -0.22, 0.18) * entries
    return jnp.clip(entries, min=-limit, max=limit).astype(kind)


def setup_inputs(seed: int = 0) -> dict:
    key_of = jax.random.split(jax.random.key(seed), 12)
    layer_input = scatter_about(key_of[0], (TOKENS, D), 1.0, 6.0, ((0, 256),))
    out_grad = scatter_about(key_of[1], (TOKENS, D), 1.0, 6.0, ((0, 256),))
    expert_ids_keys = jax.random.split(jax.random.fold_in(key_of[2], 1), TOKENS // TOK_SRC)
    expert_ids_turns = jax.random.permutation(jax.random.fold_in(key_of[2], 3), TOKENS // TOK_SRC)
    expert_ids = jax.vmap(lambda own, number: shared_out(jax.random.fold_in(key_of[2], 2), own, number, TOK_SRC, EXPERTS, TOPK, CAP, 2))(expert_ids_keys, expert_ids_turns).reshape((TOKENS, TOPK))
    gate_level = place_ends(jax.random.randint(key_of[3], (TOKENS, TOPK), 1, 9), jax.random.fold_in(key_of[3], 1), 1, 8).astype(jnp.int32)
    w_gate = scatter_about(key_of[4], (EXPERTS, D, FF), D ** -0.5, 0.09375, ((0, 64), (2, 4)))
    w_up = scatter_about(key_of[5], (EXPERTS, D, FF), D ** -0.5, 0.09375, ((0, 64), (2, 4)))
    w_down = scatter_about(key_of[6], (EXPERTS, FF, D), FF ** -0.5, 0.1875, ((0, 64), (1, 4)))
    attn_queries = draw_attn_queries(jax.random.fold_in(key_of[11], 71), 0)
    attn_keys = draw_attn_keys(jax.random.fold_in(key_of[11], 71), 0)
    attn_values = scatter_about(key_of[9], (ATT_TOKENS, KVH * HD), 1.0, 6.0, ((0, 64), (1, 4)))
    attn_grad = scatter_about(key_of[10], (ATT_TOKENS, HEADS * HD), 1.0, 6.0, ((0, 64), (1, 4)))
    return dict(layer_input=layer_input, out_grad=out_grad, expert_ids=expert_ids, gate_level=gate_level, w_gate=w_gate, w_up=w_up, w_down=w_down, attn_queries=attn_queries, attn_keys=attn_keys, attn_values=attn_values, attn_grad=attn_grad)


def attend(queries, keys, values):
    length = queries.shape[0]
    groups = keys.shape[1] // HD
    heads = queries.shape[1] // HD
    query_f = queries.astype(jnp.float32).reshape(length, groups, heads // groups, HD)
    key_f = keys.astype(jnp.float32).reshape(length, groups, HD)
    value_f = values.astype(jnp.float32).reshape(length, groups, HD)
    scores = jnp.einsum('tgrd,ugd->grtu', query_f, key_f) * HD ** (-0.5)
    causal_mask = jnp.arange(length)[:, None] >= jnp.arange(length)[None, :]
    scores = jnp.where(causal_mask, scores, -1e+30)
    top_score = lax.optimization_barrier(jnp.max(scores, axis=-1, keepdims=True))
    raised = jnp.exp(scores - top_score)
    weights = (raised / lax.optimization_barrier(jnp.sum(raised, axis=-1, keepdims=True))).astype(jnp.bfloat16)
    mixed = jnp.einsum('grtu,ugd->tgrd', weights.astype(jnp.float32), value_f)
    return mixed.reshape(length, heads * HD).astype(jnp.bfloat16)

def widen(values):
    return lax.optimization_barrier(values.astype(jnp.bfloat16)).astype(jnp.float32)

def expert_pass(rows, grad_rows, gate_w, up_w, down_w):
    group_width = gate_w.shape[1] // N_TENSOR
    gate_pre = jnp.dot(rows, gate_w, preferred_element_type=jnp.float32)
    up_pre = jnp.dot(rows, up_w, preferred_element_type=jnp.float32)
    sigma = jax.nn.sigmoid(gate_pre)
    activated = gate_pre * sigma
    hidden = (activated * up_pre).astype(jnp.bfloat16)
    contract = (((1,), (1,)), ((), ()))
    d_hidden = lax.dot_general(grad_rows, down_w, contract, preferred_element_type=jnp.float32)
    d_gate = (d_hidden * up_pre * sigma * (1.0 + gate_pre * (1.0 - sigma))).astype(jnp.bfloat16)
    d_up = (d_hidden * activated).astype(jnp.bfloat16)
    out_total = jnp.zeros((rows.shape[0], down_w.shape[1]), jnp.float32)
    grad_total = jnp.zeros((rows.shape[0], down_w.shape[1]), jnp.float32)
    for group in range(N_TENSOR):
        lower = group * group_width
        upper = lower + group_width
        out_total = out_total + widen(jnp.dot(hidden[:, lower:upper], down_w[lower:upper], preferred_element_type=jnp.float32))
        grad_term = lax.dot_general(d_gate[:, lower:upper], gate_w[:, lower:upper], contract, preferred_element_type=jnp.float32)
        grad_term = grad_term + lax.dot_general(d_up[:, lower:upper], up_w[:, lower:upper], contract, preferred_element_type=jnp.float32)
        grad_total = grad_total + widen(grad_term)
    return (out_total.astype(jnp.bfloat16), grad_total.astype(jnp.bfloat16))

def reference(layer_input, out_grad, expert_ids, gate_level, w_gate, w_up, w_down, attn_queries, attn_keys, attn_values, attn_grad):
    sources = TOKENS // TOK_SRC
    routes = TOK_SRC * TOPK
    block_ids = expert_ids.reshape(sources, routes).astype(jnp.int32)
    expert_hot = (block_ids[:, :, None] == jnp.arange(EXPERTS, dtype=jnp.int32)[None, None, :]).astype(jnp.int32)
    slot_rank = lax.optimization_barrier(jnp.sum((jnp.cumsum(expert_hot, axis=1) - expert_hot) * expert_hot, axis=2)).astype(jnp.int32)
    source_index = jnp.arange(sources, dtype=jnp.int32)[:, None]
    slot_index = (block_ids * (sources * CAP) + source_index * CAP + slot_rank).reshape(-1).astype(jnp.int32)
    token_index = (source_index * TOK_SRC + jnp.arange(routes, dtype=jnp.int32)[None, :] // TOPK).reshape(-1).astype(jnp.int32)
    slot_count = EXPERTS * sources * CAP
    token_table = jnp.full((slot_count,), TOKENS, jnp.int32).at[slot_index].set(token_index)
    gate_table = jnp.zeros((slot_count,), jnp.float32).at[slot_index].set(gate_level.reshape(-1).astype(jnp.float32) / 8.0)
    token_table = token_table.reshape(EXPERTS, sources * CAP)
    gate_table = gate_table.reshape(EXPERTS, sources * CAP)

    def one_expert(totals, inputs):
        out_acc, grad_acc = totals
        token_row, gate_row, gate_w, up_w, down_w = inputs
        safe_token = jnp.minimum(token_row, TOKENS - 1)
        live_slot = token_row < TOKENS
        rows = jnp.where(live_slot[:, None], layer_input[safe_token], jnp.zeros((), jnp.bfloat16))
        grad_rows = (gate_row[:, None] * out_grad[safe_token].astype(jnp.float32)).astype(jnp.bfloat16)
        out_rows, grad_rows_x = expert_pass(rows, grad_rows, gate_w, up_w, down_w)
        out_acc = out_acc.at[token_row].add(gate_row[:, None] * out_rows.astype(jnp.float32), mode='drop')
        grad_acc = grad_acc.at[token_row].add(grad_rows_x.astype(jnp.float32), mode='drop')
        return ((out_acc, grad_acc), None)
    start_totals = (jnp.zeros((TOKENS, D), jnp.float32), jnp.zeros((TOKENS, D), jnp.float32))
    (out_acc, grad_acc), unused = lax.scan(one_expert, start_totals, (token_table, gate_table, w_gate, w_up, w_down))
    moe_out = out_acc.astype(jnp.bfloat16)
    grad_x = grad_acc.astype(jnp.bfloat16)
    sequences = ATT_TOKENS // ATT_LEN

    def one_sequence(inputs):
        queries, keys, values, cotangent = inputs
        mixed, pull = jax.vjp(attend, queries, keys, values)
        grad_queries, grad_keys, grad_values = pull(cotangent)
        return (mixed, grad_queries, grad_keys, grad_values)
    attn_out, grad_q, grad_k, grad_v = lax.map(one_sequence, (attn_queries.reshape(sequences, ATT_LEN, HEADS * HD), attn_keys.reshape(sequences, ATT_LEN, KVH * HD), attn_values.reshape(sequences, ATT_LEN, KVH * HD), attn_grad.reshape(sequences, ATT_LEN, HEADS * HD)))
    attn_out = attn_out.reshape(ATT_TOKENS, HEADS * HD)
    grad_q = grad_q.reshape(ATT_TOKENS, HEADS * HD).astype(jnp.bfloat16)
    grad_k = grad_k.reshape(ATT_TOKENS, KVH * HD).astype(jnp.bfloat16)
    grad_v = grad_v.reshape(ATT_TOKENS, KVH * HD).astype(jnp.bfloat16)
    return (moe_out, grad_x, attn_out, grad_q, grad_k, grad_v)
```

```python
import functools

import jax
import jax.numpy as jnp
import numpy as np
from jax import lax
from jax.experimental import pallas as pl
from jax.experimental.pallas import tpu as pltpu
from jax.sharding import PartitionSpec as P

HD = 128
AXES = ("dp", "tensor")
SLOTS = 3
QUARTERS = 4
BLK = 48
VMEM_LIMIT = 40 * 1024 * 1024
BF = jnp.bfloat16
F32 = jnp.float32
NT = (((1,), (1,)), ((), ()))
TN = (((0,), (0,)), ((), ()))


def linear(x, y, z, core):
    return ((z // 2) * 16 + y * 4 + x) * 4 + (z % 2) * 2 + core


def moves(target):
    pairs = []
    for x in range(4):
        for y in range(4):
            for z in range(8):
                for core in range(2):
                    z_to, core_to = target(z, core)
                    pairs.append((linear(x, y, z, core), linear(x, y, z_to % 8, core_to)))
    return pairs


INNER = moves(lambda z, c: (z ^ 1, c))
CORES = moves(lambda z, c: (z, 1 - c))
NEAR = [
    moves(lambda z, c: (z - 2 if z % 2 else z + 2, c)),
    moves(lambda z, c: (z + 3 if z % 2 else z - 3, c)),
    moves(lambda z, c: (z + 1 if z % 2 else z - 1, c)),
]
BACK = [[(b, a) for a, b in perm] for perm in NEAR]
PLANES = [
    [linear(x, y, z, c) for y in range(4) for x in range(4)] for z in range(8) for c in range(2)
]


def send(value, perm):
    return lax.ppermute(value, AXES, perm)


def plane_exchange(value):
    return lax.all_to_all(value, AXES, 0, 0, axis_index_groups=PLANES, tiled=True)


def params(**more):
    return pltpu.CompilerParams(vmem_limit_bytes=VMEM_LIMIT, **more)


def cost(flops, nbytes):
    return pl.CostEstimate(flops=flops, bytes_accessed=nbytes, transcendentals=0)


def first_row(ids, rank, where):
    pair, odd = where[0], where[1]
    turn = ((ids >> 4) - pair) & 3
    turn = jnp.where(odd == 1, (4 - turn) & 3, turn)
    return (ids & 15) * BLK + turn * SLOTS + rank


def dispatch_kernel(where, ids_row, ids_col, level_row, x_ref, out_ref, *, scaled):
    tokens = ids_row.shape[1]
    ids = ids_row[...]
    earlier = lax.broadcasted_iota(jnp.int32, (tokens, tokens), 0) < lax.broadcasted_iota(
        jnp.int32, (tokens, tokens), 1
    )
    same = jnp.where(earlier & (ids_col[...] == ids), 1, 0)
    rank = jnp.sum(same, axis=0, keepdims=True)
    base = first_row(ids, rank, where)
    rows = out_ref.shape[0]
    width = out_ref.shape[1]
    row = lax.broadcasted_iota(jnp.int32, (rows, tokens), 0)
    if scaled:
        value = jnp.broadcast_to(level_row[...].astype(F32) * 0.125, (rows, tokens))
    else:
        value = jnp.full((rows, tokens), 1.0, F32)
    total = jnp.zeros((rows, width), F32)
    for q in range(QUARTERS):
        hot = jnp.where(row == base + q * (4 * SLOTS), value, 0.0).astype(BF)
        total = total + jnp.dot(
            hot, x_ref[:, q * width : (q + 1) * width], preferred_element_type=F32
        )
    out_ref[...] = total.astype(BF)


def dispatch(where, ids_row, ids_col, level_row, x, scaled):
    tokens, d = x.shape
    rows, width = 16 * BLK, d // QUARTERS
    vmem = pl.BlockSpec(memory_space=pltpu.VMEM)
    out = pl.pallas_call(
        functools.partial(dispatch_kernel, scaled=scaled),
        out_shape=jax.ShapeDtypeStruct((rows, width), BF),
        in_specs=[pl.BlockSpec(memory_space=pltpu.SMEM), vmem, vmem, vmem, vmem],
        out_specs=vmem,
        compiler_params=params(),
        cost_estimate=cost(2 * rows * tokens * d, 4 * rows * width),
        name="dispatch",
    )(where, ids_row, ids_col, level_row, x)
    return out.reshape(16, BLK, width)


def combine_kernel(where, ids_row, ids_col, level_col, back_ref, out_ref, *, scaled):
    q = pl.program_id(0)
    tokens = ids_row.shape[1]
    ids = ids_col[...]
    earlier = lax.broadcasted_iota(jnp.int32, (tokens, tokens), 1) < lax.broadcasted_iota(
        jnp.int32, (tokens, tokens), 0
    )
    same = jnp.where(earlier & (ids == ids_row[...]), 1, 0)
    rank = jnp.sum(same, axis=1, keepdims=True)
    base = first_row(ids, rank, where) + q * (4 * SLOTS)
    rows = back_ref.shape[0]
    row = lax.broadcasted_iota(jnp.int32, (tokens, rows), 1)
    if scaled:
        value = jnp.broadcast_to(level_col[...].astype(F32) * 0.125, (tokens, rows))
    else:
        value = jnp.full((tokens, rows), 1.0, F32)
    hot = jnp.where(row == base, value, 0.0).astype(BF)
    out_ref[...] = jnp.dot(hot, back_ref[...], preferred_element_type=F32).astype(BF)


def combine(where, ids_row, ids_col, level_col, back, scaled):
    back = back.reshape(-1, back.shape[-1])
    rows, width = back.shape
    tokens = ids_row.shape[1]
    fixed = lambda q: (0, 0)
    return pl.pallas_call(
        functools.partial(combine_kernel, scaled=scaled),
        out_shape=jax.ShapeDtypeStruct((tokens, QUARTERS * width), BF),
        grid=(QUARTERS,),
        in_specs=[
            pl.BlockSpec(memory_space=pltpu.SMEM),
            pl.BlockSpec((1, tokens), fixed),
            pl.BlockSpec((tokens, 1), fixed),
            pl.BlockSpec((tokens, 1), fixed),
            pl.BlockSpec((rows, width), fixed),
        ],
        out_specs=pl.BlockSpec((tokens, width), lambda q: (0, q)),
        compiler_params=params(),
        cost_estimate=cost(2 * rows * tokens * width * QUARTERS, 4 * rows * width),
        name="combine",
    )(where, ids_row, ids_col, level_col, back)


def shuffle_matrix():
    source, q, turn, slot = np.meshgrid(
        np.arange(16), np.arange(4), np.arange(4), np.arange(SLOTS), indexing="ij"
    )
    by_source = source * BLK + q * 12 + turn * SLOTS + slot
    by_turn = turn * 192 + q * BLK + source * SLOTS + slot
    matrix = np.zeros((768, 768), np.float32)
    matrix[by_turn.ravel(), by_source.ravel()] = 1.0
    return matrix


def shuffle_kernel(matrix, rows_ref, *outs):
    for turn, out in enumerate(outs):
        part = jnp.dot(
            matrix[turn * 192 : (turn + 1) * 192, :], rows_ref[...], preferred_element_type=F32
        )
        out[...] = part.astype(BF).reshape(out.shape)


def shuffle(rows):
    width = rows.shape[-1]
    flat = rows.reshape(768, width)
    vmem = pl.BlockSpec(memory_space=pltpu.VMEM)
    return pl.pallas_call(
        shuffle_kernel,
        out_shape=[jax.ShapeDtypeStruct((QUARTERS, BLK, width), BF)] * 4,
        in_specs=[vmem, vmem],
        out_specs=[vmem] * 4,
        compiler_params=params(),
        cost_estimate=cost(2 * 768 * 768 * width, 4 * 768 * width),
        name="shuffle",
    )(jnp.asarray(shuffle_matrix(), BF), flat)


def unshuffle_kernel(matrix, b0, b1, b2, b3, out_ref):
    total = None
    for turn, block in enumerate((b0, b1, b2, b3)):
        flat = block[...].reshape(192, block.shape[-1])
        part = jnp.dot(
            matrix[:, turn * 192 : (turn + 1) * 192], flat, preferred_element_type=F32
        )
        total = part if total is None else total + part
    out_ref[...] = total.astype(BF)


def unshuffle(blocks):
    width = blocks[0].shape[-1]
    vmem = pl.BlockSpec(memory_space=pltpu.VMEM)
    out = pl.pallas_call(
        unshuffle_kernel,
        out_shape=jax.ShapeDtypeStruct((768, width), BF),
        in_specs=[vmem] * 5,
        out_specs=vmem,
        compiler_params=params(),
        cost_estimate=cost(2 * 768 * 768 * width, 4 * 768 * width),
        name="unshuffle",
    )(jnp.asarray(shuffle_matrix().T, BF), *blocks)
    return out.reshape(16, BLK, width)


def gather_rows(blocks, rows):
    for i, block in enumerate(blocks):
        rows[i * BLK : (i + 1) * BLK, :] = block[0]


def store_rows(value, near, far):
    half = value.shape[0] // 2
    near[...] = value[:half].astype(BF).reshape(near.shape)
    far[...] = value[half:].astype(BF).reshape(far.shape)


def forward_kernel(*refs):
    blocks, (wg0, wg1, wu0, wu1, wd0, wd1, near, far, acts, rows, hidden) = refs[:8], refs[8:]
    step = pl.program_id(0)
    ff = wg0.shape[1]

    @pl.when(step < QUARTERS)
    def _():
        gather_rows(blocks, rows)
        for i, w in enumerate((wg0, wg1, wu0, wu1)):
            part = jnp.dot(rows[...], w[...], preferred_element_type=F32)
            cols = slice(i * ff, (i + 1) * ff)

            @pl.when(step == 0)
            def _():
                acts[:, cols] = part

            @pl.when(step > 0)
            def _():
                acts[:, cols] = acts[:, cols] + part

    @pl.when(step == QUARTERS)
    def _():
        gate = acts[:, : 2 * ff]
        hidden[...] = (gate * jax.nn.sigmoid(gate) * acts[:, 2 * ff :]).astype(BF)

    @pl.when(step >= QUARTERS)
    def _():
        value = jnp.dot(hidden[:, :ff], wd0[...], preferred_element_type=F32)
        value = value + jnp.dot(hidden[:, ff:], wd1[...], preferred_element_type=F32)
        store_rows(value, near, far)


def backward_kernel(*refs):
    blocks, (acts, wg0, wg1, wu0, wu1, wd0, wd1, near, far, rows, dh, dacts) = refs[:8], refs[8:]
    step = pl.program_id(0)
    ff = wg0.shape[1]

    @pl.when(step < QUARTERS)
    def _():
        gather_rows(blocks, rows)
        for i, w in enumerate((wd0, wd1)):
            part = lax.dot_general(rows[...], w[...], NT, preferred_element_type=F32)
            cols = slice(i * ff, (i + 1) * ff)

            @pl.when(step == 0)
            def _():
                dh[:, cols] = part

            @pl.when(step > 0)
            def _():
                dh[:, cols] = dh[:, cols] + part

    @pl.when(step == QUARTERS)
    def _():
        gate = acts[:, : 2 * ff]
        sigma = jax.nn.sigmoid(gate)
        d_hidden = dh[...]
        d_gate = d_hidden * acts[:, 2 * ff :] * sigma * (1.0 + gate * (1.0 - sigma))
        dacts[:, : 2 * ff] = d_gate.astype(BF)
        dacts[:, 2 * ff :] = (d_hidden * (gate * sigma)).astype(BF)

    @pl.when(step >= QUARTERS)
    def _():
        value = None
        for i, w in enumerate((wg0, wg1, wu0, wu1)):
            part = lax.dot_general(
                dacts[:, i * ff : (i + 1) * ff], w[...], NT, preferred_element_type=F32
            )
            value = part if value is None else value + part
        store_rows(value, near, far)


def first_pass(step):
    return jnp.minimum(step, QUARTERS - 1)


def second_pass(step):
    return jnp.maximum(step - QUARTERS, 0)


def expert_call(kernel, blocks, acts, weights, backward):
    wg, wu, wd = weights
    width = blocks[0].shape[-1]
    ff = wg[0].shape[1]
    rows = 8 * BLK
    up_pass, down_pass = (second_pass, first_pass) if backward else (first_pass, second_pass)
    row_spec = pl.BlockSpec((1, BLK, width), lambda s: (first_pass(s), 0, 0))
    up_spec = pl.BlockSpec((width, ff), lambda s: (up_pass(s), 0))
    down_spec = pl.BlockSpec((ff, width), lambda s: (0, down_pass(s)))
    act_spec = pl.BlockSpec((rows, 4 * ff), lambda s: (0, 0))
    out_spec = pl.BlockSpec((4, 1, BLK, width), lambda s: (0, second_pass(s), 0, 0))
    out_type = jax.ShapeDtypeStruct((4, QUARTERS, BLK, width), BF)
    act_type = jax.ShapeDtypeStruct((rows, 4 * ff), F32)
    in_specs = [row_spec] * 8 + ([act_spec] if backward else []) + [up_spec] * 4 + [down_spec] * 2
    scratch = [pltpu.VMEM((rows, width), BF)]
    if backward:
        scratch += [pltpu.VMEM((rows, 2 * ff), F32), pltpu.VMEM((rows, 4 * ff), BF)]
    else:
        scratch += [pltpu.VMEM((rows, 2 * ff), BF)]
    return pl.pallas_call(
        kernel,
        out_shape=[out_type, out_type] + ([] if backward else [act_type]),
        grid=(2 * QUARTERS,),
        in_specs=in_specs,
        out_specs=[out_spec, out_spec] + ([] if backward else [act_spec]),
        scratch_shapes=scratch,
        compiler_params=params(dimension_semantics=("arbitrary",)),
        cost_estimate=cost(12 * rows * width * QUARTERS * ff, 20 * 1024 * 1024),
        name="expert_backward" if backward else "expert_forward",
    )(*blocks, *([acts] if backward else []), *wg, *wu, *wd)


HEADS_STEP = 4


def attention_kernel(q_ref, k_ref, v_ref, do_ref, o_ref, dq_ref, dk_ref, dv_ref, dk_acc, dv_acc):
    step = pl.program_id(0)
    length = k_ref.shape[0]
    scale = HD ** (-0.5)
    k = k_ref[...]
    v = v_ref[...]
    causal = lax.broadcasted_iota(jnp.int32, (length, length), 0) >= lax.broadcasted_iota(
        jnp.int32, (length, length), 1
    )
    dk = None
    dv = None
    for h in range(HEADS_STEP):
        cols = slice(h * HD, (h + 1) * HD)
        q = q_ref[:, cols]
        do = do_ref[:, cols]
        scores = lax.dot_general(q, k, NT, preferred_element_type=F32) * scale
        scores = jnp.where(causal, scores, -1e30)
        raised = jnp.exp(scores - jnp.max(scores, axis=1, keepdims=True))
        probs = raised / jnp.sum(raised, axis=1, keepdims=True)
        rounded = probs.astype(BF)
        o_ref[:, cols] = jnp.dot(rounded, v, preferred_element_type=F32).astype(BF)
        d_probs = lax.dot_general(do, v, NT, preferred_element_type=F32).astype(BF).astype(F32)
        inner = jnp.sum(d_probs * probs, axis=1, keepdims=True)
        d_scores = (probs * (d_probs - inner) * scale).astype(BF)
        dq_ref[:, cols] = jnp.dot(d_scores, k, preferred_element_type=F32).astype(BF)
        dk_part = lax.dot_general(d_scores, q, TN, preferred_element_type=F32)
        dv_part = lax.dot_general(rounded, do, TN, preferred_element_type=F32)
        dk = dk_part if dk is None else dk + dk_part
        dv = dv_part if dv is None else dv + dv_part

    @pl.when(step == 0)
    def _():
        dk_acc[...] = dk
        dv_acc[...] = dv

    @pl.when(step > 0)
    def _():
        dk_acc[...] = dk_acc[...] + dk
        dv_acc[...] = dv_acc[...] + dv

    @pl.when(step == pl.num_programs(0) - 1)
    def _():
        dk_ref[...] = dk_acc[...].astype(BF)
        dv_ref[...] = dv_acc[...].astype(BF)


def attention(queries, keys, values, cotangent):
    length, wide = queries.shape
    head_spec = pl.BlockSpec((length, HEADS_STEP * HD), lambda s: (0, s))
    key_spec = pl.BlockSpec((length, HD), lambda s: (0, 0))
    heads = wide // HD
    return pl.pallas_call(
        attention_kernel,
        out_shape=[
            jax.ShapeDtypeStruct(queries.shape, BF),
            jax.ShapeDtypeStruct(queries.shape, BF),
            jax.ShapeDtypeStruct(keys.shape, BF),
            jax.ShapeDtypeStruct(values.shape, BF),
        ],
        grid=(heads // HEADS_STEP,),
        in_specs=[head_spec, key_spec, key_spec, head_spec],
        out_specs=[head_spec, head_spec, key_spec, key_spec],
        scratch_shapes=[pltpu.VMEM((length, HD), F32)] * 2,
        compiler_params=params(dimension_semantics=("arbitrary",)),
        cost_estimate=cost(14 * heads * length * length * HD, 10 * 1024 * 1024),
        name="attention",
    )(queries, keys, values, cotangent)


def spread(rows):
    own, *others = shuffle(rows)
    near = [own] + [send(block, perm) for block, perm in zip(others, NEAR)]
    far = [send(block, INNER) for block in near]
    return near + far


def collect(near, far):
    total = (near.astype(F32) + send(far, INNER).astype(F32)).astype(BF)
    blocks = [total[0]] + [send(total[i + 1], perm) for i, perm in enumerate(BACK)]
    return plane_exchange(unshuffle(blocks))


def on_device(
    layer_input,
    out_grad,
    expert_ids,
    gate_level,
    w_gate,
    w_up,
    w_down,
    attn_queries,
    attn_keys,
    attn_values,
    attn_grad,
):
    tokens = layer_input.shape[0]
    where = jnp.stack([lax.axis_index("dp") // 16, lax.axis_index("tensor") // 2]).astype(jnp.int32)
    ids_row = expert_ids.reshape(1, tokens)
    ids_col = expert_ids.reshape(tokens, 1)
    level_row = gate_level.reshape(1, tokens)
    level_col = gate_level.reshape(tokens, 1)

    weights = [(w[0], send(w[0], CORES)) for w in (w_gate, w_up, w_down)]

    x_rows = plane_exchange(dispatch(where, ids_row, ids_col, level_row, layer_input, False))
    x_blocks = spread(x_rows)
    g_rows = plane_exchange(dispatch(where, ids_row, ids_col, level_row, out_grad, True))
    g_blocks = spread(g_rows)

    attn_out, grad_q, grad_k, grad_v = attention(attn_queries, attn_keys, attn_values, attn_grad)

    out_near, out_far, acts = expert_call(forward_kernel, x_blocks, None, weights, False)
    out_back = collect(out_near, out_far)
    grad_near, grad_far = expert_call(backward_kernel, g_blocks, acts, weights, True)
    grad_back = collect(grad_near, grad_far)

    moe_out = combine(where, ids_row, ids_col, level_col, out_back, True)
    grad_x = combine(where, ids_row, ids_col, level_col, grad_back, False)
    return (moe_out, grad_x, attn_out, grad_q, grad_k, grad_v)


def solution(mesh):
    in_specs = (
        P(("dp", "tensor"), None),
        P(("dp", "tensor"), None),
        P(("dp", "tensor"), None),
        P(("dp", "tensor"), None),
        P("dp", None, "tensor"),
        P("dp", None, "tensor"),
        P("dp", "tensor", None),
        P("dp", "tensor"),
        P("dp", "tensor"),
        P("dp", "tensor"),
        P("dp", "tensor"),
    )
    out_specs = (
        P(("dp", "tensor"), None),
        P(("dp", "tensor"), None),
        P("dp", "tensor"),
        P("dp", "tensor"),
        P("dp", "tensor"),
        P("dp", "tensor"),
    )
    return jax.shard_map(
        on_device, mesh=mesh, in_specs=in_specs, out_specs=out_specs, check_vma=False
    )
```

```python
import functools

import jax
import jax.numpy as jnp
from jax import lax
from jax.experimental import pallas as pl
from jax.experimental.pallas import tpu as pltpu
from jax.sharding import PartitionSpec as P

HD = 128
AXES = ("dp", "tensor")
SLOTS = 3
QUARTERS = 4
BLK = 48
VMEM_LIMIT = 40 * 1024 * 1024
BF = jnp.bfloat16
F32 = jnp.float32
NT = (((1,), (1,)), ((), ()))
TN = (((0,), (0,)), ((), ()))


def linear(x, y, z, core):
    return ((z // 2) * 16 + y * 4 + x) * 4 + (z % 2) * 2 + core


def moves(target):
    pairs = []
    for x in range(4):
        for y in range(4):
            for z in range(8):
                for core in range(2):
                    z_to, core_to = target(z, core)
                    pairs.append((linear(x, y, z, core), linear(x, y, z_to % 8, core_to)))
    return pairs


INNER = moves(lambda z, c: (z ^ 1, c))
CORES = moves(lambda z, c: (z, 1 - c))
NEAR = [
    moves(lambda z, c: (z - 2 if z % 2 else z + 2, c)),
    moves(lambda z, c: (z + 3 if z % 2 else z - 3, c)),
    moves(lambda z, c: (z + 1 if z % 2 else z - 1, c)),
]
BACK = [[(b, a) for a, b in perm] for perm in NEAR]
PLANES = [
    [linear(x, y, z, c) for y in range(4) for x in range(4)] for z in range(8) for c in range(2)
]


def send(value, perm):
    return lax.ppermute(value, AXES, perm)


def plane_exchange(value):
    return lax.all_to_all(value, AXES, 0, 0, axis_index_groups=PLANES, tiled=True)


def params(**more):
    return pltpu.CompilerParams(vmem_limit_bytes=VMEM_LIMIT, **more)


WHOLE = pl.BlockSpec(memory_space=pltpu.VMEM)


def cost(flops, nbytes):
    return pl.CostEstimate(flops=flops, bytes_accessed=nbytes, transcendentals=0)


def first_row(ids, rank, where):
    pair, odd = where[0], where[1]
    turn = ((ids >> 4) - pair) & 3
    turn = jnp.where(odd == 1, (4 - turn) & 3, turn)
    return (ids & 15) * BLK + turn * SLOTS + rank


def dispatch_kernel(where, ids_row, ids_col, level_row, x_ref, out_ref, hot, quarters, *, scaled):
    tokens = ids_row.shape[1]
    ids = ids_row[...]
    earlier = lax.broadcasted_iota(jnp.int32, (tokens, tokens), 0) < lax.broadcasted_iota(
        jnp.int32, (tokens, tokens), 1
    )
    same = jnp.where(earlier & (ids_col[...] == ids), 1, 0)
    rank = jnp.sum(same, axis=0, keepdims=True)
    base = first_row(ids, rank, where)
    rows, width = out_ref.shape
    row = lax.broadcasted_iota(jnp.int32, (rows, tokens), 0)
    if scaled:
        value = jnp.broadcast_to(level_row[...].astype(F32) * 0.125, (rows, tokens))
    else:
        value = jnp.full((rows, tokens), 1.0, F32)
    for q in range(QUARTERS):
        part = slice(q * tokens, (q + 1) * tokens)
        hot[:, part] = jnp.where(row == base + q * (4 * SLOTS), value, 0.0).astype(BF)
        quarters[part, :] = x_ref[:, q * width : (q + 1) * width]
    out_ref[...] = jnp.dot(hot[...], quarters[...], preferred_element_type=F32).astype(BF)


def dispatch(where, ids_row, ids_col, level_row, x, scaled):
    tokens, d = x.shape
    rows, width = 16 * BLK, d // QUARTERS
    out = pl.pallas_call(
        functools.partial(dispatch_kernel, scaled=scaled),
        out_shape=jax.ShapeDtypeStruct((rows, width), BF),
        in_specs=[pl.BlockSpec(memory_space=pltpu.SMEM)] + [WHOLE] * 4,
        out_specs=WHOLE,
        scratch_shapes=[
            pltpu.VMEM((rows, QUARTERS * tokens), BF),
            pltpu.VMEM((QUARTERS * tokens, width), BF),
        ],
        compiler_params=params(),
        cost_estimate=cost(2 * rows * tokens * d, 4 * rows * width),
        name="dispatch",
    )(where, ids_row, ids_col, level_row, x)
    return out.reshape(16, BLK, width)


def combine_kernel(where, ids_row, ids_col, level_col, back_ref, out_ref, *, scaled):
    tokens = ids_row.shape[1]
    ids = ids_col[...]
    earlier = lax.broadcasted_iota(jnp.int32, (tokens, tokens), 1) < lax.broadcasted_iota(
        jnp.int32, (tokens, tokens), 0
    )
    same = jnp.where(earlier & (ids == ids_row[...]), 1, 0)
    rank = jnp.sum(same, axis=1, keepdims=True)
    base = first_row(ids, rank, where)
    rows, width = back_ref.shape
    row = lax.broadcasted_iota(jnp.int32, (tokens, rows), 1)
    if scaled:
        value = jnp.broadcast_to(level_col[...].astype(F32) * 0.125, (tokens, rows))
    else:
        value = jnp.full((tokens, rows), 1.0, F32)
    for q in range(QUARTERS):
        hot = jnp.where(row == base + q * (4 * SLOTS), value, 0.0).astype(BF)
        part = jnp.dot(hot, back_ref[...], preferred_element_type=F32)
        out_ref[:, q * width : (q + 1) * width] = part.astype(BF)


def combine(where, ids_row, ids_col, level_col, back, scaled):
    back = back.reshape(-1, back.shape[-1])
    rows, width = back.shape
    tokens = ids_row.shape[1]
    return pl.pallas_call(
        functools.partial(combine_kernel, scaled=scaled),
        out_shape=jax.ShapeDtypeStruct((tokens, QUARTERS * width), BF),
        in_specs=[pl.BlockSpec(memory_space=pltpu.SMEM)] + [WHOLE] * 4,
        out_specs=WHOLE,
        compiler_params=params(),
        cost_estimate=cost(2 * rows * tokens * width * QUARTERS, 4 * rows * width),
        name="combine",
    )(where, ids_row, ids_col, level_col, back)


def divide(value, by):
    return (value * ((1 << 20) // by + 1)) >> 20


def by_source_of(row):
    turn = divide(row, 192)
    rest = row - turn * 192
    quarter = divide(rest, BLK)
    rest = rest - quarter * BLK
    source = divide(rest, SLOTS)
    return source * BLK + quarter * (4 * SLOTS) + turn * SLOTS + rest - source * SLOTS


def by_turn_of(row):
    source = divide(row, BLK)
    rest = row - source * BLK
    quarter = divide(rest, 4 * SLOTS)
    rest = rest - quarter * (4 * SLOTS)
    turn = divide(rest, SLOTS)
    return turn * 192 + quarter * BLK + source * SLOTS + rest - turn * SLOTS


def one_hot(target, rows):
    row = lax.broadcasted_iota(jnp.int32, (rows, 1), 0)
    column = lax.broadcasted_iota(jnp.int32, (rows, rows), 1)
    return jnp.where(column == target(row), 1.0, 0.0).astype(BF)


def shuffle_kernel(rows_ref, *refs):
    outs, matrix = refs[:4], refs[4]
    matrix[...] = one_hot(by_source_of, matrix.shape[0])
    for turn, out in enumerate(outs):
        part = jnp.dot(
            matrix[turn * 192 : (turn + 1) * 192, :], rows_ref[...], preferred_element_type=F32
        )
        out[...] = part.astype(BF).reshape(out.shape)


def shuffle(rows):
    width = rows.shape[-1]
    return pl.pallas_call(
        shuffle_kernel,
        out_shape=[jax.ShapeDtypeStruct((QUARTERS, BLK, width), BF)] * 4,
        in_specs=[WHOLE],
        out_specs=[WHOLE] * 4,
        scratch_shapes=[pltpu.VMEM((768, 768), BF)],
        compiler_params=params(),
        cost_estimate=cost(2 * 768 * 768 * width, 4 * 768 * width),
        name="shuffle",
    )(rows.reshape(768, width))


def unshuffle_kernel(b0, b1, b2, b3, out_ref, matrix, rows):
    matrix[...] = one_hot(by_turn_of, matrix.shape[0])
    for turn, block in enumerate((b0, b1, b2, b3)):
        rows[turn * 192 : (turn + 1) * 192, :] = block[...].reshape(192, block.shape[-1])
    out_ref[...] = jnp.dot(matrix[...], rows[...], preferred_element_type=F32).astype(BF)


def unshuffle(blocks):
    width = blocks[0].shape[-1]
    out = pl.pallas_call(
        unshuffle_kernel,
        out_shape=jax.ShapeDtypeStruct((768, width), BF),
        in_specs=[WHOLE] * 4,
        out_specs=WHOLE,
        scratch_shapes=[pltpu.VMEM((768, 768), BF), pltpu.VMEM((768, width), BF)],
        compiler_params=params(),
        cost_estimate=cost(2 * 768 * 768 * width, 4 * 768 * width),
        name="unshuffle",
    )(*blocks)
    return out.reshape(16, BLK, width)


def gather_rows(blocks, rows):
    for i, block in enumerate(blocks):
        for q in range(QUARTERS):
            width = block.shape[-1]
            rows[i * BLK : (i + 1) * BLK, q * width : (q + 1) * width] = block[q]


def hidden_kernel(*refs):
    blocks, weights, (near, far, acts, rows) = refs[:8], refs[8:12], refs[12:]
    ff = weights[0].shape[1]
    half = near.shape[0]
    gather_rows(blocks, rows)
    for i, w in enumerate(weights):
        acts[:, i * ff : (i + 1) * ff] = jnp.dot(rows[...], w[...], preferred_element_type=F32)
    gate = acts[:, : 2 * ff]
    hidden = (gate * jax.nn.sigmoid(gate) * acts[:, 2 * ff :]).astype(BF)
    near[...] = hidden[:half]
    far[...] = hidden[half:]


def hidden_call(blocks, wg, wu):
    width = blocks[0].shape[-1]
    ff = wg[0].shape[1]
    rows = 8 * BLK
    part = jax.ShapeDtypeStruct((rows // 2, 2 * ff), BF)
    return pl.pallas_call(
        hidden_kernel,
        out_shape=[part, part, jax.ShapeDtypeStruct((rows, 4 * ff), F32)],
        in_specs=[WHOLE] * 12,
        out_specs=[WHOLE] * 3,
        scratch_shapes=[pltpu.VMEM((rows, QUARTERS * width), BF)],
        compiler_params=params(),
        cost_estimate=cost(8 * rows * width * QUARTERS * ff, 16 * 1024 * 1024),
        name="hidden",
    )(*blocks, *wg, *wu)


def d_hidden_kernel(*refs):
    blocks, weights, (mine, other, rows) = refs[:4], refs[4:8], refs[8:]
    ff = weights[0].shape[0]
    gather_rows(blocks, rows)
    for i, w in enumerate(weights):
        part = lax.dot_general(rows[...], w[...], NT, preferred_element_type=F32)
        out = (mine, other)[i // 2]
        out[:, (i % 2) * ff : (i % 2 + 1) * ff] = part.astype(out.dtype)


def d_hidden_call(blocks, wd):
    width = blocks[0].shape[-1]
    ff = wd[0].shape[0]
    rows = 4 * BLK
    return pl.pallas_call(
        d_hidden_kernel,
        out_shape=[
            jax.ShapeDtypeStruct((rows, 2 * ff), F32),
            jax.ShapeDtypeStruct((rows, 2 * ff), BF),
        ],
        in_specs=[WHOLE] * 8,
        out_specs=[WHOLE] * 2,
        scratch_shapes=[pltpu.VMEM((rows, QUARTERS * width), BF)],
        compiler_params=params(),
        cost_estimate=cost(8 * rows * width * QUARTERS * ff, 12 * 1024 * 1024),
        name="d_hidden",
    )(*blocks, *wd)


def store_blocks(value, outs, q):
    for i, out in enumerate(outs):
        out[q] = value[i * BLK : (i + 1) * BLK].astype(BF)


def out_kernel(near, other, wd0, wd1, wd2, wd3, *outs):
    ff = wd0.shape[0]
    width = outs[0].shape[-1]
    for q in range(QUARTERS):
        total = None
        for i, w in enumerate((wd0, wd1, wd2, wd3)):
            hidden = (near, other)[i // 2]
            part = jnp.dot(
                hidden[:, (i % 2) * ff : (i % 2 + 1) * ff],
                w[:, q * width : (q + 1) * width],
                preferred_element_type=F32,
            )
            total = part if total is None else total + part
        store_blocks(total, outs, q)


def out_call(near, other, wd):
    ff, d = wd[0].shape
    rows = near.shape[0]
    return pl.pallas_call(
        out_kernel,
        out_shape=[jax.ShapeDtypeStruct((QUARTERS, BLK, d // QUARTERS), BF)] * 4,
        in_specs=[WHOLE] * 6,
        out_specs=[WHOLE] * 4,
        compiler_params=params(),
        cost_estimate=cost(8 * rows * d * ff, 10 * 1024 * 1024),
        name="expert_out",
    )(near, other, *wd)


def grad_kernel(acts, dh, wg0, wg1, wu0, wu1, *refs, first):
    outs, dacts = refs[:4], refs[4]
    ff = wg0.shape[1]
    width = outs[0].shape[-1]
    rows = slice(first, first + dh.shape[0])
    gate = acts[rows, : 2 * ff]
    up = acts[rows, 2 * ff :]
    sigma = jax.nn.sigmoid(gate)
    d_hidden = dh[...].astype(F32)
    d_gate = d_hidden * up * sigma * (1.0 + gate * (1.0 - sigma))
    dacts[:, : 2 * ff] = d_gate.astype(BF)
    dacts[:, 2 * ff :] = (d_hidden * (gate * sigma)).astype(BF)
    for q in range(QUARTERS):
        total = None
        for i, w in enumerate((wg0, wg1, wu0, wu1)):
            part = lax.dot_general(
                dacts[:, i * ff : (i + 1) * ff],
                w[q * width : (q + 1) * width, :],
                NT,
                preferred_element_type=F32,
            )
            total = part if total is None else total + part
        store_blocks(total, outs, q)


def grad_call(acts, dh, wg, wu, first):
    d, ff = wg[0].shape
    rows = dh.shape[0]
    return pl.pallas_call(
        functools.partial(grad_kernel, first=first),
        out_shape=[jax.ShapeDtypeStruct((QUARTERS, BLK, d // QUARTERS), BF)] * 4,
        in_specs=[WHOLE] * 6,
        out_specs=[WHOLE] * 4,
        scratch_shapes=[pltpu.VMEM((rows, 4 * ff), BF)],
        compiler_params=params(),
        cost_estimate=cost(8 * rows * d * ff, 12 * 1024 * 1024),
        name="expert_grad",
    )(acts, dh, *wg, *wu)


HEADS_STEP = 4


def attention_kernel(q_ref, k_ref, v_ref, do_ref, o_ref, dq_ref, dk_ref, dv_ref, dk_acc, dv_acc):
    step = pl.program_id(0)
    length = k_ref.shape[0]
    scale = HD ** (-0.5)
    k = k_ref[...]
    v = v_ref[...]
    causal = lax.broadcasted_iota(jnp.int32, (length, length), 0) >= lax.broadcasted_iota(
        jnp.int32, (length, length), 1
    )
    dk = None
    dv = None
    for h in range(HEADS_STEP):
        cols = slice(h * HD, (h + 1) * HD)
        q = q_ref[:, cols]
        do = do_ref[:, cols]
        scores = lax.dot_general(q, k, NT, preferred_element_type=F32) * scale
        scores = jnp.where(causal, scores, -1e30)
        raised = jnp.exp(scores - jnp.max(scores, axis=1, keepdims=True))
        probs = raised / jnp.sum(raised, axis=1, keepdims=True)
        rounded = probs.astype(BF)
        o_ref[:, cols] = jnp.dot(rounded, v, preferred_element_type=F32).astype(BF)
        d_probs = lax.dot_general(do, v, NT, preferred_element_type=F32).astype(BF).astype(F32)
        inner = jnp.sum(d_probs * probs, axis=1, keepdims=True)
        d_scores = (probs * (d_probs - inner) * scale).astype(BF)
        dq_ref[:, cols] = jnp.dot(d_scores, k, preferred_element_type=F32).astype(BF)
        dk_part = lax.dot_general(d_scores, q, TN, preferred_element_type=F32)
        dv_part = lax.dot_general(rounded, do, TN, preferred_element_type=F32)
        dk = dk_part if dk is None else dk + dk_part
        dv = dv_part if dv is None else dv + dv_part

    @pl.when(step == 0)
    def _():
        dk_acc[...] = dk
        dv_acc[...] = dv

    @pl.when(step > 0)
    def _():
        dk_acc[...] = dk_acc[...] + dk
        dv_acc[...] = dv_acc[...] + dv

    @pl.when(step == pl.num_programs(0) - 1)
    def _():
        dk_ref[...] = dk_acc[...].astype(BF)
        dv_ref[...] = dv_acc[...].astype(BF)


def attention(queries, keys, values, cotangent):
    length, wide = queries.shape
    head_spec = pl.BlockSpec((length, HEADS_STEP * HD), lambda s: (0, s))
    key_spec = pl.BlockSpec((length, HD), lambda s: (0, 0))
    heads = wide // HD
    return pl.pallas_call(
        attention_kernel,
        out_shape=[
            jax.ShapeDtypeStruct(queries.shape, BF),
            jax.ShapeDtypeStruct(queries.shape, BF),
            jax.ShapeDtypeStruct(keys.shape, BF),
            jax.ShapeDtypeStruct(values.shape, BF),
        ],
        grid=(heads // HEADS_STEP,),
        in_specs=[head_spec, key_spec, key_spec, head_spec],
        out_specs=[head_spec, head_spec, key_spec, key_spec],
        scratch_shapes=[pltpu.VMEM((length, HD), F32)] * 2,
        compiler_params=params(dimension_semantics=("arbitrary",)),
        cost_estimate=cost(14 * heads * length * length * HD, 10 * 1024 * 1024),
        name="attention",
    )(queries, keys, values, cotangent)


def to_near(blocks):
    own, *others = blocks
    return [own] + [send(block, perm) for block, perm in zip(others, NEAR)]


def to_sources(blocks):
    back = [blocks[0]] + [send(block, perm) for block, perm in zip(blocks[1:], BACK)]
    return plane_exchange(unshuffle(back))


def on_device(
    layer_input,
    out_grad,
    expert_ids,
    gate_level,
    w_gate,
    w_up,
    w_down,
    attn_queries,
    attn_keys,
    attn_values,
    attn_grad,
):
    tokens = layer_input.shape[0]
    where = jnp.stack([lax.axis_index("dp") // 16, lax.axis_index("tensor") // 2]).astype(jnp.int32)
    ids_row = expert_ids.reshape(1, tokens)
    ids_col = expert_ids.reshape(tokens, 1)
    level_row = gate_level.reshape(1, tokens)
    level_col = gate_level.reshape(tokens, 1)

    down = w_down[0]
    down_other = send(down, INNER)
    wg = (w_gate[0], send(w_gate[0], CORES))
    wu = (w_up[0], send(w_up[0], CORES))
    wd = (down, send(down, CORES), down_other, send(down_other, CORES))

    x_sent = dispatch(where, ids_row, ids_col, level_row, layer_input, False)
    g_sent = dispatch(where, ids_row, ids_col, level_row, out_grad, True)
    x_rows = plane_exchange(x_sent)
    attended = attention(attn_queries, attn_keys, attn_values, attn_grad)
    x_rows, g_sent, attended = lax.optimization_barrier((x_rows, g_sent, attended))
    g_rows = plane_exchange(g_sent)

    x_near = to_near(shuffle(x_rows))
    g_blocks = shuffle(g_rows)
    x_near[2], g_blocks = lax.optimization_barrier((x_near[2], g_blocks))
    g_near = to_near(g_blocks)
    x_far = [send(block, INNER) for block in x_near]

    hidden_near, hidden_far, acts = hidden_call(x_near + x_far, wg, wu)
    hidden_other = send(hidden_far, INNER)
    dh_near, dh_far = d_hidden_call(g_near, wd)
    dh_other = send(dh_far, INNER)

    half = dh_near.shape[0]
    far_terms = grad_call(acts, dh_other, wg, wu, half)
    arrived = [send(block, INNER) for block in far_terms]
    out_blocks = out_call(hidden_near, hidden_other, wd)
    near_terms = grad_call(acts, dh_near, wg, wu, 0)
    grad_blocks = [
        (a.astype(F32) + b.astype(F32)).astype(BF) for a, b in zip(near_terms, arrived)
    ]
    out_back = to_sources(out_blocks)
    grad_back = to_sources(grad_blocks)

    moe_out = combine(where, ids_row, ids_col, level_col, out_back, True)
    grad_x = combine(where, ids_row, ids_col, level_col, grad_back, False)
    attn_out, grad_q, grad_k, grad_v = attended
    return (moe_out, grad_x, attn_out, grad_q, grad_k, grad_v)


def solution(mesh):
    in_specs = (
        P(("dp", "tensor"), None),
        P(("dp", "tensor"), None),
        P(("dp", "tensor"), None),
        P(("dp", "tensor"), None),
        P("dp", None, "tensor"),
        P("dp", None, "tensor"),
        P("dp", "tensor", None),
        P("dp", "tensor"),
        P("dp", "tensor"),
        P("dp", "tensor"),
        P("dp", "tensor"),
    )
    out_specs = (
        P(("dp", "tensor"), None),
        P(("dp", "tensor"), None),
        P("dp", "tensor"),
        P("dp", "tensor"),
        P("dp", "tensor"),
        P("dp", "tensor"),
    )
    return jax.shard_map(
        on_device, mesh=mesh, in_specs=in_specs, out_specs=out_specs, check_vma=False
    )
```

```python
import functools

import jax
import jax.numpy as jnp
from jax import lax
from jax.experimental import pallas as pl
from jax.experimental.pallas import tpu as pltpu
from jax.sharding import PartitionSpec as P

HD = 128
AXES = ("dp", "tensor")
DOWN_CUTS = (80, 192)
SLOTS = 3
QUARTERS = 4
BLK = 48
VMEM_LIMIT = 40 * 1024 * 1024
BF = jnp.bfloat16
F32 = jnp.float32
NT = (((1,), (1,)), ((), ()))
TN = (((0,), (0,)), ((), ()))


def linear(x, y, z, core):
    return ((z // 2) * 16 + y * 4 + x) * 4 + (z % 2) * 2 + core


def moves(target):
    pairs = []
    for x in range(4):
        for y in range(4):
            for z in range(8):
                for core in range(2):
                    z_to, core_to = target(z, core)
                    pairs.append((linear(x, y, z, core), linear(x, y, z_to % 8, core_to)))
    return pairs


INNER = moves(lambda z, c: (z ^ 1, c))
CORES = moves(lambda z, c: (z, 1 - c))
NEAR = [
    moves(lambda z, c: (z - 2 if z % 2 else z + 2, c)),
    moves(lambda z, c: (z + 3 if z % 2 else z - 3, c)),
    moves(lambda z, c: (z + 1 if z % 2 else z - 1, c)),
]
BACK = [[(b, a) for a, b in perm] for perm in NEAR]
PLANES = [
    [linear(x, y, z, c) for y in range(4) for x in range(4)] for z in range(8) for c in range(2)
]


def send(value, perm):
    return lax.ppermute(value, AXES, perm)


def plane_exchange(value):
    return lax.all_to_all(value, AXES, 0, 0, axis_index_groups=PLANES, tiled=True)


def params(**more):
    return pltpu.CompilerParams(vmem_limit_bytes=VMEM_LIMIT, **more)


WHOLE = pl.BlockSpec(memory_space=pltpu.VMEM)


def cost(flops, nbytes):
    return pl.CostEstimate(flops=flops, bytes_accessed=nbytes, transcendentals=0)


def first_row(ids, rank, where, by_pair):
    pair, odd = where[0], where[1]
    turn = ((ids >> 4) - pair) & 3
    turn = jnp.where(odd == 1, (4 - turn) & 3, turn)
    if by_pair:
        return turn * (4 * BLK) + (ids & 15) * SLOTS + rank
    return (ids & 15) * BLK + turn * SLOTS + rank


def quarter_step(by_pair):
    return BLK if by_pair else 4 * SLOTS


def dispatch_kernel(where, ids_row, ids_col, level_row, x_ref, *refs, scaled, by_pair):
    outs, (hot, quarters) = refs[:-2], refs[-2:]
    tokens = ids_row.shape[1]
    ids = ids_row[...]
    earlier = lax.broadcasted_iota(jnp.int32, (tokens, tokens), 0) < lax.broadcasted_iota(
        jnp.int32, (tokens, tokens), 1
    )
    same = jnp.where(earlier & (ids_col[...] == ids), 1, 0)
    rank = jnp.sum(same, axis=0, keepdims=True)
    base = first_row(ids, rank, where, by_pair)
    rows, width = hot.shape[0], quarters.shape[1]
    row = lax.broadcasted_iota(jnp.int32, (rows, tokens), 0)
    if scaled:
        value = jnp.broadcast_to(level_row[...].astype(F32) * 0.125, (rows, tokens))
    else:
        value = jnp.full((rows, tokens), 1.0, F32)
    for q in range(QUARTERS):
        part = slice(q * tokens, (q + 1) * tokens)
        hot[:, part] = jnp.where(row == base + q * quarter_step(by_pair), value, 0.0).astype(BF)
        quarters[part, :] = x_ref[:, q * width : (q + 1) * width]
    size = rows // len(outs)
    for i, out in enumerate(outs):
        part = jnp.dot(
            hot[i * size : (i + 1) * size, :], quarters[...], preferred_element_type=F32
        )
        out[...] = part.astype(BF).reshape(out.shape)


def dispatch(where, ids_row, ids_col, level_row, x, scaled, by_pair):
    tokens, d = x.shape
    rows, width = 16 * BLK, d // QUARTERS
    if by_pair:
        out_shape = [jax.ShapeDtypeStruct((QUARTERS, BLK, width), BF)] * 4
    else:
        out_shape = [jax.ShapeDtypeStruct((16, BLK, width), BF)]
    return pl.pallas_call(
        functools.partial(dispatch_kernel, scaled=scaled, by_pair=by_pair),
        out_shape=out_shape,
        in_specs=[pl.BlockSpec(memory_space=pltpu.SMEM)] + [WHOLE] * 4,
        out_specs=[WHOLE] * len(out_shape),
        scratch_shapes=[
            pltpu.VMEM((rows, QUARTERS * tokens), BF),
            pltpu.VMEM((QUARTERS * tokens, width), BF),
        ],
        compiler_params=params(),
        cost_estimate=cost(2 * rows * tokens * d, 4 * rows * width),
        name="dispatch",
    )(where, ids_row, ids_col, level_row, x)


def combine_kernel(where, ids_row, ids_col, level_col, *refs, scaled, by_pair):
    backs, out_ref, flat = refs[:-2], refs[-2], refs[-1]
    tokens = ids_row.shape[1]
    ids = ids_col[...]
    earlier = lax.broadcasted_iota(jnp.int32, (tokens, tokens), 1) < lax.broadcasted_iota(
        jnp.int32, (tokens, tokens), 0
    )
    same = jnp.where(earlier & (ids == ids_row[...]), 1, 0)
    rank = jnp.sum(same, axis=1, keepdims=True)
    base = first_row(ids, rank, where, by_pair)
    rows, width = flat.shape
    size = rows // len(backs)
    for i, back in enumerate(backs):
        flat[i * size : (i + 1) * size, :] = back[...].reshape(size, width)
    row = lax.broadcasted_iota(jnp.int32, (tokens, rows), 1)
    if scaled:
        value = jnp.broadcast_to(level_col[...].astype(F32) * 0.125, (tokens, rows))
    else:
        value = jnp.full((tokens, rows), 1.0, F32)
    for q in range(QUARTERS):
        hot = jnp.where(row == base + q * quarter_step(by_pair), value, 0.0).astype(BF)
        part = jnp.dot(hot, flat[...], preferred_element_type=F32)
        out_ref[:, q * width : (q + 1) * width] = part.astype(BF)


def combine(where, ids_row, ids_col, level_col, backs, scaled, by_pair):
    width = backs[0].shape[-1]
    rows = 16 * BLK
    tokens = ids_row.shape[1]
    return pl.pallas_call(
        functools.partial(combine_kernel, scaled=scaled, by_pair=by_pair),
        out_shape=jax.ShapeDtypeStruct((tokens, QUARTERS * width), BF),
        in_specs=[pl.BlockSpec(memory_space=pltpu.SMEM)] + [WHOLE] * (3 + len(backs)),
        out_specs=WHOLE,
        scratch_shapes=[pltpu.VMEM((rows, width), BF)],
        compiler_params=params(),
        cost_estimate=cost(2 * rows * tokens * width * QUARTERS, 4 * rows * width),
        name="combine",
    )(where, ids_row, ids_col, level_col, *backs)


def divide(value, by):
    return (value * ((1 << 20) // by + 1)) >> 20


def by_source_of(row):
    turn = divide(row, 192)
    rest = row - turn * 192
    quarter = divide(rest, BLK)
    rest = rest - quarter * BLK
    source = divide(rest, SLOTS)
    return source * BLK + quarter * (4 * SLOTS) + turn * SLOTS + rest - source * SLOTS


def by_turn_of(row):
    source = divide(row, BLK)
    rest = row - source * BLK
    quarter = divide(rest, 4 * SLOTS)
    rest = rest - quarter * (4 * SLOTS)
    turn = divide(rest, SLOTS)
    return turn * 192 + quarter * BLK + source * SLOTS + rest - turn * SLOTS


def one_hot(target, rows):
    row = lax.broadcasted_iota(jnp.int32, (rows, 1), 0)
    column = lax.broadcasted_iota(jnp.int32, (rows, rows), 1)
    return jnp.where(column == target(row), 1.0, 0.0).astype(BF)


def shuffle_kernel(rows_ref, *refs):
    outs, matrix = refs[:4], refs[4]
    matrix[...] = one_hot(by_source_of, matrix.shape[0])
    for turn, out in enumerate(outs):
        part = jnp.dot(
            matrix[turn * 192 : (turn + 1) * 192, :], rows_ref[...], preferred_element_type=F32
        )
        out[...] = part.astype(BF).reshape(out.shape)


def shuffle(rows):
    width = rows.shape[-1]
    return pl.pallas_call(
        shuffle_kernel,
        out_shape=[jax.ShapeDtypeStruct((QUARTERS, BLK, width), BF)] * 4,
        in_specs=[WHOLE],
        out_specs=[WHOLE] * 4,
        scratch_shapes=[pltpu.VMEM((768, 768), BF)],
        compiler_params=params(),
        cost_estimate=cost(2 * 768 * 768 * width, 4 * 768 * width),
        name="shuffle",
    )(rows.reshape(768, width))


def unshuffle_kernel(b0, b1, b2, b3, out_ref, matrix, rows):
    matrix[...] = one_hot(by_turn_of, matrix.shape[0])
    for turn, block in enumerate((b0, b1, b2, b3)):
        rows[turn * 192 : (turn + 1) * 192, :] = block[...].reshape(192, block.shape[-1])
    out_ref[...] = jnp.dot(matrix[...], rows[...], preferred_element_type=F32).astype(BF)


def unshuffle(blocks):
    width = blocks[0].shape[-1]
    out = pl.pallas_call(
        unshuffle_kernel,
        out_shape=jax.ShapeDtypeStruct((768, width), BF),
        in_specs=[WHOLE] * 4,
        out_specs=WHOLE,
        scratch_shapes=[pltpu.VMEM((768, 768), BF), pltpu.VMEM((768, width), BF)],
        compiler_params=params(),
        cost_estimate=cost(2 * 768 * 768 * width, 4 * 768 * width),
        name="unshuffle",
    )(*blocks)
    return out.reshape(16, BLK, width)


def gather_rows(blocks, rows):
    for i, block in enumerate(blocks):
        for q in range(QUARTERS):
            width = block.shape[-1]
            rows[i * BLK : (i + 1) * BLK, q * width : (q + 1) * width] = block[q]


def hidden_kernel(*refs):
    blocks, weights, (near, far, acts, rows) = refs[:8], refs[8:12], refs[12:]
    ff = weights[0].shape[1]
    half = near.shape[0]
    gather_rows(blocks, rows)
    for i, w in enumerate(weights):
        acts[:, i * ff : (i + 1) * ff] = jnp.dot(rows[...], w[...], preferred_element_type=F32)
    gate = acts[:, : 2 * ff]
    hidden = (gate * jax.nn.sigmoid(gate) * acts[:, 2 * ff :]).astype(BF)
    near[...] = hidden[:half]
    far[...] = hidden[half:]


def hidden_call(blocks, wg, wu):
    width = blocks[0].shape[-1]
    ff = wg[0].shape[1]
    rows = 8 * BLK
    part = jax.ShapeDtypeStruct((rows // 2, 2 * ff), BF)
    return pl.pallas_call(
        hidden_kernel,
        out_shape=[part, part, jax.ShapeDtypeStruct((rows, 4 * ff), F32)],
        in_specs=[WHOLE] * 12,
        out_specs=[WHOLE] * 3,
        scratch_shapes=[pltpu.VMEM((rows, QUARTERS * width), BF)],
        compiler_params=params(),
        cost_estimate=cost(8 * rows * width * QUARTERS * ff, 16 * 1024 * 1024),
        name="hidden",
    )(*blocks, *wg, *wu)


def hidden_parts(weights):
    place = [0, 0]
    half = sum(w.shape[0] for w in weights) // 2
    for w in weights:
        plane = 0 if place[0] < half else 1
        yield plane, place[plane], w.shape[0]
        place[plane] += w.shape[0]


def d_hidden_kernel(*refs):
    blocks, weights, (mine, other, rows) = refs[:4], refs[4:-3], refs[-3:]
    gather_rows(blocks, rows)
    for w, (plane, first, size) in zip(weights, hidden_parts(weights)):
        part = lax.dot_general(rows[...], w[...], NT, preferred_element_type=F32)
        out = (mine, other)[plane]
        out[:, first : first + size] = part.astype(out.dtype)


def d_hidden_call(blocks, wd):
    width = blocks[0].shape[-1]
    ff = sum(w.shape[0] for w in wd) // 4
    rows = 4 * BLK
    return pl.pallas_call(
        d_hidden_kernel,
        out_shape=[
            jax.ShapeDtypeStruct((rows, 2 * ff), F32),
            jax.ShapeDtypeStruct((rows, 2 * ff), BF),
        ],
        in_specs=[WHOLE] * (4 + len(wd)),
        out_specs=[WHOLE] * 2,
        scratch_shapes=[pltpu.VMEM((rows, QUARTERS * width), BF)],
        compiler_params=params(),
        cost_estimate=cost(8 * rows * width * QUARTERS * ff, 12 * 1024 * 1024),
        name="d_hidden",
    )(*blocks, *wd)


def store_blocks(value, outs, q):
    for i, out in enumerate(outs):
        out[q] = value[i * BLK : (i + 1) * BLK].astype(BF)


def out_kernel(near, other, *refs):
    weights, outs = refs[:-4], refs[-4:]
    width = outs[0].shape[-1]
    for q in range(QUARTERS):
        total = None
        for w, (plane, first, size) in zip(weights, hidden_parts(weights)):
            part = jnp.dot(
                (near, other)[plane][:, first : first + size],
                w[:, q * width : (q + 1) * width],
                preferred_element_type=F32,
            )
            total = part if total is None else total + part
        store_blocks(total, outs, q)


def out_call(near, other, wd):
    d = wd[0].shape[1]
    rows, units = near.shape
    return pl.pallas_call(
        out_kernel,
        out_shape=[jax.ShapeDtypeStruct((QUARTERS, BLK, d // QUARTERS), BF)] * 4,
        in_specs=[WHOLE] * (2 + len(wd)),
        out_specs=[WHOLE] * 4,
        compiler_params=params(),
        cost_estimate=cost(4 * rows * d * units, 10 * 1024 * 1024),
        name="expert_out",
    )(near, other, *wd)


def grad_kernel(acts, dh, wg0, wg1, wu0, wu1, *refs, first):
    outs, dacts = refs[:4], refs[4]
    ff = wg0.shape[1]
    width = outs[0].shape[-1]
    rows = slice(first, first + dh.shape[0])
    gate = acts[rows, : 2 * ff]
    up = acts[rows, 2 * ff :]
    sigma = jax.nn.sigmoid(gate)
    d_hidden = dh[...].astype(F32)
    d_gate = d_hidden * up * sigma * (1.0 + gate * (1.0 - sigma))
    dacts[:, : 2 * ff] = d_gate.astype(BF)
    dacts[:, 2 * ff :] = (d_hidden * (gate * sigma)).astype(BF)
    for q in range(QUARTERS):
        total = None
        for i, w in enumerate((wg0, wg1, wu0, wu1)):
            part = lax.dot_general(
                dacts[:, i * ff : (i + 1) * ff],
                w[q * width : (q + 1) * width, :],
                NT,
                preferred_element_type=F32,
            )
            total = part if total is None else total + part
        store_blocks(total, outs, q)


def grad_call(acts, dh, wg, wu, first):
    d, ff = wg[0].shape
    rows = dh.shape[0]
    return pl.pallas_call(
        functools.partial(grad_kernel, first=first),
        out_shape=[jax.ShapeDtypeStruct((QUARTERS, BLK, d // QUARTERS), BF)] * 4,
        in_specs=[WHOLE] * 6,
        out_specs=[WHOLE] * 4,
        scratch_shapes=[pltpu.VMEM((rows, 4 * ff), BF)],
        compiler_params=params(),
        cost_estimate=cost(8 * rows * d * ff, 12 * 1024 * 1024),
        name="expert_grad",
    )(acts, dh, *wg, *wu)


HEADS_STEP = 4


def attention_kernel(q_ref, k_ref, v_ref, do_ref, o_ref, dq_ref, dk_ref, dv_ref, dk_acc, dv_acc):
    step = pl.program_id(0)
    length = k_ref.shape[0]
    scale = HD ** (-0.5)
    k = k_ref[...]
    v = v_ref[...]
    causal = lax.broadcasted_iota(jnp.int32, (length, length), 0) >= lax.broadcasted_iota(
        jnp.int32, (length, length), 1
    )
    dk = None
    dv = None
    for h in range(HEADS_STEP):
        cols = slice(h * HD, (h + 1) * HD)
        q = q_ref[:, cols]
        do = do_ref[:, cols]
        scores = lax.dot_general(q, k, NT, preferred_element_type=F32) * scale
        scores = jnp.where(causal, scores, -1e30)
        raised = jnp.exp(scores - jnp.max(scores, axis=1, keepdims=True))
        probs = raised / jnp.sum(raised, axis=1, keepdims=True)
        rounded = probs.astype(BF)
        o_ref[:, cols] = jnp.dot(rounded, v, preferred_element_type=F32).astype(BF)
        d_probs = lax.dot_general(do, v, NT, preferred_element_type=F32).astype(BF).astype(F32)
        inner = jnp.sum(d_probs * probs, axis=1, keepdims=True)
        d_scores = (probs * (d_probs - inner) * scale).astype(BF)
        dq_ref[:, cols] = jnp.dot(d_scores, k, preferred_element_type=F32).astype(BF)
        dk_part = lax.dot_general(d_scores, q, TN, preferred_element_type=F32)
        dv_part = lax.dot_general(rounded, do, TN, preferred_element_type=F32)
        dk = dk_part if dk is None else dk + dk_part
        dv = dv_part if dv is None else dv + dv_part

    @pl.when(step == 0)
    def _():
        dk_acc[...] = dk
        dv_acc[...] = dv

    @pl.when(step > 0)
    def _():
        dk_acc[...] = dk_acc[...] + dk
        dv_acc[...] = dv_acc[...] + dv

    @pl.when(step == pl.num_programs(0) - 1)
    def _():
        dk_ref[...] = dk_acc[...].astype(BF)
        dv_ref[...] = dv_acc[...].astype(BF)


def attention(queries, keys, values, cotangent):
    length, wide = queries.shape
    head_spec = pl.BlockSpec((length, HEADS_STEP * HD), lambda s: (0, s))
    key_spec = pl.BlockSpec((length, HD), lambda s: (0, 0))
    heads = wide // HD
    return pl.pallas_call(
        attention_kernel,
        out_shape=[
            jax.ShapeDtypeStruct(queries.shape, BF),
            jax.ShapeDtypeStruct(queries.shape, BF),
            jax.ShapeDtypeStruct(keys.shape, BF),
            jax.ShapeDtypeStruct(values.shape, BF),
        ],
        grid=(heads // HEADS_STEP,),
        in_specs=[head_spec, key_spec, key_spec, head_spec],
        out_specs=[head_spec, head_spec, key_spec, key_spec],
        scratch_shapes=[pltpu.VMEM((length, HD), F32)] * 2,
        compiler_params=params(dimension_semantics=("arbitrary",)),
        cost_estimate=cost(14 * heads * length * length * HD, 10 * 1024 * 1024),
        name="attention",
    )(queries, keys, values, cotangent)


def on_device(
    layer_input,
    out_grad,
    expert_ids,
    gate_level,
    w_gate,
    w_up,
    w_down,
    attn_queries,
    attn_keys,
    attn_values,
    attn_grad,
):
    tokens = layer_input.shape[0]
    where = jnp.stack([lax.axis_index("dp") // 16, lax.axis_index("tensor") // 2]).astype(jnp.int32)
    ids_row = expert_ids.reshape(1, tokens)
    ids_col = expert_ids.reshape(tokens, 1)
    level_row = gate_level.reshape(1, tokens)
    level_col = gate_level.reshape(tokens, 1)

    tie = lax.optimization_barrier

    down = w_down[0]
    piece_a, piece_b, piece_c = jnp.split(down, DOWN_CUTS)
    down_a = send(piece_a, INNER)
    gate_mate, up_mate, down_mate = send(w_gate[0], CORES), send(w_up[0], CORES), send(down, CORES)

    (x_sent,) = dispatch(where, ids_row, ids_col, level_row, layer_input, False, False)
    g_sent = dispatch(where, ids_row, ids_col, level_row, out_grad, True, True)
    x_rows = plane_exchange(x_sent)
    g_sent, gate_mate, up_mate, down_mate, down_a, piece_b = tie(
        (g_sent, gate_mate, up_mate, down_mate, down_a, piece_b)
    )
    down_b = send(piece_b, INNER)
    g_near = [g_sent[0]] + [send(block, perm) for block, perm in zip(g_sent[1:], NEAR)]
    attended = attention(attn_queries, attn_keys, attn_values, attn_grad)
    x_rows, attended, g_near, down_b, piece_c = tie((x_rows, attended, g_near, down_b, piece_c))
    x_own, x_one, x_two, x_three = shuffle(x_rows)
    g_mixed = unshuffle(g_near)
    x_own, x_one, x_two, x_three, g_mixed = tie((x_own, x_one, x_two, x_three, g_mixed))
    far_own = send(x_own, INNER)
    down_c = send(piece_c, INNER)
    near = [send(block, perm) for block, perm in zip((x_one, x_two, x_three), NEAR)]
    g_blocks = shuffle(plane_exchange(g_mixed))
    near, far_own, g_blocks, down_c = tie((near, far_own, g_blocks, down_c))
    down_other = jnp.concatenate([down_a, down_b, down_c])
    down_other_mate = send(down_other, CORES)
    wg = (w_gate[0], gate_mate)
    wu = (w_up[0], up_mate)
    wd = (down, down_mate, down_other, down_other_mate)
    far = [send(block, INNER) for block in near]

    dh_near, dh_far = d_hidden_call(g_blocks, wd)
    dh_other = send(dh_far, INNER)
    far, dh_far = tie((far, dh_far))
    hidden_near, hidden_far, acts = hidden_call([x_own] + near + [far_own] + far, wg, wu)
    half = dh_near.shape[0]
    terms = grad_call(acts, dh_other, wg, wu, half)

    recv_two = send(terms[2], INNER)
    hidden_other = send(hidden_far, INNER)
    near_terms = grad_call(acts, dh_near, wg, wu, 0)

    def total(i, arrived):
        return (near_terms[i].astype(F32) + arrived.astype(F32)).astype(BF)

    near_terms, hidden_other, term_one, term_three, recv_two = tie(
        (near_terms, hidden_other, terms[1], terms[3], recv_two)
    )
    recv_one = send(term_one, INNER)
    recv_three = send(term_three, INNER)
    back_two = send(total(2, recv_two), BACK[1])
    out_rows = plane_exchange(unshuffle(out_call(hidden_near, hidden_other, wd)))
    term_own, recv_one, recv_three = tie((terms[0], recv_one, recv_three))
    recv_own = send(term_own, INNER)
    back_one = send(total(1, recv_one), BACK[0])
    back_three = send(total(3, recv_three), BACK[2])
    out_blocks, recv_own = tie((shuffle(out_rows), recv_own))
    backs = [back_one, back_two, back_three]
    out_blocks, backs = tie((out_blocks, backs))
    grad_rows = plane_exchange(unshuffle([total(0, recv_own)] + backs))
    out_back = [out_blocks[0]] + [send(b, perm) for b, perm in zip(out_blocks[1:], BACK)]

    moe_out = combine(where, ids_row, ids_col, level_col, out_back, True, True)
    grad_x = combine(where, ids_row, ids_col, level_col, [grad_rows], False, False)
    attn_out, grad_q, grad_k, grad_v = attended
    return (moe_out, grad_x, attn_out, grad_q, grad_k, grad_v)


def solution(mesh):
    in_specs = (
        P(("dp", "tensor"), None),
        P(("dp", "tensor"), None),
        P(("dp", "tensor"), None),
        P(("dp", "tensor"), None),
        P("dp", None, "tensor"),
        P("dp", None, "tensor"),
        P("dp", "tensor", None),
        P("dp", "tensor"),
        P("dp", "tensor"),
        P("dp", "tensor"),
        P("dp", "tensor"),
    )
    out_specs = (
        P(("dp", "tensor"), None),
        P(("dp", "tensor"), None),
        P("dp", "tensor"),
        P("dp", "tensor"),
        P("dp", "tensor"),
        P("dp", "tensor"),
    )
    return jax.shard_map(
        on_device, mesh=mesh, in_specs=in_specs, out_specs=out_specs, check_vma=False
    )
```

```python
import functools

import jax
import jax.numpy as jnp
from jax import lax
from jax.experimental import pallas as pl
from jax.experimental.pallas import tpu as pltpu
from jax.sharding import PartitionSpec as P

HD = 128
AXES = ("dp", "tensor")
SLOTS = 3
QUARTERS = 4
BLK = 48
VMEM_LIMIT = 40 * 1024 * 1024
BF = jnp.bfloat16
F32 = jnp.float32
NT = (((1,), (1,)), ((), ()))
TN = (((0,), (0,)), ((), ()))


def linear(x, y, z, core):
    return ((z // 2) * 16 + y * 4 + x) * 4 + (z % 2) * 2 + core


def moves(target):
    pairs = []
    for x in range(4):
        for y in range(4):
            for z in range(8):
                for core in range(2):
                    z_to, core_to = target(z, core)
                    pairs.append((linear(x, y, z, core), linear(x, y, z_to % 8, core_to)))
    return pairs


INNER = moves(lambda z, c: (z ^ 1, c))
CORES = moves(lambda z, c: (z, 1 - c))
NEAR = [
    moves(lambda z, c: (z - 2 if z % 2 else z + 2, c)),
    moves(lambda z, c: (z + 3 if z % 2 else z - 3, c)),
    moves(lambda z, c: (z + 1 if z % 2 else z - 1, c)),
]
BACK = [[(b, a) for a, b in perm] for perm in NEAR]
PLANES = [
    [linear(x, y, z, c) for y in range(4) for x in range(4)] for z in range(8) for c in range(2)
]


def send(value, perm):
    return lax.ppermute(value, AXES, perm)


def plane_exchange(value):
    return lax.all_to_all(value, AXES, 0, 0, axis_index_groups=PLANES, tiled=True)


def params(**more):
    return pltpu.CompilerParams(vmem_limit_bytes=VMEM_LIMIT, **more)


WHOLE = pl.BlockSpec(memory_space=pltpu.VMEM)


def cost(flops, nbytes):
    return pl.CostEstimate(flops=flops, bytes_accessed=nbytes, transcendentals=0)


def first_row(ids, rank, where, by_pair):
    pair, odd = where[0], where[1]
    turn = ((ids >> 4) - pair) & 3
    turn = jnp.where(odd == 1, (4 - turn) & 3, turn)
    if by_pair:
        return turn * (4 * BLK) + (ids & 15) * SLOTS + rank
    return (ids & 15) * BLK + turn * SLOTS + rank


def quarter_step(by_pair):
    return BLK if by_pair else 4 * SLOTS


def dispatch_kernel(where, ids_row, ids_col, level_row, x_ref, *refs, scaled, by_pair):
    outs, (hot, quarters) = refs[:-2], refs[-2:]
    tokens = ids_row.shape[1]
    ids = ids_row[...]
    earlier = lax.broadcasted_iota(jnp.int32, (tokens, tokens), 0) < lax.broadcasted_iota(
        jnp.int32, (tokens, tokens), 1
    )
    same = jnp.where(earlier & (ids_col[...] == ids), 1, 0)
    rank = jnp.sum(same, axis=0, keepdims=True)
    base = first_row(ids, rank, where, by_pair)
    rows, width = hot.shape[0], quarters.shape[1]
    row = lax.broadcasted_iota(jnp.int32, (rows, tokens), 0)
    if scaled:
        value = jnp.broadcast_to(level_row[...].astype(F32) * 0.125, (rows, tokens))
    else:
        value = jnp.full((rows, tokens), 1.0, F32)
    for q in range(QUARTERS):
        part = slice(q * tokens, (q + 1) * tokens)
        hot[:, part] = jnp.where(row == base + q * quarter_step(by_pair), value, 0.0).astype(BF)
        quarters[part, :] = x_ref[:, q * width : (q + 1) * width]
    size = rows // len(outs)
    for i, out in enumerate(outs):
        part = jnp.dot(
            hot[i * size : (i + 1) * size, :], quarters[...], preferred_element_type=F32
        )
        out[...] = part.astype(BF).reshape(out.shape)


def dispatch(where, ids_row, ids_col, level_row, x, scaled, by_pair):
    tokens, d = x.shape
    rows, width = 16 * BLK, d // QUARTERS
    if by_pair:
        out_shape = [jax.ShapeDtypeStruct((QUARTERS, BLK, width), BF)] * 4
    else:
        out_shape = [jax.ShapeDtypeStruct((16, BLK, width), BF)]
    return pl.pallas_call(
        functools.partial(dispatch_kernel, scaled=scaled, by_pair=by_pair),
        out_shape=out_shape,
        in_specs=[pl.BlockSpec(memory_space=pltpu.SMEM)] + [WHOLE] * 4,
        out_specs=[WHOLE] * len(out_shape),
        scratch_shapes=[
            pltpu.VMEM((rows, QUARTERS * tokens), BF),
            pltpu.VMEM((QUARTERS * tokens, width), BF),
        ],
        compiler_params=params(),
        cost_estimate=cost(2 * rows * tokens * d, 4 * rows * width),
        name="dispatch",
    )(where, ids_row, ids_col, level_row, x)


def combine_kernel(where, ids_row, ids_col, level_col, *refs, scaled, by_pair):
    backs, out_ref, flat = refs[:-2], refs[-2], refs[-1]
    tokens = ids_row.shape[1]
    ids = ids_col[...]
    earlier = lax.broadcasted_iota(jnp.int32, (tokens, tokens), 1) < lax.broadcasted_iota(
        jnp.int32, (tokens, tokens), 0
    )
    same = jnp.where(earlier & (ids == ids_row[...]), 1, 0)
    rank = jnp.sum(same, axis=1, keepdims=True)
    base = first_row(ids, rank, where, by_pair)
    rows, width = flat.shape
    size = rows // len(backs)
    for i, back in enumerate(backs):
        flat[i * size : (i + 1) * size, :] = back[...].reshape(size, width)
    row = lax.broadcasted_iota(jnp.int32, (tokens, rows), 1)
    if scaled:
        value = jnp.broadcast_to(level_col[...].astype(F32) * 0.125, (tokens, rows))
    else:
        value = jnp.full((tokens, rows), 1.0, F32)
    for q in range(QUARTERS):
        hot = jnp.where(row == base + q * quarter_step(by_pair), value, 0.0).astype(BF)
        part = jnp.dot(hot, flat[...], preferred_element_type=F32)
        out_ref[:, q * width : (q + 1) * width] = part.astype(BF)


def combine(where, ids_row, ids_col, level_col, backs, scaled, by_pair):
    width = backs[0].shape[-1]
    rows = 16 * BLK
    tokens = ids_row.shape[1]
    return pl.pallas_call(
        functools.partial(combine_kernel, scaled=scaled, by_pair=by_pair),
        out_shape=jax.ShapeDtypeStruct((tokens, QUARTERS * width), BF),
        in_specs=[pl.BlockSpec(memory_space=pltpu.SMEM)] + [WHOLE] * (3 + len(backs)),
        out_specs=WHOLE,
        scratch_shapes=[pltpu.VMEM((rows, width), BF)],
        compiler_params=params(),
        cost_estimate=cost(2 * rows * tokens * width * QUARTERS, 4 * rows * width),
        name="combine",
    )(where, ids_row, ids_col, level_col, *backs)


def divide(value, by):
    return (value * ((1 << 20) // by + 1)) >> 20


def by_source_of(row):
    turn = divide(row, 192)
    rest = row - turn * 192
    quarter = divide(rest, BLK)
    rest = rest - quarter * BLK
    source = divide(rest, SLOTS)
    return source * BLK + quarter * (4 * SLOTS) + turn * SLOTS + rest - source * SLOTS


def by_turn_of(row):
    source = divide(row, BLK)
    rest = row - source * BLK
    quarter = divide(rest, 4 * SLOTS)
    rest = rest - quarter * (4 * SLOTS)
    turn = divide(rest, SLOTS)
    return turn * 192 + quarter * BLK + source * SLOTS + rest - turn * SLOTS


def one_hot(target, rows):
    row = lax.broadcasted_iota(jnp.int32, (rows, 1), 0)
    column = lax.broadcasted_iota(jnp.int32, (rows, rows), 1)
    return jnp.where(column == target(row), 1.0, 0.0).astype(BF)


def shuffle_kernel(rows_ref, *refs):
    outs, matrix = refs[:-1], refs[-1]
    matrix[...] = one_hot(by_source_of, matrix.shape[0])
    size = matrix.shape[0] // len(outs)
    for i, out in enumerate(outs):
        part = jnp.dot(
            matrix[i * size : (i + 1) * size, :], rows_ref[...], preferred_element_type=F32
        )
        out[...] = part.astype(BF).reshape(out.shape)


def shuffle(rows, joined=False):
    width = rows.shape[-1]
    block = (QUARTERS, BLK, width)
    shapes = [(4,) + block] if joined else [block] * 4
    return pl.pallas_call(
        shuffle_kernel,
        out_shape=[jax.ShapeDtypeStruct(shape, BF) for shape in shapes],
        in_specs=[WHOLE],
        out_specs=[WHOLE] * len(shapes),
        scratch_shapes=[pltpu.VMEM((768, 768), BF)],
        compiler_params=params(),
        cost_estimate=cost(2 * 768 * 768 * width, 4 * 768 * width),
        name="shuffle",
    )(rows.reshape(768, width))


def unshuffle_kernel(b0, b1, b2, b3, out_ref, matrix, rows):
    matrix[...] = one_hot(by_turn_of, matrix.shape[0])
    for turn, block in enumerate((b0, b1, b2, b3)):
        rows[turn * 192 : (turn + 1) * 192, :] = block[...].reshape(192, block.shape[-1])
    out_ref[...] = jnp.dot(matrix[...], rows[...], preferred_element_type=F32).astype(BF)


def unshuffle(blocks):
    width = blocks[0].shape[-1]
    out = pl.pallas_call(
        unshuffle_kernel,
        out_shape=jax.ShapeDtypeStruct((768, width), BF),
        in_specs=[WHOLE] * 4,
        out_specs=WHOLE,
        scratch_shapes=[pltpu.VMEM((768, 768), BF), pltpu.VMEM((768, width), BF)],
        compiler_params=params(),
        cost_estimate=cost(2 * 768 * 768 * width, 4 * 768 * width),
        name="unshuffle",
    )(*blocks)
    return out.reshape(16, BLK, width)


def gather_rows(blocks, rows):
    for i, block in enumerate(blocks):
        for q in range(QUARTERS):
            width = block.shape[-1]
            rows[i * BLK : (i + 1) * BLK, q * width : (q + 1) * width] = block[q]


def hidden_kernel(*refs):
    (x_near, x_far), weights, (near, far, acts, rows) = refs[:2], refs[2:6], refs[6:]
    ff = weights[0].shape[1]
    half = near.shape[0]
    gather_rows([x_near.at[i] for i in range(4)] + [x_far.at[i] for i in range(4)], rows)
    for i, w in enumerate(weights):
        acts[:, i * ff : (i + 1) * ff] = jnp.dot(rows[...], w[...], preferred_element_type=F32)
    gate = acts[:, : 2 * ff]
    hidden = (gate * jax.nn.sigmoid(gate) * acts[:, 2 * ff :]).astype(BF)
    near[...] = hidden[:half]
    far[...] = hidden[half:]


def hidden_call(x_near, x_far, wg, wu):
    width = x_near.shape[-1]
    ff = wg[0].shape[1]
    rows = 8 * BLK
    part = jax.ShapeDtypeStruct((rows // 2, 2 * ff), BF)
    return pl.pallas_call(
        hidden_kernel,
        out_shape=[part, part, jax.ShapeDtypeStruct((rows, 4 * ff), F32)],
        in_specs=[WHOLE] * 6,
        out_specs=[WHOLE] * 3,
        scratch_shapes=[pltpu.VMEM((rows, QUARTERS * width), BF)],
        compiler_params=params(),
        cost_estimate=cost(8 * rows * width * QUARTERS * ff, 16 * 1024 * 1024),
        name="hidden",
    )(x_near, x_far, *wg, *wu)


def hidden_parts(weights):
    place = [0, 0]
    half = sum(w.shape[0] for w in weights) // 2
    for w in weights:
        plane = 0 if place[0] < half else 1
        yield plane, place[plane], w.shape[0]
        place[plane] += w.shape[0]


def d_hidden_kernel(*refs):
    blocks, weights, (mine, other, rows) = refs[:4], refs[4:-3], refs[-3:]
    gather_rows(blocks, rows)
    for w, (plane, first, size) in zip(weights, hidden_parts(weights)):
        part = lax.dot_general(rows[...], w[...], NT, preferred_element_type=F32)
        out = (mine, other)[plane]
        out[:, first : first + size] = part.astype(out.dtype)


def d_hidden_call(blocks, wd):
    width = blocks[0].shape[-1]
    ff = sum(w.shape[0] for w in wd) // 4
    rows = 4 * BLK
    return pl.pallas_call(
        d_hidden_kernel,
        out_shape=[
            jax.ShapeDtypeStruct((rows, 2 * ff), F32),
            jax.ShapeDtypeStruct((rows, 2 * ff), BF),
        ],
        in_specs=[WHOLE] * (4 + len(wd)),
        out_specs=[WHOLE] * 2,
        scratch_shapes=[pltpu.VMEM((rows, QUARTERS * width), BF)],
        compiler_params=params(),
        cost_estimate=cost(8 * rows * width * QUARTERS * ff, 12 * 1024 * 1024),
        name="d_hidden",
    )(*blocks, *wd)


def store_blocks(value, outs, q):
    for i, out in enumerate(outs):
        out[q] = value[i * BLK : (i + 1) * BLK].astype(BF)


def out_kernel(near, other, *refs):
    weights, outs = refs[:-4], refs[-4:]
    width = outs[0].shape[-1]
    for q in range(QUARTERS):
        total = None
        for w, (plane, first, size) in zip(weights, hidden_parts(weights)):
            part = jnp.dot(
                (near, other)[plane][:, first : first + size],
                w[:, q * width : (q + 1) * width],
                preferred_element_type=F32,
            )
            total = part if total is None else total + part
        store_blocks(total, outs, q)


def out_call(near, other, wd):
    d = wd[0].shape[1]
    rows, units = near.shape
    return pl.pallas_call(
        out_kernel,
        out_shape=[jax.ShapeDtypeStruct((QUARTERS, BLK, d // QUARTERS), BF)] * 4,
        in_specs=[WHOLE] * (2 + len(wd)),
        out_specs=[WHOLE] * 4,
        compiler_params=params(),
        cost_estimate=cost(4 * rows * d * units, 10 * 1024 * 1024),
        name="expert_out",
    )(near, other, *wd)


def grad_kernel(acts, dh, wg0, wg1, wu0, wu1, *refs, first):
    outs, dacts = refs[:4], refs[4]
    ff = wg0.shape[1]
    width = outs[0].shape[-1]
    rows = slice(first, first + dh.shape[0])
    gate = acts[rows, : 2 * ff]
    up = acts[rows, 2 * ff :]
    sigma = jax.nn.sigmoid(gate)
    d_hidden = dh[...].astype(F32)
    d_gate = d_hidden * up * sigma * (1.0 + gate * (1.0 - sigma))
    dacts[:, : 2 * ff] = d_gate.astype(BF)
    dacts[:, 2 * ff :] = (d_hidden * (gate * sigma)).astype(BF)
    for q in range(QUARTERS):
        total = None
        for i, w in enumerate((wg0, wg1, wu0, wu1)):
            part = lax.dot_general(
                dacts[:, i * ff : (i + 1) * ff],
                w[q * width : (q + 1) * width, :],
                NT,
                preferred_element_type=F32,
            )
            total = part if total is None else total + part
        store_blocks(total, outs, q)


def grad_call(acts, dh, wg, wu, first):
    d, ff = wg[0].shape
    rows = dh.shape[0]
    return pl.pallas_call(
        functools.partial(grad_kernel, first=first),
        out_shape=[jax.ShapeDtypeStruct((QUARTERS, BLK, d // QUARTERS), BF)] * 4,
        in_specs=[WHOLE] * 6,
        out_specs=[WHOLE] * 4,
        scratch_shapes=[pltpu.VMEM((rows, 4 * ff), BF)],
        compiler_params=params(),
        cost_estimate=cost(8 * rows * d * ff, 12 * 1024 * 1024),
        name="expert_grad",
    )(acts, dh, *wg, *wu)


HEADS_STEP = 4


def attention_kernel(q_ref, k_ref, v_ref, do_ref, o_ref, dq_ref, dk_ref, dv_ref, dk_acc, dv_acc):
    step = pl.program_id(0)
    length = k_ref.shape[0]
    scale = HD ** (-0.5)
    k = k_ref[...]
    v = v_ref[...]
    causal = lax.broadcasted_iota(jnp.int32, (length, length), 0) >= lax.broadcasted_iota(
        jnp.int32, (length, length), 1
    )
    dk = None
    dv = None
    for h in range(HEADS_STEP):
        cols = slice(h * HD, (h + 1) * HD)
        q = q_ref[:, cols]
        do = do_ref[:, cols]
        scores = lax.dot_general(q, k, NT, preferred_element_type=F32) * scale
        scores = jnp.where(causal, scores, -1e30)
        raised = jnp.exp(scores - jnp.max(scores, axis=1, keepdims=True))
        probs = raised / jnp.sum(raised, axis=1, keepdims=True)
        rounded = probs.astype(BF)
        o_ref[:, cols] = jnp.dot(rounded, v, preferred_element_type=F32).astype(BF)
        d_probs = lax.dot_general(do, v, NT, preferred_element_type=F32).astype(BF).astype(F32)
        inner = jnp.sum(d_probs * probs, axis=1, keepdims=True)
        d_scores = (probs * (d_probs - inner) * scale).astype(BF)
        dq_ref[:, cols] = jnp.dot(d_scores, k, preferred_element_type=F32).astype(BF)
        dk_part = lax.dot_general(d_scores, q, TN, preferred_element_type=F32)
        dv_part = lax.dot_general(rounded, do, TN, preferred_element_type=F32)
        dk = dk_part if dk is None else dk + dk_part
        dv = dv_part if dv is None else dv + dv_part

    @pl.when(step == 0)
    def _():
        dk_acc[...] = dk
        dv_acc[...] = dv

    @pl.when(step > 0)
    def _():
        dk_acc[...] = dk_acc[...] + dk
        dv_acc[...] = dv_acc[...] + dv

    @pl.when(step == pl.num_programs(0) - 1)
    def _():
        dk_ref[...] = dk_acc[...].astype(BF)
        dv_ref[...] = dv_acc[...].astype(BF)


def attention(queries, keys, values, cotangent):
    length, wide = queries.shape
    head_spec = pl.BlockSpec((length, HEADS_STEP * HD), lambda s: (0, s))
    key_spec = pl.BlockSpec((length, HD), lambda s: (0, 0))
    heads = wide // HD
    return pl.pallas_call(
        attention_kernel,
        out_shape=[
            jax.ShapeDtypeStruct(queries.shape, BF),
            jax.ShapeDtypeStruct(queries.shape, BF),
            jax.ShapeDtypeStruct(keys.shape, BF),
            jax.ShapeDtypeStruct(values.shape, BF),
        ],
        grid=(heads // HEADS_STEP,),
        in_specs=[head_spec, key_spec, key_spec, head_spec],
        out_specs=[head_spec, head_spec, key_spec, key_spec],
        scratch_shapes=[pltpu.VMEM((length, HD), F32)] * 2,
        compiler_params=params(dimension_semantics=("arbitrary",)),
        cost_estimate=cost(14 * heads * length * length * HD, 10 * 1024 * 1024),
        name="attention",
    )(queries, keys, values, cotangent)


def on_device(
    layer_input,
    out_grad,
    expert_ids,
    gate_level,
    w_gate,
    w_up,
    w_down,
    attn_queries,
    attn_keys,
    attn_values,
    attn_grad,
):
    tokens = layer_input.shape[0]
    where = jnp.stack([lax.axis_index("dp") // 16, lax.axis_index("tensor") // 2]).astype(jnp.int32)
    ids_row = expert_ids.reshape(1, tokens)
    ids_col = expert_ids.reshape(tokens, 1)
    level_row = gate_level.reshape(1, tokens)
    level_col = gate_level.reshape(tokens, 1)

    tie = lax.optimization_barrier

    down = w_down[0]
    gate_mate, up_mate = send(w_gate[0], CORES), send(w_up[0], CORES)
    piece_a, piece_b = jnp.split(down, [96])
    down_a = send(piece_a, INNER)

    x_sent = dispatch(where, ids_row, ids_col, level_row, layer_input, False, True)
    (g_sent,) = dispatch(where, ids_row, ids_col, level_row, out_grad, True, False)
    g_rows = plane_exchange(g_sent)
    x_sent, gate_mate, up_mate, down_a, piece_b = tie(
        (x_sent, gate_mate, up_mate, down_a, piece_b)
    )
    x_there = [x_sent[0]] + [send(block, perm) for block, perm in zip(x_sent[1:], NEAR)]
    down_b = send(piece_b, INNER)
    attended = attention(attn_queries, attn_keys, attn_values, attn_grad)
    x_there, attended, down, g_rows = tie((x_there, attended, down, g_rows))
    x_rows = plane_exchange(unshuffle(x_there))
    down_mate = send(down, CORES)
    g_blocks, down_b = tie((shuffle(g_rows), down_b))
    g_near = [g_blocks[0]] + [send(block, perm) for block, perm in zip(g_blocks[1:], NEAR)]
    down_other = jnp.concatenate([down_a, down_b])
    x_rows, down_other, g_near[1], g_near[3] = tie((x_rows, down_other, g_near[1], g_near[3]))
    (x_near,) = shuffle(x_rows, joined=True)
    x_far = send(x_near, INNER)
    down_other_mate = send(down_other, CORES)
    wg = (w_gate[0], gate_mate)
    wu = (w_up[0], up_mate)
    wd = (down, down_mate, down_other, down_other_mate)

    dh_near, dh_far = d_hidden_call(g_near, wd)
    dh_other = send(dh_far, INNER)
    x_far, dh_other = tie((x_far, dh_other))
    hidden_near, hidden_far, acts = hidden_call(x_near, x_far, wg, wu)
    half = dh_near.shape[0]
    terms = grad_call(acts, dh_other, wg, wu, half)

    arrived = [send(term, INNER) for term in terms[1:]]
    hidden_other = send(hidden_far, INNER)
    near_terms = grad_call(acts, dh_near, wg, wu, 0)
    out_sent = unshuffle(out_call(hidden_near, hidden_other, wd))
    near_terms, term_own, arrived, out_sent = tie((near_terms, terms[0], arrived, out_sent))

    def total(near, far):
        return (near.astype(F32) + far.astype(F32)).astype(BF)

    arrived_own = send(term_own, INNER)
    back = [send(total(n, f), perm) for n, f, perm in zip(near_terms[1:], arrived, BACK)]
    out_rows = plane_exchange(out_sent)
    out_rows, back = tie((out_rows, back))
    grad_rows = plane_exchange(unshuffle([total(near_terms[0], arrived_own)] + back))
    out_blocks = shuffle(out_rows)
    out_back = [out_blocks[0]] + [send(b, perm) for b, perm in zip(out_blocks[1:], BACK)]

    moe_out = combine(where, ids_row, ids_col, level_col, out_back, True, True)
    grad_x = combine(where, ids_row, ids_col, level_col, [grad_rows], False, False)
    attn_out, grad_q, grad_k, grad_v = attended
    return (moe_out, grad_x, attn_out, grad_q, grad_k, grad_v)


def solution(mesh):
    in_specs = (
        P(("dp", "tensor"), None),
        P(("dp", "tensor"), None),
        P(("dp", "tensor"), None),
        P(("dp", "tensor"), None),
        P("dp", None, "tensor"),
        P("dp", None, "tensor"),
        P("dp", "tensor", None),
        P("dp", "tensor"),
        P("dp", "tensor"),
        P("dp", "tensor"),
        P("dp", "tensor"),
    )
    out_specs = (
        P(("dp", "tensor"), None),
        P(("dp", "tensor"), None),
        P("dp", "tensor"),
        P("dp", "tensor"),
        P("dp", "tensor"),
        P("dp", "tensor"),
    )
    return jax.shard_map(
        on_device, mesh=mesh, in_specs=in_specs, out_specs=out_specs, check_vma=False
    )
```

```python
import functools

import jax
import jax.numpy as jnp
from jax import lax
from jax.experimental import pallas as pl
from jax.experimental.pallas import tpu as pltpu
from jax.sharding import PartitionSpec as P

HD = 128
AXES = ("dp", "tensor")
SLOTS = 3
CHUNKS = 8
TEAM = 16
BLK = TEAM * SLOTS
TEAM_ROWS = BLK * CHUNKS
VMEM_LIMIT = 40 * 1024 * 1024
BF = jnp.bfloat16
F32 = jnp.float32
NT = (((1,), (1,)), ((), ()))
TN = (((0,), (0,)), ((), ()))


def linear(x, y, z, core):
    return ((z // 2) * 16 + y * 4 + x) * 4 + (z % 2) * 2 + core


def moves(target):
    pairs = []
    for x in range(4):
        for y in range(4):
            for z in range(8):
                for core in range(2):
                    z_to, core_to = target(z, core)
                    pairs.append((linear(x, y, z, core), linear(x, y, z_to, core_to)))
    return pairs


INNER = moves(lambda z, c: (z ^ 1, c))
CORES = moves(lambda z, c: (z, 1 - c))
GROUPS = [
    [linear(x, y, z, c) for z in planes for y in range(4) for x in range(4)]
    for planes in ((0, 2, 5, 7), (1, 3, 4, 6))
    for c in range(2)
]


def send(value, perm):
    return lax.ppermute(value, AXES, perm)


def exchange(rows):
    parted = rows.reshape(4 * TEAM, CHUNKS * SLOTS, rows.shape[1])
    parted = lax.all_to_all(parted, AXES, 0, 0, axis_index_groups=GROUPS, tiled=True)
    return parted.reshape(rows.shape)


def params(**more):
    return pltpu.CompilerParams(vmem_limit_bytes=VMEM_LIMIT, **more)


WHOLE = pl.BlockSpec(memory_space=pltpu.VMEM)


def cost(flops, nbytes):
    return pl.CostEstimate(flops=flops // 1000, bytes_accessed=nbytes // 1000, transcendentals=0)


def divide(value, by):
    return (value * ((1 << 20) // by + 1)) >> 20


def chunk_row(row):
    device = divide(row, CHUNKS * SLOTS)
    rest = row - device * (CHUNKS * SLOTS)
    chunk = divide(rest, SLOTS)
    return chunk * BLK + device * SLOTS + rest - chunk * SLOTS


def device_row(row):
    chunk = divide(row, BLK)
    rest = row - chunk * BLK
    device = divide(rest, SLOTS)
    return device * (CHUNKS * SLOTS) + chunk * SLOTS + rest - device * SLOTS


def one_hot(target):
    row = lax.broadcasted_iota(jnp.int32, (TEAM_ROWS, 1), 0)
    column = lax.broadcasted_iota(jnp.int32, (TEAM_ROWS, TEAM_ROWS), 1)
    return jnp.where(column == target(row), 1.0, 0.0).astype(BF)


def to_devices(full, stack, out):
    order = one_hot(chunk_row)
    width = out.shape[1]
    for team in range(4):
        for chunk in range(CHUNKS):
            stack[chunk * BLK : (chunk + 1) * BLK, :] = full[
                team * BLK : (team + 1) * BLK, chunk * width : (chunk + 1) * width
            ]
        part = jnp.dot(order, stack[...], preferred_element_type=F32)
        out[team * TEAM_ROWS : (team + 1) * TEAM_ROWS, :] = part.astype(BF)


def from_devices(rows, full):
    order = one_hot(device_row)
    width = rows.shape[1]
    for team in range(4):
        part = jnp.dot(
            order, rows[team * TEAM_ROWS : (team + 1) * TEAM_ROWS, :], preferred_element_type=F32
        ).astype(BF)
        for chunk in range(CHUNKS):
            full[team * BLK : (team + 1) * BLK, chunk * width : (chunk + 1) * width] = part[
                chunk * BLK : (chunk + 1) * BLK
            ]


def travel_type(d):
    return jax.ShapeDtypeStruct((4 * TEAM_ROWS, d // CHUNKS), BF)


def full_scratch(d):
    return pltpu.VMEM((4 * BLK, d), BF)


def stack_scratch(d):
    return pltpu.VMEM((TEAM_ROWS, d // CHUNKS), BF)


def dispatch_kernel(ids_row, ids_col, level_row, x_ref, out_ref, full, stack, *, scaled):
    tokens = ids_row.shape[1]
    ids = ids_row[...]
    earlier = lax.broadcasted_iota(jnp.int32, (tokens, tokens), 0) < lax.broadcasted_iota(
        jnp.int32, (tokens, tokens), 1
    )
    same = jnp.where(earlier & (ids_col[...] == ids), 1, 0)
    slot = ids * SLOTS + jnp.sum(same, axis=0, keepdims=True)
    shape = (4 * BLK, tokens)
    if scaled:
        value = jnp.broadcast_to(level_row[...].astype(F32) * 0.125, shape)
    else:
        value = jnp.full(shape, 1.0, F32)
    hot = jnp.where(lax.broadcasted_iota(jnp.int32, shape, 0) == slot, value, 0.0).astype(BF)
    full[...] = jnp.dot(hot, x_ref[...], preferred_element_type=F32).astype(BF)
    to_devices(full, stack, out_ref)


def dispatch(ids_row, ids_col, level_row, x, scaled):
    tokens, d = x.shape
    return pl.pallas_call(
        functools.partial(dispatch_kernel, scaled=scaled),
        out_shape=travel_type(d),
        in_specs=[WHOLE] * 4,
        out_specs=WHOLE,
        scratch_shapes=[full_scratch(d), stack_scratch(d)],
        compiler_params=params(),
        cost_estimate=cost(2 * 4 * BLK * (tokens + TEAM_ROWS) * d, 3 * 1024 * 1024),
        name="dispatch",
    )(ids_row, ids_col, level_row, x)


def combine_kernel(ids_row, ids_col, level_col, rows, out_ref, full, *, scaled):
    tokens = ids_row.shape[1]
    ids = ids_col[...]
    earlier = lax.broadcasted_iota(jnp.int32, (tokens, tokens), 1) < lax.broadcasted_iota(
        jnp.int32, (tokens, tokens), 0
    )
    same = jnp.where(earlier & (ids == ids_row[...]), 1, 0)
    slot = ids * SLOTS + jnp.sum(same, axis=1, keepdims=True)
    shape = (tokens, 4 * BLK)
    if scaled:
        value = jnp.broadcast_to(level_col[...].astype(F32) * 0.125, shape)
    else:
        value = jnp.full(shape, 1.0, F32)
    hot = jnp.where(lax.broadcasted_iota(jnp.int32, shape, 1) == slot, value, 0.0).astype(BF)
    from_devices(rows, full)
    out_ref[...] = jnp.dot(hot, full[...], preferred_element_type=F32).astype(BF)


def combine(ids_row, ids_col, level_col, rows, scaled):
    d = rows.shape[1] * CHUNKS
    tokens = ids_row.shape[1]
    return pl.pallas_call(
        functools.partial(combine_kernel, scaled=scaled),
        out_shape=jax.ShapeDtypeStruct((tokens, d), BF),
        in_specs=[WHOLE] * 4,
        out_specs=WHOLE,
        scratch_shapes=[full_scratch(d)],
        compiler_params=params(),
        cost_estimate=cost(2 * 4 * BLK * (tokens + TEAM_ROWS) * d, 3 * 1024 * 1024),
        name="combine",
    )(ids_row, ids_col, level_col, rows)


def sort_kernel(rows, out_ref):
    from_devices(rows, out_ref)


def sort_rows(rows):
    d = rows.shape[1] * CHUNKS
    return pl.pallas_call(
        sort_kernel,
        out_shape=jax.ShapeDtypeStruct((4 * BLK, d), BF),
        in_specs=[WHOLE],
        out_specs=WHOLE,
        compiler_params=params(),
        cost_estimate=cost(2 * 4 * BLK * TEAM_ROWS * d, 3 * 1024 * 1024),
        name="sort_rows",
    )(rows)


def sum_kernel(near, far, out_ref, full, stack):
    full[...] = (near[...].astype(F32) + far[...].astype(F32)).astype(BF)
    to_devices(full, stack, out_ref)


def sum_and_sort(near, far):
    d = near.shape[1]
    return pl.pallas_call(
        sum_kernel,
        out_shape=travel_type(d),
        in_specs=[WHOLE] * 2,
        out_specs=WHOLE,
        scratch_shapes=[full_scratch(d), stack_scratch(d)],
        compiler_params=params(),
        cost_estimate=cost(2 * 4 * BLK * TEAM_ROWS * d, 5 * 1024 * 1024),
        name="sum_and_sort",
    )(near, far)


def hidden_kernel(rows, wg0, wg1, wu0, wu1, hidden, acts):
    ff = wg0.shape[1]
    for i, w in enumerate((wg0, wg1, wu0, wu1)):
        acts[:, i * ff : (i + 1) * ff] = jnp.dot(rows[...], w[...], preferred_element_type=F32)
    gate = acts[:, : 2 * ff]
    hidden[...] = (gate * jax.nn.sigmoid(gate) * acts[:, 2 * ff :]).astype(BF)


def hidden_call(rows, wg, wu):
    ff = wg[0].shape[1]
    count, d = rows.shape
    return pl.pallas_call(
        hidden_kernel,
        out_shape=[
            jax.ShapeDtypeStruct((count, 2 * ff), BF),
            jax.ShapeDtypeStruct((count, 4 * ff), F32),
        ],
        in_specs=[WHOLE] * 5,
        out_specs=[WHOLE] * 2,
        compiler_params=params(),
        cost_estimate=cost(8 * count * d * ff, 12 * 1024 * 1024),
        name="hidden",
    )(rows, *wg, *wu)


def hidden_parts(weights):
    place = [0, 0]
    half = sum(w.shape[0] for w in weights) // 2
    for w in weights:
        plane = 0 if place[0] < half else 1
        yield plane, place[plane], w.shape[0]
        place[plane] += w.shape[0]


def d_hidden_kernel(rows, *refs):
    weights, (mine, other, full) = refs[:-3], refs[-3:]
    from_devices(rows, full)
    for w, (plane, first, size) in zip(weights, hidden_parts(weights)):
        part = lax.dot_general(full[...], w[...], NT, preferred_element_type=F32)
        out = (mine, other)[plane]
        out[:, first : first + size] = part.astype(out.dtype)


def d_hidden_call(rows, wd):
    d = wd[0].shape[1]
    units = sum(w.shape[0] for w in wd)
    return pl.pallas_call(
        d_hidden_kernel,
        out_shape=[
            jax.ShapeDtypeStruct((4 * BLK, units // 2), F32),
            jax.ShapeDtypeStruct((4 * BLK, units // 2), BF),
        ],
        in_specs=[WHOLE] * (1 + len(wd)),
        out_specs=[WHOLE] * 2,
        scratch_shapes=[full_scratch(d)],
        compiler_params=params(),
        cost_estimate=cost(2 * 4 * BLK * (units + TEAM_ROWS) * d, 12 * 1024 * 1024),
        name="d_hidden",
    )(rows, *wd)


def out_kernel(near, other, *refs):
    weights, (out_ref, full, stack) = refs[:-3], refs[-3:]
    width = full.shape[1] // 4
    for q in range(4):
        cols = slice(q * width, (q + 1) * width)
        total = None
        for w, (plane, first, size) in zip(weights, hidden_parts(weights)):
            part = jnp.dot(
                (near, other)[plane][:, first : first + size],
                w[:, cols],
                preferred_element_type=F32,
            )
            total = part if total is None else total + part
        full[:, cols] = total.astype(BF)
    to_devices(full, stack, out_ref)


def out_call(near, other, wd):
    d = wd[0].shape[1]
    rows, units = near.shape
    return pl.pallas_call(
        out_kernel,
        out_shape=travel_type(d),
        in_specs=[WHOLE] * (2 + len(wd)),
        out_specs=WHOLE,
        scratch_shapes=[full_scratch(d), stack_scratch(d)],
        compiler_params=params(),
        cost_estimate=cost(2 * rows * d * (2 * units + TEAM_ROWS), 12 * 1024 * 1024),
        name="expert_out",
    )(near, other, *wd)


def grad_kernel(acts, dh, wg0, wg1, wu0, wu1, out_ref, dacts):
    ff = wg0.shape[1]
    gate = acts[:, : 2 * ff]
    up = acts[:, 2 * ff :]
    sigma = jax.nn.sigmoid(gate)
    d_hidden = dh[...].astype(F32)
    d_gate = d_hidden * up * sigma * (1.0 + gate * (1.0 - sigma))
    dacts[:, : 2 * ff] = d_gate.astype(BF)
    dacts[:, 2 * ff :] = (d_hidden * (gate * sigma)).astype(BF)
    width = out_ref.shape[1] // 4
    for q in range(4):
        cols = slice(q * width, (q + 1) * width)
        total = None
        for i, w in enumerate((wg0, wg1, wu0, wu1)):
            part = lax.dot_general(
                dacts[:, i * ff : (i + 1) * ff], w[cols, :], NT, preferred_element_type=F32
            )
            total = part if total is None else total + part
        out_ref[:, cols] = total.astype(BF)


def grad_call(acts, dh, wg, wu):
    d, ff = wg[0].shape
    rows = dh.shape[0]
    return pl.pallas_call(
        grad_kernel,
        out_shape=jax.ShapeDtypeStruct((rows, d), BF),
        in_specs=[WHOLE] * 6,
        out_specs=WHOLE,
        scratch_shapes=[pltpu.VMEM((rows, 4 * ff), BF)],
        compiler_params=params(),
        cost_estimate=cost(8 * rows * d * ff, 12 * 1024 * 1024),
        name="expert_grad",
    )(acts, dh, *wg, *wu)


HEADS_STEP = 4


def attention_kernel(q_ref, k_ref, v_ref, do_ref, o_ref, dq_ref, dk_ref, dv_ref, dk_acc, dv_acc):
    step = pl.program_id(0)
    length = k_ref.shape[0]
    scale = HD ** (-0.5)
    k = k_ref[...]
    v = v_ref[...]
    causal = lax.broadcasted_iota(jnp.int32, (length, length), 0) >= lax.broadcasted_iota(
        jnp.int32, (length, length), 1
    )
    dk = None
    dv = None
    for h in range(HEADS_STEP):
        cols = slice(h * HD, (h + 1) * HD)
        q = q_ref[:, cols]
        do = do_ref[:, cols]
        scores = lax.dot_general(q, k, NT, preferred_element_type=F32) * scale
        scores = jnp.where(causal, scores, -1e30)
        raised = jnp.exp(scores - jnp.max(scores, axis=1, keepdims=True))
        probs = raised / jnp.sum(raised, axis=1, keepdims=True)
        rounded = probs.astype(BF)
        o_ref[:, cols] = jnp.dot(rounded, v, preferred_element_type=F32).astype(BF)
        d_probs = lax.dot_general(do, v, NT, preferred_element_type=F32).astype(BF).astype(F32)
        inner = jnp.sum(d_probs * probs, axis=1, keepdims=True)
        d_scores = (probs * (d_probs - inner) * scale).astype(BF)
        dq_ref[:, cols] = jnp.dot(d_scores, k, preferred_element_type=F32).astype(BF)
        dk_part = lax.dot_general(d_scores, q, TN, preferred_element_type=F32)
        dv_part = lax.dot_general(rounded, do, TN, preferred_element_type=F32)
        dk = dk_part if dk is None else dk + dk_part
        dv = dv_part if dv is None else dv + dv_part

    @pl.when(step == 0)
    def _():
        dk_acc[...] = dk
        dv_acc[...] = dv

    @pl.when(step > 0)
    def _():
        dk_acc[...] = dk_acc[...] + dk
        dv_acc[...] = dv_acc[...] + dv

    @pl.when(step == pl.num_programs(0) - 1)
    def _():
        dk_ref[...] = dk_acc[...].astype(BF)
        dv_ref[...] = dv_acc[...].astype(BF)


def attention(queries, keys, values, cotangent):
    length, wide = queries.shape
    head_spec = pl.BlockSpec((length, HEADS_STEP * HD), lambda s: (0, s))
    key_spec = pl.BlockSpec((length, HD), lambda s: (0, 0))
    heads = wide // HD
    return pl.pallas_call(
        attention_kernel,
        out_shape=[
            jax.ShapeDtypeStruct(queries.shape, BF),
            jax.ShapeDtypeStruct(queries.shape, BF),
            jax.ShapeDtypeStruct(keys.shape, BF),
            jax.ShapeDtypeStruct(values.shape, BF),
        ],
        grid=(heads // HEADS_STEP,),
        in_specs=[head_spec, key_spec, key_spec, head_spec],
        out_specs=[head_spec, head_spec, key_spec, key_spec],
        scratch_shapes=[pltpu.VMEM((length, HD), F32)] * 2,
        compiler_params=params(dimension_semantics=("arbitrary",)),
        cost_estimate=cost(14 * heads * length * length * HD, 10 * 1024 * 1024),
        name="attention",
    )(queries, keys, values, cotangent)


def on_device(
    layer_input,
    out_grad,
    expert_ids,
    gate_level,
    w_gate,
    w_up,
    w_down,
    attn_queries,
    attn_keys,
    attn_values,
    attn_grad,
):
    tokens = layer_input.shape[0]
    ids_row = expert_ids.reshape(1, tokens)
    ids_col = expert_ids.reshape(tokens, 1)
    level_row = gate_level.reshape(1, tokens)
    level_col = gate_level.reshape(tokens, 1)
    tie = lax.optimization_barrier

    gate, up, down = w_gate[0], w_up[0], w_down[0]
    wg = (gate, send(gate, CORES))
    wu = (up, send(up, CORES))
    down_mate = send(down, CORES)
    piece_a, piece_b = jnp.split(down, [160])
    down_a = send(piece_a, INNER)

    x_sent = dispatch(ids_row, ids_col, level_row, layer_input, False)
    x_rows = exchange(x_sent)
    g_sent = dispatch(ids_row, ids_col, level_row, out_grad, True)
    attended = attention(attn_queries, attn_keys, attn_values, attn_grad)
    x_rows, g_sent, attended, wg, wu, down_mate, down_a, piece_b = tie(
        (x_rows, g_sent, attended, wg, wu, down_mate, down_a, piece_b)
    )
    x_near, g_sent = tie((sort_rows(x_rows), g_sent))
    x_far = send(x_near, INNER)
    g_rows = exchange(g_sent)
    down_b = send(piece_b, INNER)
    hidden_near, acts_near = hidden_call(x_near, wg, wu)
    x_far, hidden_near, acts_near, down_b = tie((x_far, hidden_near, acts_near, down_b))
    down_other = jnp.concatenate([down_a, down_b])
    wd = (down, down_mate, down_other, send(down_other, CORES))
    hidden_far, acts_far = hidden_call(x_far, wg, wu)
    hidden_other = send(hidden_far, INNER)

    g_rows, hidden_far = tie((g_rows, hidden_far))
    dh_near, dh_far = d_hidden_call(g_rows, wd)
    dh_other = send(dh_far, INNER)
    grad_far = grad_call(acts_far, dh_other, wg, wu)

    arrived = send(grad_far, INNER)
    hidden_other, _ = tie((hidden_other, grad_far))
    out_rows = exchange(out_call(hidden_near, hidden_other, wd))
    grad_near = grad_call(acts_near, dh_near, wg, wu)
    grad_rows = exchange(sum_and_sort(grad_near, arrived))

    moe_out = combine(ids_row, ids_col, level_col, out_rows, True)
    grad_x = combine(ids_row, ids_col, level_col, grad_rows, False)
    attn_out, grad_q, grad_k, grad_v = attended
    return (moe_out, grad_x, attn_out, grad_q, grad_k, grad_v)


def solution(mesh):
    in_specs = (
        P(("dp", "tensor"), None),
        P(("dp", "tensor"), None),
        P(("dp", "tensor"), None),
        P(("dp", "tensor"), None),
        P("dp", None, "tensor"),
        P("dp", None, "tensor"),
        P("dp", "tensor", None),
        P("dp", "tensor"),
        P("dp", "tensor"),
        P("dp", "tensor"),
        P("dp", "tensor"),
    )
    out_specs = (
        P(("dp", "tensor"), None),
        P(("dp", "tensor"), None),
        P("dp", "tensor"),
        P("dp", "tensor"),
        P("dp", "tensor"),
        P("dp", "tensor"),
    )
    return jax.shard_map(
        on_device, mesh=mesh, in_specs=in_specs, out_specs=out_specs, check_vma=False
    )
```

```python
import functools

import jax
import jax.numpy as jnp
from jax import lax
from jax.experimental import pallas as pl
from jax.experimental.pallas import tpu as pltpu
from jax.sharding import PartitionSpec as P

HD = 128
AXES = ("dp", "tensor")
SLOTS = 3
QUARTERS = 4
TEAM = 16
BLK = TEAM * SLOTS
VMEM_LIMIT = 40 * 1024 * 1024
BF = jnp.bfloat16
F32 = jnp.float32
NT = (((1,), (1,)), ((), ()))
TN = (((0,), (0,)), ((), ()))


def linear(x, y, z, core):
    return ((z // 2) * 16 + y * 4 + x) * 4 + (z % 2) * 2 + core


def moves(target):
    pairs = []
    for x in range(4):
        for y in range(4):
            for z in range(8):
                for core in range(2):
                    z_to, core_to = target(z, core)
                    pairs.append((linear(x, y, z, core), linear(x, y, z_to % 8, core_to)))
    return pairs


INNER = moves(lambda z, c: (z ^ 1, c))
CORES = moves(lambda z, c: (z, 1 - c))
NEAR = [
    moves(lambda z, c: (z - 2 if z % 2 else z + 2, c)),
    moves(lambda z, c: (z + 3 if z % 2 else z - 3, c)),
    moves(lambda z, c: (z + 1 if z % 2 else z - 1, c)),
]
BACK = [[(b, a) for a, b in perm] for perm in NEAR]
PLANES = [
    [linear(x, y, z, c) for y in range(4) for x in range(4)] for z in range(8) for c in range(2)
]


def send(value, perm):
    return lax.ppermute(value, AXES, perm)


def plane_exchange(value):
    return lax.all_to_all(value, AXES, 0, 0, axis_index_groups=PLANES, tiled=True)


def params(**more):
    return pltpu.CompilerParams(vmem_limit_bytes=VMEM_LIMIT, **more)


WHOLE = pl.BlockSpec(memory_space=pltpu.VMEM)


def cost(flops, nbytes):
    return pl.CostEstimate(flops=flops, bytes_accessed=nbytes, transcendentals=0)


def turn_of(ids, where):
    pair, odd = where[0], where[1]
    turn = ((ids >> 4) - pair) & 3
    return jnp.where(odd == 1, (4 - turn) & 3, turn)


def divide(value, by):
    return (value * ((1 << 20) // by + 1)) >> 20


def by_source_of(row):
    turn = divide(row, 192)
    rest = row - turn * 192
    quarter = divide(rest, BLK)
    rest = rest - quarter * BLK
    source = divide(rest, SLOTS)
    return source * BLK + quarter * (4 * SLOTS) + turn * SLOTS + rest - source * SLOTS


def by_turn_of(row):
    source = divide(row, BLK)
    rest = row - source * BLK
    quarter = divide(rest, 4 * SLOTS)
    rest = rest - quarter * (4 * SLOTS)
    turn = divide(rest, SLOTS)
    return turn * 192 + quarter * BLK + source * SLOTS + rest - turn * SLOTS


def one_hot(target, rows):
    row = lax.broadcasted_iota(jnp.int32, (rows, 1), 0)
    column = lax.broadcasted_iota(jnp.int32, (rows, rows), 1)
    return jnp.where(column == target(row), 1.0, 0.0).astype(BF)


def from_pair_order(part, block):
    width = part.shape[1]
    for q in range(QUARTERS):
        block[:, q * width : (q + 1) * width] = part[q * BLK : (q + 1) * BLK]


def to_source_order(blocks, stack, out_ref):
    width = stack.shape[1]
    for turn, block in enumerate(blocks):
        for q in range(QUARTERS):
            first = (turn * QUARTERS + q) * BLK
            stack[first : first + BLK, :] = block(slice(q * width, (q + 1) * width))
    order = one_hot(by_turn_of, stack.shape[0])
    out_ref[...] = jnp.dot(order, stack[...], preferred_element_type=F32).astype(BF)


def travel_type(d):
    return jax.ShapeDtypeStruct((TEAM * BLK, d // QUARTERS), BF)


def block_types(d):
    return [jax.ShapeDtypeStruct((BLK, d), BF)] * 4


def stack_scratch(d):
    return pltpu.VMEM((TEAM * BLK, d // QUARTERS), BF)


def rows_scratch(d):
    return pltpu.VMEM((4 * BLK, d), BF)


def parted(rows):
    return rows.reshape(TEAM, BLK, rows.shape[1])


def ranks(ids_row, ids_col, axis):
    tokens = ids_row.shape[1]
    shape = (tokens, tokens)
    earlier = lax.broadcasted_iota(jnp.int32, shape, axis) < lax.broadcasted_iota(
        jnp.int32, shape, 1 - axis
    )
    same = jnp.where(earlier & (ids_col[...] == ids_row[...]), 1, 0)
    return jnp.sum(same, axis=axis, keepdims=True)


def gates(level, shape, scaled):
    if scaled:
        return jnp.broadcast_to(level[...].astype(F32) * 0.125, shape)
    return jnp.full(shape, 1.0, F32)


def dispatch_plane_kernel(where, ids_row, ids_col, level_row, x_ref, out_ref, hot, quarters, *, scaled):
    tokens = ids_row.shape[1]
    ids = ids_row[...]
    rank = ranks(ids_row, ids_col, 0)
    base = (ids & 15) * BLK + turn_of(ids, where) * SLOTS + rank
    rows, width = hot.shape[0], quarters.shape[1]
    row = lax.broadcasted_iota(jnp.int32, (rows, tokens), 0)
    value = gates(level_row, (rows, tokens), scaled)
    for q in range(QUARTERS):
        part = slice(q * tokens, (q + 1) * tokens)
        hot[:, part] = jnp.where(row == base + q * (4 * SLOTS), value, 0.0).astype(BF)
        quarters[part, :] = x_ref[:, q * width : (q + 1) * width]
    out_ref[...] = jnp.dot(hot[...], quarters[...], preferred_element_type=F32).astype(BF)


def dispatch_pairs_kernel(where, ids_row, ids_col, level_row, x_ref, *outs, scaled):
    ids = ids_row[...]
    rank = ranks(ids_row, ids_col, 0)
    base = turn_of(ids, where) * BLK + (ids & 15) * SLOTS + rank
    shape = (4 * BLK, ids_row.shape[1])
    row = lax.broadcasted_iota(jnp.int32, shape, 0)
    hot = jnp.where(row == base, gates(level_row, shape, scaled), 0.0).astype(BF)
    for i, out in enumerate(outs):
        part = jnp.dot(hot[i * BLK : (i + 1) * BLK], x_ref[...], preferred_element_type=F32)
        out[...] = part.astype(BF)


def dispatch(where, ids_row, ids_col, level_row, x, scaled, by_pair):
    tokens, d = x.shape
    rows = TEAM * BLK
    if by_pair:
        kernel, out_shape, scratch = dispatch_pairs_kernel, block_types(d), []
    else:
        kernel, out_shape = dispatch_plane_kernel, [travel_type(d)]
        scratch = [pltpu.VMEM((rows, QUARTERS * tokens), BF)]
        scratch += [pltpu.VMEM((QUARTERS * tokens, d // QUARTERS), BF)]
    return pl.pallas_call(
        functools.partial(kernel, scaled=scaled),
        out_shape=out_shape,
        in_specs=[pl.BlockSpec(memory_space=pltpu.SMEM)] + [WHOLE] * 4,
        out_specs=[WHOLE] * len(out_shape),
        scratch_shapes=scratch,
        compiler_params=params(),
        cost_estimate=cost(2 * rows * tokens * d, 3 * 1024 * 1024),
        name="dispatch",
    )(where, ids_row, ids_col, level_row, x)


def combine_plane_kernel(where, ids_row, ids_col, level_col, back, out_ref, *, scaled):
    ids = ids_col[...]
    base = (ids & 15) * BLK + turn_of(ids, where) * SLOTS + ranks(ids_row, ids_col, 1)
    rows, width = back.shape
    shape = (ids_row.shape[1], rows)
    row = lax.broadcasted_iota(jnp.int32, shape, 1)
    value = gates(level_col, shape, scaled)
    for q in range(QUARTERS):
        hot = jnp.where(row == base + q * (4 * SLOTS), value, 0.0).astype(BF)
        part = jnp.dot(hot, back[...], preferred_element_type=F32)
        out_ref[:, q * width : (q + 1) * width] = part.astype(BF)


def combine_pairs_kernel(where, ids_row, ids_col, level_col, *refs, scaled):
    backs, out_ref, rows = refs[:4], refs[4], refs[5]
    ids = ids_col[...]
    base = turn_of(ids, where) * BLK + (ids & 15) * SLOTS + ranks(ids_row, ids_col, 1)
    shape = (ids_row.shape[1], 4 * BLK)
    gather_rows(backs, rows)
    row = lax.broadcasted_iota(jnp.int32, shape, 1)
    hot = jnp.where(row == base, gates(level_col, shape, scaled), 0.0).astype(BF)
    out_ref[...] = jnp.dot(hot, rows[...], preferred_element_type=F32).astype(BF)


def combine(where, ids_row, ids_col, level_col, backs, scaled, d):
    tokens = ids_row.shape[1]
    by_pair = len(backs) == 4
    return pl.pallas_call(
        functools.partial(combine_pairs_kernel if by_pair else combine_plane_kernel, scaled=scaled),
        out_shape=jax.ShapeDtypeStruct((tokens, d), BF),
        in_specs=[pl.BlockSpec(memory_space=pltpu.SMEM)] + [WHOLE] * (3 + len(backs)),
        out_specs=WHOLE,
        scratch_shapes=[rows_scratch(d)] if by_pair else [],
        compiler_params=params(),
        cost_estimate=cost(2 * TEAM * BLK * tokens * d, 3 * 1024 * 1024),
        name="combine",
    )(where, ids_row, ids_col, level_col, *backs)


def shuffle_kernel(rows_ref, *refs):
    outs, order = refs[:4], refs[4]
    order[...] = one_hot(by_source_of, order.shape[0])
    size = QUARTERS * BLK
    for turn, out in enumerate(outs):
        part = jnp.dot(
            order[turn * size : (turn + 1) * size, :], rows_ref[...], preferred_element_type=F32
        )
        from_pair_order(part.astype(BF), out)


def shuffle(rows):
    rows = rows.reshape(TEAM * BLK, rows.shape[-1])
    count, width = rows.shape
    return pl.pallas_call(
        shuffle_kernel,
        out_shape=block_types(width * QUARTERS),
        in_specs=[WHOLE],
        out_specs=[WHOLE] * 4,
        scratch_shapes=[pltpu.VMEM((count, count), BF)],
        compiler_params=params(),
        cost_estimate=cost(2 * count * count * width, 4 * count * width),
        name="shuffle",
    )(rows)


def unshuffle_kernel(*refs, summed):
    blocks, (out_ref, stack) = refs[:-2], refs[-2:]

    def own(cols):
        if summed:
            return (blocks[0][:, cols].astype(F32) + blocks[4][:, cols].astype(F32)).astype(BF)
        return blocks[0][:, cols]

    others = [lambda cols, block=block: block[:, cols] for block in blocks[1:4]]
    to_source_order([own] + others, stack, out_ref)


def unshuffle(blocks):
    d = blocks[0].shape[1]
    rows = TEAM * BLK
    out = pl.pallas_call(
        functools.partial(unshuffle_kernel, summed=len(blocks) == 5),
        out_shape=travel_type(d),
        in_specs=[WHOLE] * len(blocks),
        out_specs=WHOLE,
        scratch_shapes=[stack_scratch(d)],
        compiler_params=params(),
        cost_estimate=cost(2 * rows * rows * d // QUARTERS, 3 * 1024 * 1024),
        name="unshuffle",
    )(*blocks)
    return parted(out)


def gather_rows(blocks, rows):
    for i, block in enumerate(blocks):
        rows[i * BLK : (i + 1) * BLK, :] = block[...]


def hidden_kernel(b0, b1, b2, b3, wg0, wg1, wu0, wu1, hidden, acts, rows):
    gather_rows((b0, b1, b2, b3), rows)
    ff = wg0.shape[1]
    for i, w in enumerate((wg0, wg1, wu0, wu1)):
        acts[:, i * ff : (i + 1) * ff] = jnp.dot(rows[...], w[...], preferred_element_type=F32)
    gate = acts[:, : 2 * ff]
    hidden[...] = (gate * jax.nn.sigmoid(gate) * acts[:, 2 * ff :]).astype(BF)


def hidden_call(blocks, wg, wu):
    d, ff = wg[0].shape
    count = 4 * BLK
    return pl.pallas_call(
        hidden_kernel,
        out_shape=[
            jax.ShapeDtypeStruct((count, 2 * ff), BF),
            jax.ShapeDtypeStruct((count, 4 * ff), F32),
        ],
        in_specs=[WHOLE] * 8,
        out_specs=[WHOLE] * 2,
        scratch_shapes=[rows_scratch(d)],
        compiler_params=params(),
        cost_estimate=cost(8 * count * d * ff, 12 * 1024 * 1024),
        name="hidden",
    )(*blocks, *wg, *wu)


def hidden_parts(weights):
    place = [0, 0]
    half = sum(w.shape[0] for w in weights) // 2
    for w in weights:
        plane = 0 if place[0] < half else 1
        yield plane, place[plane], w.shape[0]
        place[plane] += w.shape[0]


def d_hidden_kernel(b0, b1, b2, b3, *refs):
    weights, (mine, other, rows) = refs[:-3], refs[-3:]
    gather_rows((b0, b1, b2, b3), rows)
    for w, (plane, first, size) in zip(weights, hidden_parts(weights)):
        part = lax.dot_general(rows[...], w[...], NT, preferred_element_type=F32)
        out = (mine, other)[plane]
        out[:, first : first + size] = part.astype(out.dtype)


def d_hidden_call(blocks, wd):
    d = wd[0].shape[1]
    units = sum(w.shape[0] for w in wd)
    return pl.pallas_call(
        d_hidden_kernel,
        out_shape=[
            jax.ShapeDtypeStruct((4 * BLK, units // 2), F32),
            jax.ShapeDtypeStruct((4 * BLK, units // 2), BF),
        ],
        in_specs=[WHOLE] * (4 + len(wd)),
        out_specs=[WHOLE] * 2,
        scratch_shapes=[rows_scratch(d)],
        compiler_params=params(),
        cost_estimate=cost(8 * BLK * units * d, 12 * 1024 * 1024),
        name="d_hidden",
    )(*blocks, *wd)


def out_kernel(near, other, *refs):
    weights, (out_ref, rows, stack) = refs[:-3], refs[-3:]
    width = rows.shape[1] // 4
    for q in range(4):
        cols = slice(q * width, (q + 1) * width)
        total = None
        for w, (plane, first, size) in zip(weights, hidden_parts(weights)):
            part = jnp.dot(
                (near, other)[plane][:, first : first + size],
                w[:, cols],
                preferred_element_type=F32,
            )
            total = part if total is None else total + part
        rows[:, cols] = total.astype(BF)
    blocks = [lambda cols, i=i: rows[i * BLK : (i + 1) * BLK, cols] for i in range(4)]
    to_source_order(blocks, stack, out_ref)


def out_call(near, other, wd):
    d = wd[0].shape[1]
    rows, units = near.shape
    out = pl.pallas_call(
        out_kernel,
        out_shape=travel_type(d),
        in_specs=[WHOLE] * (2 + len(wd)),
        out_specs=WHOLE,
        scratch_shapes=[rows_scratch(d), stack_scratch(d)],
        compiler_params=params(),
        cost_estimate=cost(4 * rows * d * units, 12 * 1024 * 1024),
        name="expert_out",
    )(near, other, *wd)
    return parted(out)


def grad_kernel(acts, dh, wg0, wg1, wu0, wu1, *refs):
    outs, dacts = refs[:4], refs[4]
    ff = wg0.shape[1]
    gate = acts[:, : 2 * ff]
    up = acts[:, 2 * ff :]
    sigma = jax.nn.sigmoid(gate)
    d_hidden = dh[...].astype(F32)
    d_gate = d_hidden * up * sigma * (1.0 + gate * (1.0 - sigma))
    dacts[:, : 2 * ff] = d_gate.astype(BF)
    dacts[:, 2 * ff :] = (d_hidden * (gate * sigma)).astype(BF)
    width = outs[0].shape[1] // 4
    for q in range(4):
        cols = slice(q * width, (q + 1) * width)
        total = None
        for i, w in enumerate((wg0, wg1, wu0, wu1)):
            part = lax.dot_general(
                dacts[:, i * ff : (i + 1) * ff], w[cols, :], NT, preferred_element_type=F32
            )
            total = part if total is None else total + part
        for i, out in enumerate(outs):
            out[:, cols] = total[i * BLK : (i + 1) * BLK].astype(BF)


def grad_call(acts, dh, wg, wu):
    d, ff = wg[0].shape
    rows = dh.shape[0]
    return pl.pallas_call(
        grad_kernel,
        out_shape=block_types(d),
        in_specs=[WHOLE] * 6,
        out_specs=[WHOLE] * 4,
        scratch_shapes=[pltpu.VMEM((rows, 4 * ff), BF)],
        compiler_params=params(),
        cost_estimate=cost(8 * rows * d * ff, 12 * 1024 * 1024),
        name="expert_grad",
    )(acts, dh, *wg, *wu)


HEADS_STEP = 4


def attention_kernel(q_ref, k_ref, v_ref, do_ref, o_ref, dq_ref, dk_ref, dv_ref, dk_acc, dv_acc):
    step = pl.program_id(0)
    length = k_ref.shape[0]
    scale = HD ** (-0.5)
    k = k_ref[...]
    v = v_ref[...]
    causal = lax.broadcasted_iota(jnp.int32, (length, length), 0) >= lax.broadcasted_iota(
        jnp.int32, (length, length), 1
    )
    dk = None
    dv = None
    for h in range(HEADS_STEP):
        cols = slice(h * HD, (h + 1) * HD)
        q = q_ref[:, cols]
        do = do_ref[:, cols]
        scores = lax.dot_general(q, k, NT, preferred_element_type=F32) * scale
        scores = jnp.where(causal, scores, -1e30)
        raised = jnp.exp(scores - jnp.max(scores, axis=1, keepdims=True))
        probs = raised / jnp.sum(raised, axis=1, keepdims=True)
        rounded = probs.astype(BF)
        o_ref[:, cols] = jnp.dot(rounded, v, preferred_element_type=F32).astype(BF)
        d_probs = lax.dot_general(do, v, NT, preferred_element_type=F32).astype(BF).astype(F32)
        inner = jnp.sum(d_probs * probs, axis=1, keepdims=True)
        d_scores = (probs * (d_probs - inner) * scale).astype(BF)
        dq_ref[:, cols] = jnp.dot(d_scores, k, preferred_element_type=F32).astype(BF)
        dk_part = lax.dot_general(d_scores, q, TN, preferred_element_type=F32)
        dv_part = lax.dot_general(rounded, do, TN, preferred_element_type=F32)
        dk = dk_part if dk is None else dk + dk_part
        dv = dv_part if dv is None else dv + dv_part

    @pl.when(step == 0)
    def _():
        dk_acc[...] = dk
        dv_acc[...] = dv

    @pl.when(step > 0)
    def _():
        dk_acc[...] = dk_acc[...] + dk
        dv_acc[...] = dv_acc[...] + dv

    @pl.when(step == pl.num_programs(0) - 1)
    def _():
        dk_ref[...] = dk_acc[...].astype(BF)
        dv_ref[...] = dv_acc[...].astype(BF)


def attention(queries, keys, values, cotangent):
    length, wide = queries.shape
    head_spec = pl.BlockSpec((length, HEADS_STEP * HD), lambda s: (0, s))
    key_spec = pl.BlockSpec((length, HD), lambda s: (0, 0))
    heads = wide // HD
    return pl.pallas_call(
        attention_kernel,
        out_shape=[
            jax.ShapeDtypeStruct(queries.shape, BF),
            jax.ShapeDtypeStruct(queries.shape, BF),
            jax.ShapeDtypeStruct(keys.shape, BF),
            jax.ShapeDtypeStruct(values.shape, BF),
        ],
        grid=(heads // HEADS_STEP,),
        in_specs=[head_spec, key_spec, key_spec, head_spec],
        out_specs=[head_spec, head_spec, key_spec, key_spec],
        scratch_shapes=[pltpu.VMEM((length, HD), F32)] * 2,
        compiler_params=params(dimension_semantics=("arbitrary",)),
        cost_estimate=cost(14 * heads * length * length * HD, 10 * 1024 * 1024),
        name="attention",
    )(queries, keys, values, cotangent)


def on_device(
    layer_input,
    out_grad,
    expert_ids,
    gate_level,
    w_gate,
    w_up,
    w_down,
    attn_queries,
    attn_keys,
    attn_values,
    attn_grad,
):
    tokens, d = layer_input.shape
    where = jnp.stack([lax.axis_index("dp") // 16, lax.axis_index("tensor") // 2]).astype(jnp.int32)
    ids_row = expert_ids.reshape(1, tokens)
    ids_col = expert_ids.reshape(tokens, 1)
    level_row = gate_level.reshape(1, tokens)
    level_col = gate_level.reshape(tokens, 1)
    tie = lax.optimization_barrier

    gate, up, down = w_gate[0], w_up[0], w_down[0]
    gate_mate, up_mate, down_mate = send(gate, CORES), send(up, CORES), send(down, CORES)
    piece_a, piece_b = jnp.split(down, 2)
    down_a = send(piece_a, INNER)

    (x_sent,) = dispatch(where, ids_row, ids_col, level_row, layer_input, False, False)
    x_rows = plane_exchange(parted(x_sent))
    g_sent = dispatch(where, ids_row, ids_col, level_row, out_grad, True, True)
    g_sent, gate_mate, up_mate, down_mate, down_a, piece_b = tie(
        (g_sent, gate_mate, up_mate, down_mate, down_a, piece_b)
    )
    g_near = [g_sent[0]] + [send(block, perm) for block, perm in zip(g_sent[1:], NEAR)]
    down_b = send(piece_b, INNER)
    attended = attention(attn_queries, attn_keys, attn_values, attn_grad)
    x_rows, attended = tie((x_rows, attended))
    (x_own, x_one, x_two, x_three), g_near, down_b = tie((shuffle(x_rows), g_near, down_b))
    x_two_near = send(x_two, NEAR[1])
    x_own_far = send(x_own, INNER)
    g_rows = plane_exchange(unshuffle(g_near))
    x_one, x_three, x_two_near, x_own_far = tie((x_one, x_three, x_two_near, x_own_far))
    x_one_near = send(x_one, NEAR[0])
    x_three_near = send(x_three, NEAR[2])
    x_two_far = send(x_two_near, INNER)
    g_rows, x_two_far, _ = tie((g_rows, x_two_far, [x_one_near, x_three_near]))
    wg, wu = (gate, gate_mate), (up, up_mate)
    wd = (down, down_mate, down_a, down_b, send(down_a, CORES), send(down_b, CORES))
    x_one_far = send(x_one_near, INNER)
    x_three_far = send(x_three_near, INNER)
    hidden_near, acts_near = hidden_call([x_own, x_one_near, x_two_near, x_three_near], wg, wu)

    dh_near, dh_far = d_hidden_call(shuffle(g_rows), wd)
    dh_other = send(dh_far, INNER)
    x_far, _, _ = tie(([x_own_far, x_one_far, x_two_far, x_three_far], dh_far, hidden_near))
    hidden_far, acts_far = hidden_call(x_far, wg, wu)
    terms = grad_call(acts_far, dh_other, wg, wu)

    arrived = [send(term, INNER) for term in terms[1:]]
    hidden_other = send(hidden_far, INNER)
    near_terms = grad_call(acts_near, dh_near, wg, wu)
    out_sent = out_call(hidden_near, hidden_other, wd)
    out_rows = plane_exchange(out_sent)
    near_terms, own_term, arrived, _ = tie((near_terms, terms[0], arrived, out_sent))
    own_arrived = send(own_term, INNER)
    totals = [(a.astype(F32) + b.astype(F32)).astype(BF) for a, b in zip(near_terms[1:], arrived)]
    backs = [send(total, perm) for total, perm in zip(totals, BACK)]
    (out_own, out_one, out_two, out_three), backs = tie((shuffle(out_rows), backs))
    grad_rows = plane_exchange(unshuffle([near_terms[0]] + backs + [own_arrived]))
    out_two = send(out_two, BACK[1])
    out_one, out_three, out_two = tie((out_one, out_three, out_two))
    out_back = [out_own, send(out_one, BACK[0]), out_two, send(out_three, BACK[2])]

    grad_back = [grad_rows.reshape(TEAM * BLK, d // QUARTERS)]
    moe_out = combine(where, ids_row, ids_col, level_col, out_back, True, d)
    grad_x = combine(where, ids_row, ids_col, level_col, grad_back, False, d)
    attn_out, grad_q, grad_k, grad_v = attended
    return (moe_out, grad_x, attn_out, grad_q, grad_k, grad_v)


def solution(mesh):
    in_specs = (
        P(("dp", "tensor"), None),
        P(("dp", "tensor"), None),
        P(("dp", "tensor"), None),
        P(("dp", "tensor"), None),
        P("dp", None, "tensor"),
        P("dp", None, "tensor"),
        P("dp", "tensor", None),
        P("dp", "tensor"),
        P("dp", "tensor"),
        P("dp", "tensor"),
        P("dp", "tensor"),
    )
    out_specs = (
        P(("dp", "tensor"), None),
        P(("dp", "tensor"), None),
        P("dp", "tensor"),
        P("dp", "tensor"),
        P("dp", "tensor"),
        P("dp", "tensor"),
    )
    return jax.shard_map(
        on_device, mesh=mesh, in_specs=in_specs, out_specs=out_specs, check_vma=False
    )
```

```python
import functools

import jax
import jax.numpy as jnp
from jax import lax
from jax.experimental import pallas as pl
from jax.experimental.pallas import tpu as pltpu
from jax.sharding import PartitionSpec as P

HD = 128
AXES = ("dp", "tensor")
SLOTS = 3
QUARTERS = 4
TEAM = 16
BLK = TEAM * SLOTS
VMEM_LIMIT = 40 * 1024 * 1024
BF = jnp.bfloat16
F32 = jnp.float32
NT = (((1,), (1,)), ((), ()))
TN = (((0,), (0,)), ((), ()))


def linear(x, y, z, core):
    return ((z // 2) * 16 + y * 4 + x) * 4 + (z % 2) * 2 + core


def moves(target):
    pairs = []
    for x in range(4):
        for y in range(4):
            for z in range(8):
                for core in range(2):
                    z_to, core_to = target(z, core)
                    pairs.append((linear(x, y, z, core), linear(x, y, z_to % 8, core_to)))
    return pairs


INNER = moves(lambda z, c: (z ^ 1, c))
CORES = moves(lambda z, c: (z, 1 - c))
NEAR = [
    moves(lambda z, c: (z - 2 if z % 2 else z + 2, c)),
    moves(lambda z, c: (z + 3 if z % 2 else z - 3, c)),
    moves(lambda z, c: (z + 1 if z % 2 else z - 1, c)),
]
BACK = [[(b, a) for a, b in perm] for perm in NEAR]
PLANES = [
    [linear(x, y, z, c) for y in range(4) for x in range(4)] for z in range(8) for c in range(2)
]


def send(value, perm):
    return lax.ppermute(value, AXES, perm)


def plane_exchange(value):
    return lax.all_to_all(value, AXES, 0, 0, axis_index_groups=PLANES, tiled=True)


def params(**more):
    return pltpu.CompilerParams(vmem_limit_bytes=VMEM_LIMIT, **more)


WHOLE = pl.BlockSpec(memory_space=pltpu.VMEM)


def cost(flops, nbytes):
    return pl.CostEstimate(flops=flops, bytes_accessed=nbytes, transcendentals=0)


def turn_of(ids, where):
    pair, odd = where[0], where[1]
    turn = ((ids >> 4) - pair) & 3
    return jnp.where(odd == 1, (4 - turn) & 3, turn)


def divide(value, by):
    return (value * ((1 << 20) // by + 1)) >> 20


def by_source_of(row):
    turn = divide(row, 192)
    rest = row - turn * 192
    quarter = divide(rest, BLK)
    rest = rest - quarter * BLK
    source = divide(rest, SLOTS)
    return source * BLK + quarter * (4 * SLOTS) + turn * SLOTS + rest - source * SLOTS


def by_turn_of(row):
    source = divide(row, BLK)
    rest = row - source * BLK
    quarter = divide(rest, 4 * SLOTS)
    rest = rest - quarter * (4 * SLOTS)
    turn = divide(rest, SLOTS)
    return turn * 192 + quarter * BLK + source * SLOTS + rest - turn * SLOTS


def one_hot(target, rows):
    row = lax.broadcasted_iota(jnp.int32, (rows, 1), 0)
    column = lax.broadcasted_iota(jnp.int32, (rows, rows), 1)
    return jnp.where(column == target(row), 1.0, 0.0).astype(BF)


def from_pair_order(part, block):
    width = part.shape[1]
    for q in range(QUARTERS):
        block[:, q * width : (q + 1) * width] = part[q * BLK : (q + 1) * BLK]


def to_source_order(blocks, stack, out_ref):
    width = stack.shape[1]
    for turn, block in enumerate(blocks):
        for q in range(QUARTERS):
            first = (turn * QUARTERS + q) * BLK
            stack[first : first + BLK, :] = block(slice(q * width, (q + 1) * width))
    order = one_hot(by_turn_of, stack.shape[0])
    out_ref[...] = jnp.dot(order, stack[...], preferred_element_type=F32).astype(BF)


def travel_type(d):
    return jax.ShapeDtypeStruct((TEAM * BLK, d // QUARTERS), BF)


def block_types(d):
    return [jax.ShapeDtypeStruct((BLK, d), BF)] * 4


def stack_scratch(d):
    return pltpu.VMEM((TEAM * BLK, d // QUARTERS), BF)


def rows_scratch(d):
    return pltpu.VMEM((4 * BLK, d), BF)


def parted(rows):
    return rows.reshape(TEAM, BLK, rows.shape[1])


def ranks(ids_row, ids_col, axis):
    tokens = ids_row.shape[1]
    shape = (tokens, tokens)
    earlier = lax.broadcasted_iota(jnp.int32, shape, axis) < lax.broadcasted_iota(
        jnp.int32, shape, 1 - axis
    )
    same = jnp.where(earlier & (ids_col[...] == ids_row[...]), 1, 0)
    return jnp.sum(same, axis=axis, keepdims=True)


def gates(level, shape, scaled):
    if scaled:
        return jnp.broadcast_to(level[...].astype(F32) * 0.125, shape)
    return jnp.full(shape, 1.0, F32)


def dispatch_kernel(where, ids_row, ids_col, level_row, x_ref, out_ref, hot, quarters, *, scaled):
    tokens = ids_row.shape[1]
    ids = ids_row[...]
    rank = ranks(ids_row, ids_col, 0)
    base = (ids & 15) * BLK + turn_of(ids, where) * SLOTS + rank
    rows, width = hot.shape[0], quarters.shape[1]
    row = lax.broadcasted_iota(jnp.int32, (rows, tokens), 0)
    value = gates(level_row, (rows, tokens), scaled)
    for q in range(QUARTERS):
        part = slice(q * tokens, (q + 1) * tokens)
        hot[:, part] = jnp.where(row == base + q * (4 * SLOTS), value, 0.0).astype(BF)
        quarters[part, :] = x_ref[:, q * width : (q + 1) * width]
    out_ref[...] = jnp.dot(hot[...], quarters[...], preferred_element_type=F32).astype(BF)


def dispatch(where, ids_row, ids_col, level_row, x, scaled):
    tokens, d = x.shape
    rows = TEAM * BLK
    return pl.pallas_call(
        functools.partial(dispatch_kernel, scaled=scaled),
        out_shape=travel_type(d),
        in_specs=[pl.BlockSpec(memory_space=pltpu.SMEM)] + [WHOLE] * 4,
        out_specs=WHOLE,
        scratch_shapes=[
            pltpu.VMEM((rows, QUARTERS * tokens), BF),
            pltpu.VMEM((QUARTERS * tokens, d // QUARTERS), BF),
        ],
        compiler_params=params(),
        cost_estimate=cost(2 * rows * tokens * d, 3 * 1024 * 1024),
        name="dispatch",
    )(where, ids_row, ids_col, level_row, x)


def combine_plane_kernel(where, ids_row, ids_col, level_col, back, out_ref, *, scaled):
    ids = ids_col[...]
    base = (ids & 15) * BLK + turn_of(ids, where) * SLOTS + ranks(ids_row, ids_col, 1)
    rows, width = back.shape
    shape = (ids_row.shape[1], rows)
    row = lax.broadcasted_iota(jnp.int32, shape, 1)
    value = gates(level_col, shape, scaled)
    for q in range(QUARTERS):
        hot = jnp.where(row == base + q * (4 * SLOTS), value, 0.0).astype(BF)
        part = jnp.dot(hot, back[...], preferred_element_type=F32)
        out_ref[:, q * width : (q + 1) * width] = part.astype(BF)


def combine_pairs_kernel(where, ids_row, ids_col, level_col, *refs, scaled):
    backs, out_ref, rows = refs[:4], refs[4], refs[5]
    ids = ids_col[...]
    base = turn_of(ids, where) * BLK + (ids & 15) * SLOTS + ranks(ids_row, ids_col, 1)
    shape = (ids_row.shape[1], 4 * BLK)
    gather_rows(backs, rows)
    row = lax.broadcasted_iota(jnp.int32, shape, 1)
    hot = jnp.where(row == base, gates(level_col, shape, scaled), 0.0).astype(BF)
    out_ref[...] = jnp.dot(hot, rows[...], preferred_element_type=F32).astype(BF)


def combine(where, ids_row, ids_col, level_col, backs, scaled, d):
    tokens = ids_row.shape[1]
    by_pair = len(backs) == 4
    return pl.pallas_call(
        functools.partial(combine_pairs_kernel if by_pair else combine_plane_kernel, scaled=scaled),
        out_shape=jax.ShapeDtypeStruct((tokens, d), BF),
        in_specs=[pl.BlockSpec(memory_space=pltpu.SMEM)] + [WHOLE] * (3 + len(backs)),
        out_specs=WHOLE,
        scratch_shapes=[rows_scratch(d)] if by_pair else [],
        compiler_params=params(),
        cost_estimate=cost(2 * TEAM * BLK * tokens * d, 3 * 1024 * 1024),
        name="combine",
    )(where, ids_row, ids_col, level_col, *backs)


def shuffle_kernel(rows_ref, *refs):
    outs, order = refs[:4], refs[4]
    order[...] = one_hot(by_source_of, order.shape[0])
    size = QUARTERS * BLK
    for turn, out in enumerate(outs):
        part = jnp.dot(
            order[turn * size : (turn + 1) * size, :], rows_ref[...], preferred_element_type=F32
        )
        from_pair_order(part.astype(BF), out)


def shuffle(rows):
    rows = rows.reshape(TEAM * BLK, rows.shape[-1])
    count, width = rows.shape
    return pl.pallas_call(
        shuffle_kernel,
        out_shape=block_types(width * QUARTERS),
        in_specs=[WHOLE],
        out_specs=[WHOLE] * 4,
        scratch_shapes=[pltpu.VMEM((count, count), BF)],
        compiler_params=params(),
        cost_estimate=cost(2 * count * count * width, 4 * count * width),
        name="shuffle",
    )(rows)


def unshuffle_kernel(*refs, summed):
    blocks, (out_ref, stack) = refs[:-2], refs[-2:]

    def own(cols):
        if summed:
            return (blocks[0][:, cols].astype(F32) + blocks[4][:, cols].astype(F32)).astype(BF)
        return blocks[0][:, cols]

    others = [lambda cols, block=block: block[:, cols] for block in blocks[1:4]]
    to_source_order([own] + others, stack, out_ref)


def unshuffle(blocks):
    d = blocks[0].shape[1]
    rows = TEAM * BLK
    out = pl.pallas_call(
        functools.partial(unshuffle_kernel, summed=len(blocks) == 5),
        out_shape=travel_type(d),
        in_specs=[WHOLE] * len(blocks),
        out_specs=WHOLE,
        scratch_shapes=[stack_scratch(d)],
        compiler_params=params(),
        cost_estimate=cost(2 * rows * rows * d // QUARTERS, 3 * 1024 * 1024),
        name="unshuffle",
    )(*blocks)
    return parted(out)


def gather_rows(blocks, rows):
    for i, block in enumerate(blocks):
        rows[i * BLK : (i + 1) * BLK, :] = block[...]


def hidden_kernel(b0, b1, b2, b3, wg0, wg1, wu0, wu1, hidden, acts, rows):
    gather_rows((b0, b1, b2, b3), rows)
    ff = wg0.shape[1]
    for i, w in enumerate((wg0, wg1, wu0, wu1)):
        acts[:, i * ff : (i + 1) * ff] = jnp.dot(rows[...], w[...], preferred_element_type=F32)
    gate = acts[:, : 2 * ff]
    hidden[...] = (gate * jax.nn.sigmoid(gate) * acts[:, 2 * ff :]).astype(BF)


def hidden_call(blocks, wg, wu):
    d, ff = wg[0].shape
    count = 4 * BLK
    return pl.pallas_call(
        hidden_kernel,
        out_shape=[
            jax.ShapeDtypeStruct((count, 2 * ff), BF),
            jax.ShapeDtypeStruct((count, 4 * ff), F32),
        ],
        in_specs=[WHOLE] * 8,
        out_specs=[WHOLE] * 2,
        scratch_shapes=[rows_scratch(d)],
        compiler_params=params(),
        cost_estimate=cost(8 * count * d * ff, 12 * 1024 * 1024),
        name="hidden",
    )(*blocks, *wg, *wu)


def hidden_parts(weights):
    place = [0, 0]
    half = sum(w.shape[0] for w in weights) // 2
    for w in weights:
        plane = 0 if place[0] < half else 1
        yield plane, place[plane], w.shape[0]
        place[plane] += w.shape[0]


def d_hidden_kernel(b0, b1, b2, b3, *refs):
    weights, (mine, other, rows) = refs[:-3], refs[-3:]
    gather_rows((b0, b1, b2, b3), rows)
    for w, (plane, first, size) in zip(weights, hidden_parts(weights)):
        part = lax.dot_general(rows[...], w[...], NT, preferred_element_type=F32)
        out = (mine, other)[plane]
        out[:, first : first + size] = part.astype(out.dtype)


def d_hidden_call(blocks, wd):
    d = wd[0].shape[1]
    units = sum(w.shape[0] for w in wd)
    return pl.pallas_call(
        d_hidden_kernel,
        out_shape=[
            jax.ShapeDtypeStruct((4 * BLK, units // 2), F32),
            jax.ShapeDtypeStruct((4 * BLK, units // 2), BF),
        ],
        in_specs=[WHOLE] * (4 + len(wd)),
        out_specs=[WHOLE] * 2,
        scratch_shapes=[rows_scratch(d)],
        compiler_params=params(),
        cost_estimate=cost(8 * BLK * units * d, 12 * 1024 * 1024),
        name="d_hidden",
    )(*blocks, *wd)


def out_kernel(near, other, *refs):
    weights, (out_ref, rows, stack) = refs[:-3], refs[-3:]
    width = rows.shape[1] // 4
    for q in range(4):
        cols = slice(q * width, (q + 1) * width)
        total = None
        for w, (plane, first, size) in zip(weights, hidden_parts(weights)):
            part = jnp.dot(
                (near, other)[plane][:, first : first + size],
                w[:, cols],
                preferred_element_type=F32,
            )
            total = part if total is None else total + part
        rows[:, cols] = total.astype(BF)
    blocks = [lambda cols, i=i: rows[i * BLK : (i + 1) * BLK, cols] for i in range(4)]
    to_source_order(blocks, stack, out_ref)


def out_call(near, other, wd):
    d = wd[0].shape[1]
    rows, units = near.shape
    out = pl.pallas_call(
        out_kernel,
        out_shape=travel_type(d),
        in_specs=[WHOLE] * (2 + len(wd)),
        out_specs=WHOLE,
        scratch_shapes=[rows_scratch(d), stack_scratch(d)],
        compiler_params=params(),
        cost_estimate=cost(4 * rows * d * units, 12 * 1024 * 1024),
        name="expert_out",
    )(near, other, *wd)
    return parted(out)


def grad_kernel(acts, dh, wg0, wg1, wu0, wu1, *refs):
    outs, dacts = refs[:4], refs[4]
    ff = wg0.shape[1]
    gate = acts[:, : 2 * ff]
    up = acts[:, 2 * ff :]
    sigma = jax.nn.sigmoid(gate)
    d_hidden = dh[...].astype(F32)
    d_gate = d_hidden * up * sigma * (1.0 + gate * (1.0 - sigma))
    dacts[:, : 2 * ff] = d_gate.astype(BF)
    dacts[:, 2 * ff :] = (d_hidden * (gate * sigma)).astype(BF)
    width = outs[0].shape[1] // 4
    for q in range(4):
        cols = slice(q * width, (q + 1) * width)
        total = None
        for i, w in enumerate((wg0, wg1, wu0, wu1)):
            part = lax.dot_general(
                dacts[:, i * ff : (i + 1) * ff], w[cols, :], NT, preferred_element_type=F32
            )
            total = part if total is None else total + part
        for i, out in enumerate(outs):
            out[:, cols] = total[i * BLK : (i + 1) * BLK].astype(BF)


def grad_call(acts, dh, wg, wu):
    d, ff = wg[0].shape
    rows = dh.shape[0]
    return pl.pallas_call(
        grad_kernel,
        out_shape=block_types(d),
        in_specs=[WHOLE] * 6,
        out_specs=[WHOLE] * 4,
        scratch_shapes=[pltpu.VMEM((rows, 4 * ff), BF)],
        compiler_params=params(),
        cost_estimate=cost(8 * rows * d * ff, 12 * 1024 * 1024),
        name="expert_grad",
    )(acts, dh, *wg, *wu)


HEADS_STEP = 4


def attention_kernel(q_ref, k_ref, v_ref, do_ref, o_ref, dq_ref, dk_ref, dv_ref, dk_acc, dv_acc):
    step = pl.program_id(0)
    length = k_ref.shape[0]
    scale = HD ** (-0.5)
    k = k_ref[...]
    v = v_ref[...]
    causal = lax.broadcasted_iota(jnp.int32, (length, length), 0) >= lax.broadcasted_iota(
        jnp.int32, (length, length), 1
    )
    dk = None
    dv = None
    for h in range(HEADS_STEP):
        cols = slice(h * HD, (h + 1) * HD)
        q = q_ref[:, cols]
        do = do_ref[:, cols]
        scores = lax.dot_general(q, k, NT, preferred_element_type=F32) * scale
        scores = jnp.where(causal, scores, -1e30)
        raised = jnp.exp(scores - jnp.max(scores, axis=1, keepdims=True))
        probs = raised / jnp.sum(raised, axis=1, keepdims=True)
        rounded = probs.astype(BF)
        o_ref[:, cols] = jnp.dot(rounded, v, preferred_element_type=F32).astype(BF)
        d_probs = lax.dot_general(do, v, NT, preferred_element_type=F32).astype(BF).astype(F32)
        inner = jnp.sum(d_probs * probs, axis=1, keepdims=True)
        d_scores = (probs * (d_probs - inner) * scale).astype(BF)
        dq_ref[:, cols] = jnp.dot(d_scores, k, preferred_element_type=F32).astype(BF)
        dk_part = lax.dot_general(d_scores, q, TN, preferred_element_type=F32)
        dv_part = lax.dot_general(rounded, do, TN, preferred_element_type=F32)
        dk = dk_part if dk is None else dk + dk_part
        dv = dv_part if dv is None else dv + dv_part

    @pl.when(step == 0)
    def _():
        dk_acc[...] = dk
        dv_acc[...] = dv

    @pl.when(step > 0)
    def _():
        dk_acc[...] = dk_acc[...] + dk
        dv_acc[...] = dv_acc[...] + dv

    @pl.when(step == pl.num_programs(0) - 1)
    def _():
        dk_ref[...] = dk_acc[...].astype(BF)
        dv_ref[...] = dv_acc[...].astype(BF)


def attention(queries, keys, values, cotangent):
    length, wide = queries.shape
    head_spec = pl.BlockSpec((length, HEADS_STEP * HD), lambda s: (0, s))
    key_spec = pl.BlockSpec((length, HD), lambda s: (0, 0))
    heads = wide // HD
    return pl.pallas_call(
        attention_kernel,
        out_shape=[
            jax.ShapeDtypeStruct(queries.shape, BF),
            jax.ShapeDtypeStruct(queries.shape, BF),
            jax.ShapeDtypeStruct(keys.shape, BF),
            jax.ShapeDtypeStruct(values.shape, BF),
        ],
        grid=(heads // HEADS_STEP,),
        in_specs=[head_spec, key_spec, key_spec, head_spec],
        out_specs=[head_spec, head_spec, key_spec, key_spec],
        scratch_shapes=[pltpu.VMEM((length, HD), F32)] * 2,
        compiler_params=params(dimension_semantics=("arbitrary",)),
        cost_estimate=cost(14 * heads * length * length * HD, 10 * 1024 * 1024),
        name="attention",
    )(queries, keys, values, cotangent)


def on_device(
    layer_input,
    out_grad,
    expert_ids,
    gate_level,
    w_gate,
    w_up,
    w_down,
    attn_queries,
    attn_keys,
    attn_values,
    attn_grad,
):
    tokens, d = layer_input.shape
    where = jnp.stack([lax.axis_index("dp") // 16, lax.axis_index("tensor") // 2]).astype(jnp.int32)
    ids_row = expert_ids.reshape(1, tokens)
    ids_col = expert_ids.reshape(tokens, 1)
    level_row = gate_level.reshape(1, tokens)
    level_col = gate_level.reshape(tokens, 1)
    tie = lax.optimization_barrier

    gate, up, down = w_gate[0], w_up[0], w_down[0]
    down_other = send(down, INNER)
    mates = [send(w, CORES) for w in (gate, up, down)]

    x_sent = dispatch(where, ids_row, ids_col, level_row, layer_input, False)
    g_sent = dispatch(where, ids_row, ids_col, level_row, out_grad, True)
    x_rows = plane_exchange(parted(x_sent))
    attended = attention(attn_queries, attn_keys, attn_values, attn_grad)
    x_rows, g_sent, attended, mates = tie((x_rows, g_sent, attended, mates))
    g_rows = plane_exchange(parted(g_sent))
    x_own, x_one, x_two, x_three = shuffle(x_rows)
    x_two_near = send(x_two, NEAR[1])
    x_own_far = send(x_own, INNER)
    x_one, x_three, x_two_near, x_own_far, down_other = tie(
        (x_one, x_three, x_two_near, x_own_far, down_other)
    )
    x_one_near = send(x_one, NEAR[0])
    x_three_near = send(x_three, NEAR[2])
    x_two_far = send(x_two_near, INNER)
    wg, wu = (gate, mates[0]), (up, mates[1])
    wd = (down, mates[2], down_other, send(down_other, CORES))
    g_blocks, x_one_near, x_three_near = tie((shuffle(g_rows), x_one_near, x_three_near))
    x_one_far = send(x_one_near, INNER)
    x_three_far = send(x_three_near, INNER)
    g_near = [g_blocks[0]] + [send(block, perm) for block, perm in zip(g_blocks[1:], NEAR)]
    hidden_near, acts_near = hidden_call([x_own, x_one_near, x_two_near, x_three_near], wg, wu)
    hidden_far, acts_far = hidden_call([x_own_far, x_one_far, x_two_far, x_three_far], wg, wu)
    hidden_other = send(hidden_far, INNER)

    g_near, hidden_other, hidden_near = tie((g_near, hidden_other, hidden_near))
    dh_near, dh_far = d_hidden_call(g_near, wd)
    dh_other = send(dh_far, INNER)
    terms = grad_call(acts_far, dh_other, wg, wu)

    arrived = [send(term, INNER) for term in terms[1:]]
    near_terms = grad_call(acts_near, dh_near, wg, wu)
    near_terms, hidden_other = tie((near_terms, hidden_other))
    out_sent = out_call(hidden_near, hidden_other, wd)
    out_rows = plane_exchange(out_sent)
    near_terms, own_term, arrived, _ = tie((near_terms, terms[0], arrived, out_sent))
    own_arrived = send(own_term, INNER)
    totals = [(a.astype(F32) + b.astype(F32)).astype(BF) for a, b in zip(near_terms[1:], arrived)]
    backs = [send(total, perm) for total, perm in zip(totals, BACK)]
    (out_own, out_one, out_two, out_three), backs = tie((shuffle(out_rows), backs))
    grad_rows = plane_exchange(unshuffle([near_terms[0]] + backs + [own_arrived]))
    out_two = send(out_two, BACK[1])
    out_one, out_three, out_two = tie((out_one, out_three, out_two))
    out_back = [out_own, send(out_one, BACK[0]), out_two, send(out_three, BACK[2])]

    grad_back = [grad_rows.reshape(TEAM * BLK, d // QUARTERS)]
    moe_out = combine(where, ids_row, ids_col, level_col, out_back, True, d)
    grad_x = combine(where, ids_row, ids_col, level_col, grad_back, False, d)
    attn_out, grad_q, grad_k, grad_v = attended
    return (moe_out, grad_x, attn_out, grad_q, grad_k, grad_v)


def solution(mesh):
    in_specs = (
        P(("dp", "tensor"), None),
        P(("dp", "tensor"), None),
        P(("dp", "tensor"), None),
        P(("dp", "tensor"), None),
        P("dp", None, "tensor"),
        P("dp", None, "tensor"),
        P("dp", "tensor", None),
        P("dp", "tensor"),
        P("dp", "tensor"),
        P("dp", "tensor"),
        P("dp", "tensor"),
    )
    out_specs = (
        P(("dp", "tensor"), None),
        P(("dp", "tensor"), None),
        P("dp", "tensor"),
        P("dp", "tensor"),
        P("dp", "tensor"),
        P("dp", "tensor"),
    )
    return jax.shard_map(
        on_device, mesh=mesh, in_specs=in_specs, out_specs=out_specs, check_vma=False
    )
```

```python
import functools

import jax
import jax.numpy as jnp
from jax import lax
from jax.experimental import pallas as pl
from jax.experimental.pallas import tpu as pltpu
from jax.sharding import PartitionSpec as P

HD = 128
AXES = ("dp", "tensor")
SLOTS = 3
QUARTERS = 4
TEAM = 16
BLK = TEAM * SLOTS
VMEM_LIMIT = 24 * 1024 * 1024
BF = jnp.bfloat16
F32 = jnp.float32
NT = (((1,), (1,)), ((), ()))
TN = (((0,), (0,)), ((), ()))


def linear(x, y, z, core):
    return ((z // 2) * 16 + y * 4 + x) * 4 + (z % 2) * 2 + core


def moves(target):
    pairs = []
    for x in range(4):
        for y in range(4):
            for z in range(8):
                for core in range(2):
                    z_to, core_to = target(z, core)
                    pairs.append((linear(x, y, z, core), linear(x, y, z_to % 8, core_to)))
    return pairs


INNER = moves(lambda z, c: (z ^ 1, c))
CORES = moves(lambda z, c: (z, 1 - c))
NEAR = [
    moves(lambda z, c: (z - 2 if z % 2 else z + 2, c)),
    moves(lambda z, c: (z + 3 if z % 2 else z - 3, c)),
    moves(lambda z, c: (z + 1 if z % 2 else z - 1, c)),
]
BACK = [[(b, a) for a, b in perm] for perm in NEAR]
PLANES = [
    [linear(x, y, z, c) for y in range(4) for x in range(4)] for z in range(8) for c in range(2)
]


def send(value, perm):
    return lax.ppermute(value, AXES, perm)


def plane_exchange(value):
    return lax.all_to_all(value, AXES, 0, 0, axis_index_groups=PLANES, tiled=True)


def params(**more):
    return pltpu.CompilerParams(vmem_limit_bytes=VMEM_LIMIT, **more)


WHOLE = pl.BlockSpec(memory_space=pltpu.VMEM)


def cost(flops, nbytes):
    return pl.CostEstimate(flops=flops, bytes_accessed=nbytes, transcendentals=0)


def turn_of(ids, where):
    pair, odd = where[0], where[1]
    turn = ((ids >> 4) - pair) & 3
    return jnp.where(odd == 1, (4 - turn) & 3, turn)


def divide(value, by):
    return (value * ((1 << 20) // by + 1)) >> 20


def by_source_of(row):
    turn = divide(row, 192)
    rest = row - turn * 192
    quarter = divide(rest, BLK)
    rest = rest - quarter * BLK
    source = divide(rest, SLOTS)
    return source * BLK + quarter * (4 * SLOTS) + turn * SLOTS + rest - source * SLOTS


def by_turn_of(row):
    source = divide(row, BLK)
    rest = row - source * BLK
    quarter = divide(rest, 4 * SLOTS)
    rest = rest - quarter * (4 * SLOTS)
    turn = divide(rest, SLOTS)
    return turn * 192 + quarter * BLK + source * SLOTS + rest - turn * SLOTS


def one_hot(target, rows):
    row = lax.broadcasted_iota(jnp.int32, (rows, 1), 0)
    column = lax.broadcasted_iota(jnp.int32, (rows, rows), 1)
    return jnp.where(column == target(row), 1.0, 0.0).astype(BF)


def from_pair_order(part, block):
    width = part.shape[1]
    for q in range(QUARTERS):
        block[:, q * width : (q + 1) * width] = part[q * BLK : (q + 1) * BLK]


def to_source_order(blocks, stack, out_ref):
    width = stack.shape[1]
    for turn, block in enumerate(blocks):
        for q in range(QUARTERS):
            first = (turn * QUARTERS + q) * BLK
            stack[first : first + BLK, :] = block(slice(q * width, (q + 1) * width))
    order = one_hot(by_turn_of, stack.shape[0])
    out_ref[...] = jnp.dot(order, stack[...], preferred_element_type=F32).astype(BF)


def travel_type(d):
    return jax.ShapeDtypeStruct((TEAM * BLK, d // QUARTERS), BF)


def block_types(d):
    return [jax.ShapeDtypeStruct((BLK, d), BF)] * 4


def stack_scratch(d):
    return pltpu.VMEM((TEAM * BLK, d // QUARTERS), BF)


def rows_scratch(d):
    return pltpu.VMEM((4 * BLK, d), BF)


def parted(rows):
    return rows.reshape(TEAM, BLK, rows.shape[1])


def as_column(row):
    count = row.shape[1]
    shape = (count, count)
    here = lax.broadcasted_iota(jnp.int32, shape, 0) == lax.broadcasted_iota(jnp.int32, shape, 1)
    return jnp.sum(jnp.where(here, row, 0), axis=1, keepdims=True)


def ranks(ids_row, ids_col, axis):
    tokens = ids_row.shape[1]
    shape = (tokens, tokens)
    earlier = lax.broadcasted_iota(jnp.int32, shape, axis) < lax.broadcasted_iota(
        jnp.int32, shape, 1 - axis
    )
    same = jnp.where(earlier & (ids_col == ids_row), 1, 0)
    return jnp.sum(same, axis=axis, keepdims=True)


def gates(level, shape, scaled):
    if scaled:
        return jnp.broadcast_to(level.astype(F32) * 0.125, shape)
    return jnp.full(shape, 1.0, F32)


def dispatch_kernel(where, ids_row, level_row, x_ref, out_ref, hot, quarters, *, scaled):
    tokens = ids_row.shape[1]
    ids = ids_row[...]
    rank = ranks(ids, as_column(ids), 0)
    base = (ids & 15) * BLK + turn_of(ids, where) * SLOTS + rank
    rows, width = hot.shape[0], quarters.shape[1]
    row = lax.broadcasted_iota(jnp.int32, (rows, tokens), 0)
    value = gates(level_row[...], (rows, tokens), scaled)
    for q in range(QUARTERS):
        part = slice(q * tokens, (q + 1) * tokens)
        hot[:, part] = jnp.where(row == base + q * (4 * SLOTS), value, 0.0).astype(BF)
        quarters[part, :] = x_ref[:, q * width : (q + 1) * width]
    out_ref[...] = jnp.dot(hot[...], quarters[...], preferred_element_type=F32).astype(BF)


def dispatch(where, ids_row, level_row, x, scaled):
    tokens, d = x.shape
    rows = TEAM * BLK
    return pl.pallas_call(
        functools.partial(dispatch_kernel, scaled=scaled),
        out_shape=travel_type(d),
        in_specs=[pl.BlockSpec(memory_space=pltpu.SMEM)] + [WHOLE] * 3,
        out_specs=WHOLE,
        scratch_shapes=[
            pltpu.VMEM((rows, QUARTERS * tokens), BF),
            pltpu.VMEM((QUARTERS * tokens, d // QUARTERS), BF),
        ],
        compiler_params=params(),
        cost_estimate=cost(2 * rows * tokens * d, 3 * 1024 * 1024),
        name="dispatch",
    )(where, ids_row, level_row, x)


def combine_plane_kernel(where, ids_row, level_row, back, out_ref, *, scaled):
    ids = as_column(ids_row[...])
    base = (ids & 15) * BLK + turn_of(ids, where) * SLOTS + ranks(ids_row[...], ids, 1)
    rows, width = back.shape
    shape = (ids_row.shape[1], rows)
    row = lax.broadcasted_iota(jnp.int32, shape, 1)
    value = gates(as_column(level_row[...]), shape, scaled)
    for q in range(QUARTERS):
        hot = jnp.where(row == base + q * (4 * SLOTS), value, 0.0).astype(BF)
        part = jnp.dot(hot, back[...], preferred_element_type=F32)
        out_ref[:, q * width : (q + 1) * width] = part.astype(BF)


def combine_pairs_kernel(where, ids_row, level_row, *refs, scaled):
    backs, out_ref, rows = refs[:4], refs[4], refs[5]
    ids = as_column(ids_row[...])
    base = turn_of(ids, where) * BLK + (ids & 15) * SLOTS + ranks(ids_row[...], ids, 1)
    shape = (ids_row.shape[1], 4 * BLK)
    gather_rows(backs, rows)
    row = lax.broadcasted_iota(jnp.int32, shape, 1)
    value = gates(as_column(level_row[...]), shape, scaled)
    hot = jnp.where(row == base, value, 0.0).astype(BF)
    out_ref[...] = jnp.dot(hot, rows[...], preferred_element_type=F32).astype(BF)


def combine(where, ids_row, level_row, backs, scaled, d):
    tokens = ids_row.shape[1]
    by_pair = len(backs) == 4
    return pl.pallas_call(
        functools.partial(combine_pairs_kernel if by_pair else combine_plane_kernel, scaled=scaled),
        out_shape=jax.ShapeDtypeStruct((tokens, d), BF),
        in_specs=[pl.BlockSpec(memory_space=pltpu.SMEM)] + [WHOLE] * (2 + len(backs)),
        out_specs=WHOLE,
        scratch_shapes=[rows_scratch(d)] if by_pair else [],
        compiler_params=params(),
        cost_estimate=cost(2 * TEAM * BLK * tokens * d, 3 * 1024 * 1024),
        name="combine",
    )(where, ids_row, level_row, *backs)


def shuffle_kernel(rows_ref, *refs):
    outs, order = refs[:4], refs[4]
    order[...] = one_hot(by_source_of, order.shape[0])
    size = QUARTERS * BLK
    for turn, out in enumerate(outs):
        part = jnp.dot(
            order[turn * size : (turn + 1) * size, :], rows_ref[...], preferred_element_type=F32
        )
        from_pair_order(part.astype(BF), out)


def shuffle(rows):
    rows = rows.reshape(TEAM * BLK, rows.shape[-1])
    count, width = rows.shape
    return pl.pallas_call(
        shuffle_kernel,
        out_shape=block_types(width * QUARTERS),
        in_specs=[WHOLE],
        out_specs=[WHOLE] * 4,
        scratch_shapes=[pltpu.VMEM((count, count), BF)],
        compiler_params=params(),
        cost_estimate=cost(2 * count * count * width, 4 * count * width),
        name="shuffle",
    )(rows)


def unshuffle_kernel(*refs, summed):
    blocks, (out_ref, stack) = refs[:-2], refs[-2:]

    def own(cols):
        if summed:
            return (blocks[0][:, cols].astype(F32) + blocks[4][:, cols].astype(F32)).astype(BF)
        return blocks[0][:, cols]

    others = [lambda cols, block=block: block[:, cols] for block in blocks[1:4]]
    to_source_order([own] + others, stack, out_ref)


def unshuffle(blocks):
    d = blocks[0].shape[1]
    rows = TEAM * BLK
    out = pl.pallas_call(
        functools.partial(unshuffle_kernel, summed=len(blocks) == 5),
        out_shape=travel_type(d),
        in_specs=[WHOLE] * len(blocks),
        out_specs=WHOLE,
        scratch_shapes=[stack_scratch(d)],
        compiler_params=params(),
        cost_estimate=cost(2 * rows * rows * d // QUARTERS, 3 * 1024 * 1024),
        name="unshuffle",
    )(*blocks)
    return parted(out)


def gather_rows(blocks, rows):
    for i, block in enumerate(blocks):
        rows[i * BLK : (i + 1) * BLK, :] = block[...]


def hidden_kernel(b0, b1, b2, b3, wg0, wg1, wu0, wu1, hidden, acts, rows):
    gather_rows((b0, b1, b2, b3), rows)
    ff = wg0.shape[1]
    for i, w in enumerate((wg0, wg1, wu0, wu1)):
        acts[:, i * ff : (i + 1) * ff] = jnp.dot(rows[...], w[...], preferred_element_type=F32)
    gate = acts[:, : 2 * ff]
    hidden[...] = (gate * jax.nn.sigmoid(gate) * acts[:, 2 * ff :]).astype(BF)


def hidden_call(blocks, wg, wu):
    d, ff = wg[0].shape
    count = 4 * BLK
    return pl.pallas_call(
        hidden_kernel,
        out_shape=[
            jax.ShapeDtypeStruct((count, 2 * ff), BF),
            jax.ShapeDtypeStruct((count, 4 * ff), F32),
        ],
        in_specs=[WHOLE] * 8,
        out_specs=[WHOLE] * 2,
        scratch_shapes=[rows_scratch(d)],
        compiler_params=params(),
        cost_estimate=cost(8 * count * d * ff, 12 * 1024 * 1024),
        name="hidden",
    )(*blocks, *wg, *wu)


def hidden_parts(weights):
    place = [0, 0]
    half = sum(w.shape[0] for w in weights) // 2
    for w in weights:
        plane = 0 if place[0] < half else 1
        yield plane, place[plane], w.shape[0]
        place[plane] += w.shape[0]


def d_hidden_kernel(b0, b1, b2, b3, *refs):
    weights, (mine, other, rows) = refs[:-3], refs[-3:]
    gather_rows((b0, b1, b2, b3), rows)
    for w, (plane, first, size) in zip(weights, hidden_parts(weights)):
        part = lax.dot_general(rows[...], w[...], NT, preferred_element_type=F32)
        out = (mine, other)[plane]
        out[:, first : first + size] = part.astype(out.dtype)


def d_hidden_call(blocks, wd):
    d = wd[0].shape[1]
    units = sum(w.shape[0] for w in wd)
    return pl.pallas_call(
        d_hidden_kernel,
        out_shape=[
            jax.ShapeDtypeStruct((4 * BLK, units // 2), F32),
            jax.ShapeDtypeStruct((4 * BLK, units // 2), BF),
        ],
        in_specs=[WHOLE] * (4 + len(wd)),
        out_specs=[WHOLE] * 2,
        scratch_shapes=[rows_scratch(d)],
        compiler_params=params(),
        cost_estimate=cost(8 * BLK * units * d, 12 * 1024 * 1024),
        name="d_hidden",
    )(*blocks, *wd)


def out_kernel(near, other, *refs):
    weights, (out_ref, rows, stack) = refs[:-3], refs[-3:]
    width = rows.shape[1] // 4
    for q in range(4):
        cols = slice(q * width, (q + 1) * width)
        total = None
        for w, (plane, first, size) in zip(weights, hidden_parts(weights)):
            part = jnp.dot(
                (near, other)[plane][:, first : first + size],
                w[:, cols],
                preferred_element_type=F32,
            )
            total = part if total is None else total + part
        rows[:, cols] = total.astype(BF)
    blocks = [lambda cols, i=i: rows[i * BLK : (i + 1) * BLK, cols] for i in range(4)]
    to_source_order(blocks, stack, out_ref)


def out_call(near, other, wd):
    d = wd[0].shape[1]
    rows, units = near.shape
    out = pl.pallas_call(
        out_kernel,
        out_shape=travel_type(d),
        in_specs=[WHOLE] * (2 + len(wd)),
        out_specs=WHOLE,
        scratch_shapes=[rows_scratch(d), stack_scratch(d)],
        compiler_params=params(),
        cost_estimate=cost(4 * rows * d * units, 12 * 1024 * 1024),
        name="expert_out",
    )(near, other, *wd)
    return parted(out)


def grad_kernel(acts, dh, wg0, wg1, wu0, wu1, *refs):
    outs, dacts = refs[:4], refs[4]
    ff = wg0.shape[1]
    gate = acts[:, : 2 * ff]
    up = acts[:, 2 * ff :]
    sigma = jax.nn.sigmoid(gate)
    d_hidden = dh[...].astype(F32)
    d_gate = d_hidden * up * sigma * (1.0 + gate * (1.0 - sigma))
    dacts[:, : 2 * ff] = d_gate.astype(BF)
    dacts[:, 2 * ff :] = (d_hidden * (gate * sigma)).astype(BF)
    width = outs[0].shape[1] // 4
    for q in range(4):
        cols = slice(q * width, (q + 1) * width)
        total = None
        for i, w in enumerate((wg0, wg1, wu0, wu1)):
            part = lax.dot_general(
                dacts[:, i * ff : (i + 1) * ff], w[cols, :], NT, preferred_element_type=F32
            )
            total = part if total is None else total + part
        for i, out in enumerate(outs):
            out[:, cols] = total[i * BLK : (i + 1) * BLK].astype(BF)


def grad_call(acts, dh, wg, wu):
    d, ff = wg[0].shape
    rows = dh.shape[0]
    return pl.pallas_call(
        grad_kernel,
        out_shape=block_types(d),
        in_specs=[WHOLE] * 6,
        out_specs=[WHOLE] * 4,
        scratch_shapes=[pltpu.VMEM((rows, 4 * ff), BF)],
        compiler_params=params(),
        cost_estimate=cost(8 * rows * d * ff, 12 * 1024 * 1024),
        name="expert_grad",
    )(acts, dh, *wg, *wu)


HEADS_STEP = 4


def attention_kernel(q_ref, k_ref, v_ref, do_ref, o_ref, dq_ref, dk_ref, dv_ref, dk_acc, dv_acc):
    step = pl.program_id(0)
    length = k_ref.shape[0]
    scale = HD ** (-0.5)
    k = k_ref[...]
    v = v_ref[...]
    causal = lax.broadcasted_iota(jnp.int32, (length, length), 0) >= lax.broadcasted_iota(
        jnp.int32, (length, length), 1
    )
    dk = None
    dv = None
    for h in range(HEADS_STEP):
        cols = slice(h * HD, (h + 1) * HD)
        q = q_ref[:, cols]
        do = do_ref[:, cols]
        scores = lax.dot_general(q, k, NT, preferred_element_type=F32) * scale
        scores = jnp.where(causal, scores, -1e30)
        raised = jnp.exp(scores - jnp.max(scores, axis=1, keepdims=True))
        probs = raised / jnp.sum(raised, axis=1, keepdims=True)
        rounded = probs.astype(BF)
        o_ref[:, cols] = jnp.dot(rounded, v, preferred_element_type=F32).astype(BF)
        d_probs = lax.dot_general(do, v, NT, preferred_element_type=F32).astype(BF).astype(F32)
        inner = jnp.sum(d_probs * probs, axis=1, keepdims=True)
        d_scores = (probs * (d_probs - inner) * scale).astype(BF)
        dq_ref[:, cols] = jnp.dot(d_scores, k, preferred_element_type=F32).astype(BF)
        dk_part = lax.dot_general(d_scores, q, TN, preferred_element_type=F32)
        dv_part = lax.dot_general(rounded, do, TN, preferred_element_type=F32)
        dk = dk_part if dk is None else dk + dk_part
        dv = dv_part if dv is None else dv + dv_part

    @pl.when(step == 0)
    def _():
        dk_acc[...] = dk
        dv_acc[...] = dv

    @pl.when(step > 0)
    def _():
        dk_acc[...] = dk_acc[...] + dk
        dv_acc[...] = dv_acc[...] + dv

    @pl.when(step == pl.num_programs(0) - 1)
    def _():
        dk_ref[...] = dk_acc[...].astype(BF)
        dv_ref[...] = dv_acc[...].astype(BF)


def attention(queries, keys, values, cotangent):
    length, wide = queries.shape
    head_spec = pl.BlockSpec((length, HEADS_STEP * HD), lambda s: (0, s))
    key_spec = pl.BlockSpec((length, HD), lambda s: (0, 0))
    heads = wide // HD
    return pl.pallas_call(
        attention_kernel,
        out_shape=[
            jax.ShapeDtypeStruct(queries.shape, BF),
            jax.ShapeDtypeStruct(queries.shape, BF),
            jax.ShapeDtypeStruct(keys.shape, BF),
            jax.ShapeDtypeStruct(values.shape, BF),
        ],
        grid=(heads // HEADS_STEP,),
        in_specs=[head_spec, key_spec, key_spec, head_spec],
        out_specs=[head_spec, head_spec, key_spec, key_spec],
        scratch_shapes=[pltpu.VMEM((length, HD), F32)] * 2,
        compiler_params=params(dimension_semantics=("arbitrary",)),
        cost_estimate=cost(14 * heads * length * length * HD, 10 * 1024 * 1024),
        name="attention",
    )(queries, keys, values, cotangent)


def on_device(
    layer_input,
    out_grad,
    expert_ids,
    gate_level,
    w_gate,
    w_up,
    w_down,
    attn_queries,
    attn_keys,
    attn_values,
    attn_grad,
):
    tokens, d = layer_input.shape
    where = jnp.stack([lax.axis_index("dp") // 16, lax.axis_index("tensor") // 2]).astype(jnp.int32)
    ids_row = expert_ids.reshape(1, tokens)
    level_row = gate_level.reshape(1, tokens)
    tie = lax.optimization_barrier

    gate, up, down = w_gate[0], w_up[0], w_down[0]
    down_other = send(down, INNER)
    mates = [send(w, CORES) for w in (gate, up, down)]

    x_sent = dispatch(where, ids_row, level_row, layer_input, False)
    g_sent = dispatch(where, ids_row, level_row, out_grad, True)
    x_rows = plane_exchange(parted(x_sent))
    attended = attention(attn_queries, attn_keys, attn_values, attn_grad)
    x_rows, g_sent, attended, mates = tie((x_rows, g_sent, attended, mates))
    g_rows = plane_exchange(parted(g_sent))
    x_own, x_one, x_two, x_three = shuffle(x_rows)
    x_two_near = send(x_two, NEAR[1])
    x_own_far = send(x_own, INNER)
    x_one, x_three, x_two_near, x_own_far, down_other = tie(
        (x_one, x_three, x_two_near, x_own_far, down_other)
    )
    x_one_near = send(x_one, NEAR[0])
    x_three_near = send(x_three, NEAR[2])
    x_two_far = send(x_two_near, INNER)
    wg, wu = (gate, mates[0]), (up, mates[1])
    g_blocks, x_one_near, x_three_near = tie((shuffle(g_rows), x_one_near, x_three_near))
    down_other_mate = send(down_other, CORES)
    wd = (down, mates[2], down_other, down_other_mate)
    x_one_far = send(x_one_near, INNER)
    x_three_far = send(x_three_near, INNER)
    g_near = [g_blocks[0]] + [send(block, perm) for block, perm in zip(g_blocks[1:], NEAR)]
    hidden_near, acts_near = hidden_call([x_own, x_one_near, x_two_near, x_three_near], wg, wu)
    hidden_far, acts_far = hidden_call([x_own_far, x_one_far, x_two_far, x_three_far], wg, wu)
    hidden_other = send(hidden_far, INNER)

    g_near, hidden_other, hidden_near = tie((g_near, hidden_other, hidden_near))
    dh_near, dh_far = d_hidden_call(g_near, wd)
    dh_other = send(dh_far, INNER)
    terms = grad_call(acts_far, dh_other, wg, wu)

    arrived = [send(term, INNER) for term in terms[1:]]
    near_terms = grad_call(acts_near, dh_near, wg, wu)
    near_terms, hidden_other = tie((near_terms, hidden_other))
    out_sent = out_call(hidden_near, hidden_other, wd)
    out_rows = plane_exchange(out_sent)
    near_terms, own_term, arrived, _ = tie((near_terms, terms[0], arrived, out_sent))
    own_arrived = send(own_term, INNER)
    totals = [(a.astype(F32) + b.astype(F32)).astype(BF) for a, b in zip(near_terms[1:], arrived)]
    backs = [send(total, perm) for total, perm in zip(totals, BACK)]
    (out_own, out_one, out_two, out_three), backs = tie((shuffle(out_rows), backs))
    grad_rows = plane_exchange(unshuffle([near_terms[0]] + backs + [own_arrived]))
    out_back = [out_own] + [send(b, perm) for b, perm in zip((out_one, out_two, out_three), BACK)]

    grad_back = [grad_rows.reshape(TEAM * BLK, d // QUARTERS)]
    moe_out = combine(where, ids_row, level_row, out_back, True, d)
    grad_x = combine(where, ids_row, level_row, grad_back, False, d)
    attn_out, grad_q, grad_k, grad_v = attended
    return (moe_out, grad_x, attn_out, grad_q, grad_k, grad_v)


def solution(mesh):
    in_specs = (
        P(("dp", "tensor"), None),
        P(("dp", "tensor"), None),
        P(("dp", "tensor"), None),
        P(("dp", "tensor"), None),
        P("dp", None, "tensor"),
        P("dp", None, "tensor"),
        P("dp", "tensor", None),
        P("dp", "tensor"),
        P("dp", "tensor"),
        P("dp", "tensor"),
        P("dp", "tensor"),
    )
    out_specs = (
        P(("dp", "tensor"), None),
        P(("dp", "tensor"), None),
        P("dp", "tensor"),
        P("dp", "tensor"),
        P("dp", "tensor"),
        P("dp", "tensor"),
    )
    return jax.shard_map(
        on_device, mesh=mesh, in_specs=in_specs, out_specs=out_specs, check_vma=False
    )
```

```python
import functools

import jax
import jax.numpy as jnp
from jax import lax
from jax.experimental import pallas as pl
from jax.experimental.pallas import tpu as pltpu
from jax.sharding import PartitionSpec as P

HD = 128
AXES = ("dp", "tensor")
SLOTS = 3
QUARTERS = 4
TEAM = 16
BLK = TEAM * SLOTS
VMEM_LIMIT = 24 * 1024 * 1024
BF = jnp.bfloat16
F32 = jnp.float32
NT = (((1,), (1,)), ((), ()))
TN = (((0,), (0,)), ((), ()))


def linear(x, y, z, core):
    return ((z // 2) * 16 + y * 4 + x) * 4 + (z % 2) * 2 + core


def moves(target):
    pairs = []
    for x in range(4):
        for y in range(4):
            for z in range(8):
                for core in range(2):
                    z_to, core_to = target(z, core)
                    pairs.append((linear(x, y, z, core), linear(x, y, z_to % 8, core_to)))
    return pairs


INNER = moves(lambda z, c: (z ^ 1, c))
CORES = moves(lambda z, c: (z, 1 - c))
NEAR = [
    moves(lambda z, c: (z - 2 if z % 2 else z + 2, c)),
    moves(lambda z, c: (z + 3 if z % 2 else z - 3, c)),
    moves(lambda z, c: (z + 1 if z % 2 else z - 1, c)),
]
BACK = [[(b, a) for a, b in perm] for perm in NEAR]
PLANES = [
    [linear(x, y, z, c) for y in range(4) for x in range(4)] for z in range(8) for c in range(2)
]


def send(value, perm):
    return lax.ppermute(value, AXES, perm)


def plane_exchange(value):
    return lax.all_to_all(value, AXES, 0, 0, axis_index_groups=PLANES, tiled=True)


def params(**more):
    return pltpu.CompilerParams(vmem_limit_bytes=VMEM_LIMIT, **more)


WHOLE = pl.BlockSpec(memory_space=pltpu.VMEM)


def cost(flops, nbytes):
    return pl.CostEstimate(flops=flops, bytes_accessed=nbytes, transcendentals=0)


def turn_of(ids, where):
    pair, odd = where[0], where[1]
    turn = ((ids >> 4) - pair) & 3
    return jnp.where(odd == 1, (4 - turn) & 3, turn)


def divide(value, by):
    return (value * ((1 << 20) // by + 1)) >> 20


def by_source_of(row):
    turn = divide(row, 192)
    rest = row - turn * 192
    quarter = divide(rest, BLK)
    rest = rest - quarter * BLK
    source = divide(rest, SLOTS)
    return source * BLK + quarter * (4 * SLOTS) + turn * SLOTS + rest - source * SLOTS


def by_turn_of(row):
    source = divide(row, BLK)
    rest = row - source * BLK
    quarter = divide(rest, 4 * SLOTS)
    rest = rest - quarter * (4 * SLOTS)
    turn = divide(rest, SLOTS)
    return turn * 192 + quarter * BLK + source * SLOTS + rest - turn * SLOTS


def one_hot(target, rows):
    row = lax.broadcasted_iota(jnp.int32, (rows, 1), 0)
    column = lax.broadcasted_iota(jnp.int32, (rows, rows), 1)
    return jnp.where(column == target(row), 1.0, 0.0).astype(BF)


def from_pair_order(part, block):
    width = part.shape[1]
    for q in range(QUARTERS):
        block[:, q * width : (q + 1) * width] = part[q * BLK : (q + 1) * BLK]


def to_source_order(blocks, stack, out_ref):
    width = stack.shape[1]
    for turn, block in enumerate(blocks):
        for q in range(QUARTERS):
            first = (turn * QUARTERS + q) * BLK
            stack[first : first + BLK, :] = block(slice(q * width, (q + 1) * width))
    order = one_hot(by_turn_of, stack.shape[0])
    out_ref[...] = jnp.dot(order, stack[...], preferred_element_type=F32).astype(BF)


def travel_type(d):
    return jax.ShapeDtypeStruct((TEAM * BLK, d // QUARTERS), BF)


def block_types(d):
    return [jax.ShapeDtypeStruct((BLK, d), BF)] * 4


def stack_scratch(d):
    return pltpu.VMEM((TEAM * BLK, d // QUARTERS), BF)


def rows_scratch(d):
    return pltpu.VMEM((4 * BLK, d), BF)


def parted(rows):
    return rows.reshape(TEAM, BLK, rows.shape[1])


def as_column(row):
    count = row.shape[1]
    shape = (count, count)
    here = lax.broadcasted_iota(jnp.int32, shape, 0) == lax.broadcasted_iota(jnp.int32, shape, 1)
    return jnp.sum(jnp.where(here, row, 0), axis=1, keepdims=True)


def ranks(ids_row, ids_col, axis):
    tokens = ids_row.shape[1]
    shape = (tokens, tokens)
    earlier = lax.broadcasted_iota(jnp.int32, shape, axis) < lax.broadcasted_iota(
        jnp.int32, shape, 1 - axis
    )
    same = jnp.where(earlier & (ids_col == ids_row), 1, 0)
    return jnp.sum(same, axis=axis, keepdims=True)


def gates(level, shape, scaled):
    if scaled:
        return jnp.broadcast_to(level.astype(F32) * 0.125, shape)
    return jnp.full(shape, 1.0, F32)


def dispatch_kernel(where, ids_row, level_row, x_ref, out_ref, hot, quarters, *, scaled):
    tokens = ids_row.shape[1]
    ids = ids_row[...]
    rank = ranks(ids, as_column(ids), 0)
    base = (ids & 15) * BLK + turn_of(ids, where) * SLOTS + rank
    rows, width = hot.shape[0], quarters.shape[1]
    row = lax.broadcasted_iota(jnp.int32, (rows, tokens), 0)
    value = gates(level_row[...], (rows, tokens), scaled)
    for q in range(QUARTERS):
        part = slice(q * tokens, (q + 1) * tokens)
        hot[:, part] = jnp.where(row == base + q * (4 * SLOTS), value, 0.0).astype(BF)
        quarters[part, :] = x_ref[:, q * width : (q + 1) * width]
    out_ref[...] = jnp.dot(hot[...], quarters[...], preferred_element_type=F32).astype(BF)


def dispatch(where, ids_row, level_row, x, scaled):
    tokens, d = x.shape
    rows = TEAM * BLK
    return pl.pallas_call(
        functools.partial(dispatch_kernel, scaled=scaled),
        out_shape=travel_type(d),
        in_specs=[pl.BlockSpec(memory_space=pltpu.SMEM)] + [WHOLE] * 3,
        out_specs=WHOLE,
        scratch_shapes=[
            pltpu.VMEM((rows, QUARTERS * tokens), BF),
            pltpu.VMEM((QUARTERS * tokens, d // QUARTERS), BF),
        ],
        compiler_params=params(),
        cost_estimate=cost(2 * rows * tokens * d, 3 * 1024 * 1024),
        name="dispatch",
    )(where, ids_row, level_row, x)


def combine_plane_kernel(where, ids_row, level_row, back, out_ref, *, scaled):
    ids = as_column(ids_row[...])
    base = (ids & 15) * BLK + turn_of(ids, where) * SLOTS + ranks(ids_row[...], ids, 1)
    rows, width = back.shape
    shape = (ids_row.shape[1], rows)
    row = lax.broadcasted_iota(jnp.int32, shape, 1)
    value = gates(as_column(level_row[...]), shape, scaled)
    for q in range(QUARTERS):
        hot = jnp.where(row == base + q * (4 * SLOTS), value, 0.0).astype(BF)
        part = jnp.dot(hot, back[...], preferred_element_type=F32)
        out_ref[:, q * width : (q + 1) * width] = part.astype(BF)


def combine_pairs_kernel(where, ids_row, level_row, *refs, scaled):
    backs, out_ref, rows = refs[:4], refs[4], refs[5]
    ids = as_column(ids_row[...])
    base = turn_of(ids, where) * BLK + (ids & 15) * SLOTS + ranks(ids_row[...], ids, 1)
    shape = (ids_row.shape[1], 4 * BLK)
    gather_rows(backs, rows)
    row = lax.broadcasted_iota(jnp.int32, shape, 1)
    value = gates(as_column(level_row[...]), shape, scaled)
    hot = jnp.where(row == base, value, 0.0).astype(BF)
    out_ref[...] = jnp.dot(hot, rows[...], preferred_element_type=F32).astype(BF)


def combine(where, ids_row, level_row, backs, scaled, d):
    tokens = ids_row.shape[1]
    by_pair = len(backs) == 4
    return pl.pallas_call(
        functools.partial(combine_pairs_kernel if by_pair else combine_plane_kernel, scaled=scaled),
        out_shape=jax.ShapeDtypeStruct((tokens, d), BF),
        in_specs=[pl.BlockSpec(memory_space=pltpu.SMEM)] + [WHOLE] * (2 + len(backs)),
        out_specs=WHOLE,
        scratch_shapes=[rows_scratch(d)] if by_pair else [],
        compiler_params=params(),
        cost_estimate=cost((100 if by_pair else 2) * TEAM * BLK * tokens * d, 3 * 1024 * 1024),
        name="combine",
    )(where, ids_row, level_row, *backs)


def shuffle_kernel(rows_ref, *refs):
    outs, order = refs[:4], refs[4]
    order[...] = one_hot(by_source_of, order.shape[0])
    size = QUARTERS * BLK
    for turn, out in enumerate(outs):
        part = jnp.dot(
            order[turn * size : (turn + 1) * size, :], rows_ref[...], preferred_element_type=F32
        )
        from_pair_order(part.astype(BF), out)


def shuffle(rows):
    rows = rows.reshape(TEAM * BLK, rows.shape[-1])
    count, width = rows.shape
    return pl.pallas_call(
        shuffle_kernel,
        out_shape=block_types(width * QUARTERS),
        in_specs=[WHOLE],
        out_specs=[WHOLE] * 4,
        scratch_shapes=[pltpu.VMEM((count, count), BF)],
        compiler_params=params(),
        cost_estimate=cost(2 * count * count * width, 4 * count * width),
        name="shuffle",
    )(rows)


def unshuffle_kernel(*refs, summed):
    blocks, (out_ref, stack) = refs[:-2], refs[-2:]

    def own(cols):
        if summed:
            return (blocks[0][:, cols].astype(F32) + blocks[4][:, cols].astype(F32)).astype(BF)
        return blocks[0][:, cols]

    others = [lambda cols, block=block: block[:, cols] for block in blocks[1:4]]
    to_source_order([own] + others, stack, out_ref)


def unshuffle(blocks):
    d = blocks[0].shape[1]
    rows = TEAM * BLK
    out = pl.pallas_call(
        functools.partial(unshuffle_kernel, summed=len(blocks) == 5),
        out_shape=travel_type(d),
        in_specs=[WHOLE] * len(blocks),
        out_specs=WHOLE,
        scratch_shapes=[stack_scratch(d)],
        compiler_params=params(),
        cost_estimate=cost(2 * rows * rows * d // QUARTERS, 3 * 1024 * 1024),
        name="unshuffle",
    )(*blocks)
    return parted(out)


def gather_rows(blocks, rows):
    for i, block in enumerate(blocks):
        rows[i * BLK : (i + 1) * BLK, :] = block[...]


def hidden_kernel(b0, b1, b2, b3, wg0, wg1, wu0, wu1, hidden, acts, rows):
    gather_rows((b0, b1, b2, b3), rows)
    ff = wg0.shape[1]
    for i, w in enumerate((wg0, wg1, wu0, wu1)):
        acts[:, i * ff : (i + 1) * ff] = jnp.dot(rows[...], w[...], preferred_element_type=F32)
    gate = acts[:, : 2 * ff]
    hidden[...] = (gate * jax.nn.sigmoid(gate) * acts[:, 2 * ff :]).astype(BF)


def hidden_call(blocks, wg, wu):
    d, ff = wg[0].shape
    count = 4 * BLK
    return pl.pallas_call(
        hidden_kernel,
        out_shape=[
            jax.ShapeDtypeStruct((count, 2 * ff), BF),
            jax.ShapeDtypeStruct((count, 4 * ff), F32),
        ],
        in_specs=[WHOLE] * 8,
        out_specs=[WHOLE] * 2,
        scratch_shapes=[rows_scratch(d)],
        compiler_params=params(),
        cost_estimate=cost(8 * count * d * ff, 12 * 1024 * 1024),
        name="hidden",
    )(*blocks, *wg, *wu)


def hidden_parts(weights):
    place = [0, 0]
    half = sum(w.shape[0] for w in weights) // 2
    for w in weights:
        plane = 0 if place[0] < half else 1
        yield plane, place[plane], w.shape[0]
        place[plane] += w.shape[0]


def d_hidden_kernel(b0, b1, b2, b3, *refs):
    weights, (mine, other, rows) = refs[:-3], refs[-3:]
    gather_rows((b0, b1, b2, b3), rows)
    for w, (plane, first, size) in zip(weights, hidden_parts(weights)):
        part = lax.dot_general(rows[...], w[...], NT, preferred_element_type=F32)
        out = (mine, other)[plane]
        out[:, first : first + size] = part.astype(out.dtype)


def d_hidden_call(blocks, wd):
    d = wd[0].shape[1]
    units = sum(w.shape[0] for w in wd)
    return pl.pallas_call(
        d_hidden_kernel,
        out_shape=[
            jax.ShapeDtypeStruct((4 * BLK, units // 2), F32),
            jax.ShapeDtypeStruct((4 * BLK, units // 2), BF),
        ],
        in_specs=[WHOLE] * (4 + len(wd)),
        out_specs=[WHOLE] * 2,
        scratch_shapes=[rows_scratch(d)],
        compiler_params=params(),
        cost_estimate=cost(8 * BLK * units * d, 12 * 1024 * 1024),
        name="d_hidden",
    )(*blocks, *wd)


def out_kernel(near, other, *refs):
    weights, (out_ref, rows, stack) = refs[:-3], refs[-3:]
    width = rows.shape[1] // 4
    for q in range(4):
        cols = slice(q * width, (q + 1) * width)
        total = None
        for w, (plane, first, size) in zip(weights, hidden_parts(weights)):
            part = jnp.dot(
                (near, other)[plane][:, first : first + size],
                w[:, cols],
                preferred_element_type=F32,
            )
            total = part if total is None else total + part
        rows[:, cols] = total.astype(BF)
    blocks = [lambda cols, i=i: rows[i * BLK : (i + 1) * BLK, cols] for i in range(4)]
    to_source_order(blocks, stack, out_ref)


def out_call(near, other, wd):
    d = wd[0].shape[1]
    rows, units = near.shape
    out = pl.pallas_call(
        out_kernel,
        out_shape=travel_type(d),
        in_specs=[WHOLE] * (2 + len(wd)),
        out_specs=WHOLE,
        scratch_shapes=[rows_scratch(d), stack_scratch(d)],
        compiler_params=params(),
        cost_estimate=cost(4 * rows * d * units, 12 * 1024 * 1024),
        name="expert_out",
    )(near, other, *wd)
    return parted(out)


def grad_kernel(acts, dh, wg0, wg1, wu0, wu1, *refs):
    outs, dacts = refs[:4], refs[4]
    ff = wg0.shape[1]
    gate = acts[:, : 2 * ff]
    up = acts[:, 2 * ff :]
    sigma = jax.nn.sigmoid(gate)
    d_hidden = dh[...].astype(F32)
    d_gate = d_hidden * up * sigma * (1.0 + gate * (1.0 - sigma))
    dacts[:, : 2 * ff] = d_gate.astype(BF)
    dacts[:, 2 * ff :] = (d_hidden * (gate * sigma)).astype(BF)
    width = outs[0].shape[1] // 4
    for q in range(4):
        cols = slice(q * width, (q + 1) * width)
        total = None
        for i, w in enumerate((wg0, wg1, wu0, wu1)):
            part = lax.dot_general(
                dacts[:, i * ff : (i + 1) * ff], w[cols, :], NT, preferred_element_type=F32
            )
            total = part if total is None else total + part
        for i, out in enumerate(outs):
            out[:, cols] = total[i * BLK : (i + 1) * BLK].astype(BF)


def grad_call(acts, dh, wg, wu):
    d, ff = wg[0].shape
    rows = dh.shape[0]
    return pl.pallas_call(
        grad_kernel,
        out_shape=block_types(d),
        in_specs=[WHOLE] * 6,
        out_specs=[WHOLE] * 4,
        scratch_shapes=[pltpu.VMEM((rows, 4 * ff), BF)],
        compiler_params=params(),
        cost_estimate=cost(8 * rows * d * ff, 12 * 1024 * 1024),
        name="expert_grad",
    )(acts, dh, *wg, *wu)


HEADS_STEP = 4


def attention_kernel(q_ref, k_ref, v_ref, do_ref, o_ref, dq_ref, dk_ref, dv_ref, dk_acc, dv_acc):
    step = pl.program_id(0)
    length = k_ref.shape[0]
    scale = HD ** (-0.5)
    k = k_ref[...]
    v = v_ref[...]
    causal = lax.broadcasted_iota(jnp.int32, (length, length), 0) >= lax.broadcasted_iota(
        jnp.int32, (length, length), 1
    )
    dk = None
    dv = None
    for h in range(HEADS_STEP):
        cols = slice(h * HD, (h + 1) * HD)
        q = q_ref[:, cols]
        do = do_ref[:, cols]
        scores = lax.dot_general(q, k, NT, preferred_element_type=F32) * scale
        scores = jnp.where(causal, scores, -1e30)
        raised = jnp.exp(scores - jnp.max(scores, axis=1, keepdims=True))
        probs = raised / jnp.sum(raised, axis=1, keepdims=True)
        rounded = probs.astype(BF)
        o_ref[:, cols] = jnp.dot(rounded, v, preferred_element_type=F32).astype(BF)
        d_probs = lax.dot_general(do, v, NT, preferred_element_type=F32).astype(BF).astype(F32)
        inner = jnp.sum(d_probs * probs, axis=1, keepdims=True)
        d_scores = (probs * (d_probs - inner) * scale).astype(BF)
        dq_ref[:, cols] = jnp.dot(d_scores, k, preferred_element_type=F32).astype(BF)
        dk_part = lax.dot_general(d_scores, q, TN, preferred_element_type=F32)
        dv_part = lax.dot_general(rounded, do, TN, preferred_element_type=F32)
        dk = dk_part if dk is None else dk + dk_part
        dv = dv_part if dv is None else dv + dv_part

    @pl.when(step == 0)
    def _():
        dk_acc[...] = dk
        dv_acc[...] = dv

    @pl.when(step > 0)
    def _():
        dk_acc[...] = dk_acc[...] + dk
        dv_acc[...] = dv_acc[...] + dv

    @pl.when(step == pl.num_programs(0) - 1)
    def _():
        dk_ref[...] = dk_acc[...].astype(BF)
        dv_ref[...] = dv_acc[...].astype(BF)


def attention(queries, keys, values, cotangent):
    length, wide = queries.shape
    head_spec = pl.BlockSpec((length, HEADS_STEP * HD), lambda s: (0, s))
    key_spec = pl.BlockSpec((length, HD), lambda s: (0, 0))
    heads = wide // HD
    return pl.pallas_call(
        attention_kernel,
        out_shape=[
            jax.ShapeDtypeStruct(queries.shape, BF),
            jax.ShapeDtypeStruct(queries.shape, BF),
            jax.ShapeDtypeStruct(keys.shape, BF),
            jax.ShapeDtypeStruct(values.shape, BF),
        ],
        grid=(heads // HEADS_STEP,),
        in_specs=[head_spec, key_spec, key_spec, head_spec],
        out_specs=[head_spec, head_spec, key_spec, key_spec],
        scratch_shapes=[pltpu.VMEM((length, HD), F32)] * 2,
        compiler_params=params(dimension_semantics=("arbitrary",)),
        cost_estimate=cost(14 * heads * length * length * HD, 10 * 1024 * 1024),
        name="attention",
    )(queries, keys, values, cotangent)


def on_device(
    layer_input,
    out_grad,
    expert_ids,
    gate_level,
    w_gate,
    w_up,
    w_down,
    attn_queries,
    attn_keys,
    attn_values,
    attn_grad,
):
    tokens, d = layer_input.shape
    where = jnp.stack([lax.axis_index("dp") // 16, lax.axis_index("tensor") // 2]).astype(jnp.int32)
    ids_row = expert_ids.reshape(1, tokens)
    level_row = gate_level.reshape(1, tokens)
    tie = lax.optimization_barrier

    gate, up, down = w_gate[0], w_up[0], w_down[0]
    down_other = send(down, INNER)
    mates = [send(w, CORES) for w in (gate, up, down)]

    x_sent = dispatch(where, ids_row, level_row, layer_input, False)
    g_sent = dispatch(where, ids_row, level_row, out_grad, True)
    x_rows = plane_exchange(parted(x_sent))
    attended = attention(attn_queries, attn_keys, attn_values, attn_grad)
    x_rows, g_sent, attended, mates = tie((x_rows, g_sent, attended, mates))
    g_rows = plane_exchange(parted(g_sent))
    x_own, x_one, x_two, x_three = shuffle(x_rows)
    x_two_near = send(x_two, NEAR[1])
    x_own_far = send(x_own, INNER)
    x_one, x_three, x_two_near, x_own_far, down_other = tie(
        (x_one, x_three, x_two_near, x_own_far, down_other)
    )
    x_one_near = send(x_one, NEAR[0])
    x_three_near = send(x_three, NEAR[2])
    x_two_far = send(x_two_near, INNER)
    wg, wu = (gate, mates[0]), (up, mates[1])
    g_blocks, x_one_near, x_three_near = tie((shuffle(g_rows), x_one_near, x_three_near))
    down_other_mate = send(down_other, CORES)
    wd = (down, mates[2], down_other, down_other_mate)
    x_one_far = send(x_one_near, INNER)
    x_three_far = send(x_three_near, INNER)
    g_near = [g_blocks[0]] + [send(block, perm) for block, perm in zip(g_blocks[1:], NEAR)]
    hidden_near, acts_near = hidden_call([x_own, x_one_near, x_two_near, x_three_near], wg, wu)
    hidden_far, acts_far = hidden_call([x_own_far, x_one_far, x_two_far, x_three_far], wg, wu)
    hidden_other = send(hidden_far, INNER)

    g_near, hidden_other, hidden_near = tie((g_near, hidden_other, hidden_near))
    dh_near, dh_far = d_hidden_call(g_near, wd)
    dh_other = send(dh_far, INNER)
    terms = grad_call(acts_far, dh_other, wg, wu)

    arrived = [send(term, INNER) for term in terms[1:]]
    near_terms = grad_call(acts_near, dh_near, wg, wu)
    near_terms, hidden_other = tie((near_terms, hidden_other))
    out_sent = out_call(hidden_near, hidden_other, wd)
    out_rows = plane_exchange(out_sent)
    near_terms, own_term, arrived, _ = tie((near_terms, terms[0], arrived, out_sent))
    own_arrived = send(own_term, INNER)
    totals = [(a.astype(F32) + b.astype(F32)).astype(BF) for a, b in zip(near_terms[1:], arrived)]
    backs = [send(total, perm) for total, perm in zip(totals, BACK)]
    (out_own, out_one, out_two, out_three), backs = tie((shuffle(out_rows), backs))
    grad_rows = plane_exchange(unshuffle([near_terms[0]] + backs + [own_arrived]))
    out_back = [out_own] + [send(b, perm) for b, perm in zip((out_one, out_two, out_three), BACK)]

    moe_out = combine(where, ids_row, level_row, out_back, True, d)
    grad_rows, moe_out = tie((grad_rows, moe_out))
    grad_back = [grad_rows.reshape(TEAM * BLK, d // QUARTERS)]
    grad_x = combine(where, ids_row, level_row, grad_back, False, d)
    attn_out, grad_q, grad_k, grad_v = attended
    return (moe_out, grad_x, attn_out, grad_q, grad_k, grad_v)


def solution(mesh):
    in_specs = (
        P(("dp", "tensor"), None),
        P(("dp", "tensor"), None),
        P(("dp", "tensor"), None),
        P(("dp", "tensor"), None),
        P("dp", None, "tensor"),
        P("dp", None, "tensor"),
        P("dp", "tensor", None),
        P("dp", "tensor"),
        P("dp", "tensor"),
        P("dp", "tensor"),
        P("dp", "tensor"),
    )
    out_specs = (
        P(("dp", "tensor"), None),
        P(("dp", "tensor"), None),
        P("dp", "tensor"),
        P("dp", "tensor"),
        P("dp", "tensor"),
        P("dp", "tensor"),
    )
    return jax.shard_map(
        on_device, mesh=mesh, in_specs=in_specs, out_specs=out_specs, check_vma=False
    )
```

```python
import functools

import jax
import jax.numpy as jnp
from jax import lax
from jax.experimental import pallas as pl
from jax.experimental.pallas import tpu as pltpu
from jax.sharding import PartitionSpec as P

HD = 128
AXES = ("dp", "tensor")
SLOTS = 3
QUARTERS = 4
TEAM = 16
BLK = TEAM * SLOTS
VMEM_LIMIT = 24 * 1024 * 1024
BF = jnp.bfloat16
F32 = jnp.float32
NT = (((1,), (1,)), ((), ()))
TN = (((0,), (0,)), ((), ()))


def linear(x, y, z, core):
    return ((z // 2) * 16 + y * 4 + x) * 4 + (z % 2) * 2 + core


def moves(target):
    pairs = []
    for x in range(4):
        for y in range(4):
            for z in range(8):
                for core in range(2):
                    z_to, core_to = target(z, core)
                    pairs.append((linear(x, y, z, core), linear(x, y, z_to % 8, core_to)))
    return pairs


INNER = moves(lambda z, c: (z ^ 1, c))
CORES = moves(lambda z, c: (z, 1 - c))
NEAR = [
    moves(lambda z, c: (z - 2 if z % 2 else z + 2, c)),
    moves(lambda z, c: (z + 3 if z % 2 else z - 3, c)),
    moves(lambda z, c: (z + 1 if z % 2 else z - 1, c)),
]
BACK = [[(b, a) for a, b in perm] for perm in NEAR]
PLANES = [
    [linear(x, y, z, c) for y in range(4) for x in range(4)] for z in range(8) for c in range(2)
]


def send(value, perm):
    return lax.ppermute(value, AXES, perm)


def plane_exchange(value):
    return lax.all_to_all(value, AXES, 0, 0, axis_index_groups=PLANES, tiled=True)


def params(**more):
    return pltpu.CompilerParams(vmem_limit_bytes=VMEM_LIMIT, **more)


WHOLE = pl.BlockSpec(memory_space=pltpu.VMEM)


def cost(flops, nbytes):
    return pl.CostEstimate(flops=flops, bytes_accessed=nbytes, transcendentals=0)


def turn_of(ids, where):
    pair, odd = where[0], where[1]
    turn = ((ids >> 4) - pair) & 3
    return jnp.where(odd == 1, (4 - turn) & 3, turn)


def divide(value, by):
    return (value * ((1 << 20) // by + 1)) >> 20


def by_source_of(row):
    turn = divide(row, 192)
    rest = row - turn * 192
    quarter = divide(rest, BLK)
    rest = rest - quarter * BLK
    source = divide(rest, SLOTS)
    return source * BLK + quarter * (4 * SLOTS) + turn * SLOTS + rest - source * SLOTS


def by_turn_of(row):
    source = divide(row, BLK)
    rest = row - source * BLK
    quarter = divide(rest, 4 * SLOTS)
    rest = rest - quarter * (4 * SLOTS)
    turn = divide(rest, SLOTS)
    return turn * 192 + quarter * BLK + source * SLOTS + rest - turn * SLOTS


def one_hot(target, rows):
    row = lax.broadcasted_iota(jnp.int32, (rows, 1), 0)
    column = lax.broadcasted_iota(jnp.int32, (rows, rows), 1)
    return jnp.where(column == target(row), 1.0, 0.0).astype(BF)


def from_pair_order(part, block):
    width = part.shape[1]
    for q in range(QUARTERS):
        block[:, q * width : (q + 1) * width] = part[q * BLK : (q + 1) * BLK]


def to_source_order(blocks, stack, out_ref):
    width = stack.shape[1]
    for turn, block in enumerate(blocks):
        for q in range(QUARTERS):
            first = (turn * QUARTERS + q) * BLK
            stack[first : first + BLK, :] = block(slice(q * width, (q + 1) * width))
    order = one_hot(by_turn_of, stack.shape[0])
    out_ref[...] = jnp.dot(order, stack[...], preferred_element_type=F32).astype(BF)


def travel_type(d):
    return jax.ShapeDtypeStruct((TEAM * BLK, d // QUARTERS), BF)


def block_types(d):
    return [jax.ShapeDtypeStruct((BLK, d), BF)] * 4


def stack_scratch(d):
    return pltpu.VMEM((TEAM * BLK, d // QUARTERS), BF)


def rows_scratch(d):
    return pltpu.VMEM((4 * BLK, d), BF)


def parted(rows):
    return rows.reshape(TEAM, BLK, rows.shape[1])


def as_column(row):
    count = row.shape[1]
    shape = (count, count)
    here = lax.broadcasted_iota(jnp.int32, shape, 0) == lax.broadcasted_iota(jnp.int32, shape, 1)
    return jnp.sum(jnp.where(here, row, 0), axis=1, keepdims=True)


def ranks(ids_row, ids_col, axis):
    tokens = ids_row.shape[1]
    shape = (tokens, tokens)
    earlier = lax.broadcasted_iota(jnp.int32, shape, axis) < lax.broadcasted_iota(
        jnp.int32, shape, 1 - axis
    )
    same = jnp.where(earlier & (ids_col == ids_row), 1, 0)
    return jnp.sum(same, axis=axis, keepdims=True)


def gates(level, shape, scaled):
    if scaled:
        return jnp.broadcast_to(level.astype(F32) * 0.125, shape)
    return jnp.full(shape, 1.0, F32)


def dispatch_kernel(where, ids_row, level_row, x_ref, out_ref, hot, quarters, *, scaled):
    tokens = ids_row.shape[1]
    ids = ids_row[...]
    rank = ranks(ids, as_column(ids), 0)
    base = (ids & 15) * BLK + turn_of(ids, where) * SLOTS + rank
    rows, width = hot.shape[0], quarters.shape[1]
    row = lax.broadcasted_iota(jnp.int32, (rows, tokens), 0)
    value = gates(level_row[...], (rows, tokens), scaled)
    for q in range(QUARTERS):
        part = slice(q * tokens, (q + 1) * tokens)
        hot[:, part] = jnp.where(row == base + q * (4 * SLOTS), value, 0.0).astype(BF)
        quarters[part, :] = x_ref[:, q * width : (q + 1) * width]
    out_ref[...] = jnp.dot(hot[...], quarters[...], preferred_element_type=F32).astype(BF)


def dispatch(where, ids_row, level_row, x, scaled):
    tokens, d = x.shape
    rows = TEAM * BLK
    return pl.pallas_call(
        functools.partial(dispatch_kernel, scaled=scaled),
        out_shape=travel_type(d),
        in_specs=[pl.BlockSpec(memory_space=pltpu.SMEM)] + [WHOLE] * 3,
        out_specs=WHOLE,
        scratch_shapes=[
            pltpu.VMEM((rows, QUARTERS * tokens), BF),
            pltpu.VMEM((QUARTERS * tokens, d // QUARTERS), BF),
        ],
        compiler_params=params(),
        cost_estimate=cost(2 * rows * tokens * d, 3 * 1024 * 1024),
        name="dispatch",
    )(where, ids_row, level_row, x)


def combine_plane_kernel(where, ids_row, level_row, back, out_ref, *, scaled):
    ids = as_column(ids_row[...])
    base = (ids & 15) * BLK + turn_of(ids, where) * SLOTS + ranks(ids_row[...], ids, 1)
    rows, width = back.shape
    shape = (ids_row.shape[1], rows)
    row = lax.broadcasted_iota(jnp.int32, shape, 1)
    value = gates(as_column(level_row[...]), shape, scaled)
    for q in range(QUARTERS):
        hot = jnp.where(row == base + q * (4 * SLOTS), value, 0.0).astype(BF)
        part = jnp.dot(hot, back[...], preferred_element_type=F32)
        out_ref[:, q * width : (q + 1) * width] = part.astype(BF)


def combine_pairs_kernel(where, ids_row, level_row, *refs, scaled):
    backs, out_ref, rows = refs[:4], refs[4], refs[5]
    ids = as_column(ids_row[...])
    base = turn_of(ids, where) * BLK + (ids & 15) * SLOTS + ranks(ids_row[...], ids, 1)
    shape = (ids_row.shape[1], 4 * BLK)
    gather_rows(backs, rows)
    row = lax.broadcasted_iota(jnp.int32, shape, 1)
    value = gates(as_column(level_row[...]), shape, scaled)
    hot = jnp.where(row == base, value, 0.0).astype(BF)
    out_ref[...] = jnp.dot(hot, rows[...], preferred_element_type=F32).astype(BF)


def combine(where, ids_row, level_row, backs, scaled, d):
    tokens = ids_row.shape[1]
    by_pair = len(backs) == 4
    return pl.pallas_call(
        functools.partial(combine_pairs_kernel if by_pair else combine_plane_kernel, scaled=scaled),
        out_shape=jax.ShapeDtypeStruct((tokens, d), BF),
        in_specs=[pl.BlockSpec(memory_space=pltpu.SMEM)] + [WHOLE] * (2 + len(backs)),
        out_specs=WHOLE,
        scratch_shapes=[rows_scratch(d)] if by_pair else [],
        compiler_params=params(),
        cost_estimate=cost((100 if by_pair else 2) * TEAM * BLK * tokens * d, 3 * 1024 * 1024),
        name="combine",
    )(where, ids_row, level_row, *backs)


def shuffle_kernel(rows_ref, *refs):
    outs, order = refs[:4], refs[4]
    order[...] = one_hot(by_source_of, order.shape[0])
    size = QUARTERS * BLK
    for turn, out in enumerate(outs):
        part = jnp.dot(
            order[turn * size : (turn + 1) * size, :], rows_ref[...], preferred_element_type=F32
        )
        from_pair_order(part.astype(BF), out)


def shuffle(rows):
    rows = rows.reshape(TEAM * BLK, rows.shape[-1])
    count, width = rows.shape
    return pl.pallas_call(
        shuffle_kernel,
        out_shape=block_types(width * QUARTERS),
        in_specs=[WHOLE],
        out_specs=[WHOLE] * 4,
        scratch_shapes=[pltpu.VMEM((count, count), BF)],
        compiler_params=params(),
        cost_estimate=cost(2 * count * count * width, 4 * count * width),
        name="shuffle",
    )(rows)


def unshuffle_kernel(*refs, summed):
    blocks, (out_ref, stack) = refs[:-2], refs[-2:]

    def own(cols):
        if summed:
            return (blocks[0][:, cols].astype(F32) + blocks[4][:, cols].astype(F32)).astype(BF)
        return blocks[0][:, cols]

    others = [lambda cols, block=block: block[:, cols] for block in blocks[1:4]]
    to_source_order([own] + others, stack, out_ref)


def unshuffle(blocks):
    d = blocks[0].shape[1]
    rows = TEAM * BLK
    out = pl.pallas_call(
        functools.partial(unshuffle_kernel, summed=len(blocks) == 5),
        out_shape=travel_type(d),
        in_specs=[WHOLE] * len(blocks),
        out_specs=WHOLE,
        scratch_shapes=[stack_scratch(d)],
        compiler_params=params(),
        cost_estimate=cost(2 * rows * rows * d // QUARTERS, 3 * 1024 * 1024),
        name="unshuffle",
    )(*blocks)
    return parted(out)


def gather_rows(blocks, rows):
    for i, block in enumerate(blocks):
        rows[i * BLK : (i + 1) * BLK, :] = block[...]


def hidden_kernel(b0, b1, b2, b3, wg0, wg1, wu0, wu1, hidden, acts, rows):
    gather_rows((b0, b1, b2, b3), rows)
    ff = wg0.shape[1]
    for i, w in enumerate((wg0, wg1, wu0, wu1)):
        acts[:, i * ff : (i + 1) * ff] = jnp.dot(rows[...], w[...], preferred_element_type=F32)
    gate = acts[:, : 2 * ff]
    hidden[...] = (gate * jax.nn.sigmoid(gate) * acts[:, 2 * ff :]).astype(BF)


def hidden_call(blocks, wg, wu):
    d, ff = wg[0].shape
    count = 4 * BLK
    return pl.pallas_call(
        hidden_kernel,
        out_shape=[
            jax.ShapeDtypeStruct((count, 2 * ff), BF),
            jax.ShapeDtypeStruct((count, 4 * ff), F32),
        ],
        in_specs=[WHOLE] * 8,
        out_specs=[WHOLE] * 2,
        scratch_shapes=[rows_scratch(d)],
        compiler_params=params(),
        cost_estimate=cost(8 * count * d * ff, 12 * 1024 * 1024),
        name="hidden",
    )(*blocks, *wg, *wu)


def hidden_parts(weights):
    place = [0, 0]
    half = sum(w.shape[0] for w in weights) // 2
    for w in weights:
        plane = 0 if place[0] < half else 1
        yield plane, place[plane], w.shape[0]
        place[plane] += w.shape[0]


def d_hidden_kernel(b0, b1, b2, b3, *refs):
    weights, (mine, other, rows) = refs[:-3], refs[-3:]
    gather_rows((b0, b1, b2, b3), rows)
    for w, (plane, first, size) in zip(weights, hidden_parts(weights)):
        part = lax.dot_general(rows[...], w[...], NT, preferred_element_type=F32)
        out = (mine, other)[plane]
        out[:, first : first + size] = part.astype(out.dtype)


def d_hidden_call(blocks, wd):
    d = wd[0].shape[1]
    units = sum(w.shape[0] for w in wd)
    return pl.pallas_call(
        d_hidden_kernel,
        out_shape=[
            jax.ShapeDtypeStruct((4 * BLK, units // 2), F32),
            jax.ShapeDtypeStruct((4 * BLK, units // 2), BF),
        ],
        in_specs=[WHOLE] * (4 + len(wd)),
        out_specs=[WHOLE] * 2,
        scratch_shapes=[rows_scratch(d)],
        compiler_params=params(),
        cost_estimate=cost(8 * BLK * units * d, 12 * 1024 * 1024),
        name="d_hidden",
    )(*blocks, *wd)


def out_kernel(near, other, *refs):
    weights, (out_ref, rows, stack) = refs[:-3], refs[-3:]
    width = rows.shape[1] // 4
    for q in range(4):
        cols = slice(q * width, (q + 1) * width)
        total = None
        for w, (plane, first, size) in zip(weights, hidden_parts(weights)):
            part = jnp.dot(
                (near, other)[plane][:, first : first + size],
                w[:, cols],
                preferred_element_type=F32,
            )
            total = part if total is None else total + part
        rows[:, cols] = total.astype(BF)
    blocks = [lambda cols, i=i: rows[i * BLK : (i + 1) * BLK, cols] for i in range(4)]
    to_source_order(blocks, stack, out_ref)


def out_call(near, other, wd):
    d = wd[0].shape[1]
    rows, units = near.shape
    out = pl.pallas_call(
        out_kernel,
        out_shape=travel_type(d),
        in_specs=[WHOLE] * (2 + len(wd)),
        out_specs=WHOLE,
        scratch_shapes=[rows_scratch(d), stack_scratch(d)],
        compiler_params=params(),
        cost_estimate=cost(4 * rows * d * units, 12 * 1024 * 1024),
        name="expert_out",
    )(near, other, *wd)
    return parted(out)


def grad_kernel(acts, dh, wg0, wg1, wu0, wu1, *refs):
    outs, dacts = refs[:4], refs[4]
    ff = wg0.shape[1]
    gate = acts[:, : 2 * ff]
    up = acts[:, 2 * ff :]
    sigma = jax.nn.sigmoid(gate)
    d_hidden = dh[...].astype(F32)
    d_gate = d_hidden * up * sigma * (1.0 + gate * (1.0 - sigma))
    dacts[:, : 2 * ff] = d_gate.astype(BF)
    dacts[:, 2 * ff :] = (d_hidden * (gate * sigma)).astype(BF)
    width = outs[0].shape[1] // 4
    for q in range(4):
        cols = slice(q * width, (q + 1) * width)
        total = None
        for i, w in enumerate((wg0, wg1, wu0, wu1)):
            part = lax.dot_general(
                dacts[:, i * ff : (i + 1) * ff], w[cols, :], NT, preferred_element_type=F32
            )
            total = part if total is None else total + part
        for i, out in enumerate(outs):
            out[:, cols] = total[i * BLK : (i + 1) * BLK].astype(BF)


def grad_call(acts, dh, wg, wu):
    d, ff = wg[0].shape
    rows = dh.shape[0]
    return pl.pallas_call(
        grad_kernel,
        out_shape=block_types(d),
        in_specs=[WHOLE] * 6,
        out_specs=[WHOLE] * 4,
        scratch_shapes=[pltpu.VMEM((rows, 4 * ff), BF)],
        compiler_params=params(),
        cost_estimate=cost(8 * rows * d * ff, 12 * 1024 * 1024),
        name="expert_grad",
    )(acts, dh, *wg, *wu)


HEADS_STEP = 4


def attention_kernel(q_ref, k_ref, v_ref, do_ref, o_ref, dq_ref, dk_ref, dv_ref, dk_acc, dv_acc):
    step = pl.program_id(0)
    length = k_ref.shape[0]
    scale = HD ** (-0.5)
    k = k_ref[...]
    v = v_ref[...]
    causal = lax.broadcasted_iota(jnp.int32, (length, length), 0) >= lax.broadcasted_iota(
        jnp.int32, (length, length), 1
    )
    dk = None
    dv = None
    for h in range(HEADS_STEP):
        cols = slice(h * HD, (h + 1) * HD)
        q = q_ref[:, cols]
        do = do_ref[:, cols]
        scores = lax.dot_general(q, k, NT, preferred_element_type=F32) * scale
        scores = jnp.where(causal, scores, -1e30)
        raised = jnp.exp(scores - jnp.max(scores, axis=1, keepdims=True))
        probs = raised / jnp.sum(raised, axis=1, keepdims=True)
        rounded = probs.astype(BF)
        o_ref[:, cols] = jnp.dot(rounded, v, preferred_element_type=F32).astype(BF)
        d_probs = lax.dot_general(do, v, NT, preferred_element_type=F32).astype(BF).astype(F32)
        inner = jnp.sum(d_probs * probs, axis=1, keepdims=True)
        d_scores = (probs * (d_probs - inner) * scale).astype(BF)
        dq_ref[:, cols] = jnp.dot(d_scores, k, preferred_element_type=F32).astype(BF)
        dk_part = lax.dot_general(d_scores, q, TN, preferred_element_type=F32)
        dv_part = lax.dot_general(rounded, do, TN, preferred_element_type=F32)
        dk = dk_part if dk is None else dk + dk_part
        dv = dv_part if dv is None else dv + dv_part

    @pl.when(step == 0)
    def _():
        dk_acc[...] = dk
        dv_acc[...] = dv

    @pl.when(step > 0)
    def _():
        dk_acc[...] = dk_acc[...] + dk
        dv_acc[...] = dv_acc[...] + dv

    @pl.when(step == pl.num_programs(0) - 1)
    def _():
        dk_ref[...] = dk_acc[...].astype(BF)
        dv_ref[...] = dv_acc[...].astype(BF)


def attention(queries, keys, values, cotangent):
    length, wide = queries.shape
    head_spec = pl.BlockSpec((length, HEADS_STEP * HD), lambda s: (0, s))
    key_spec = pl.BlockSpec((length, HD), lambda s: (0, 0))
    heads = wide // HD
    return pl.pallas_call(
        attention_kernel,
        out_shape=[
            jax.ShapeDtypeStruct(queries.shape, BF),
            jax.ShapeDtypeStruct(queries.shape, BF),
            jax.ShapeDtypeStruct(keys.shape, BF),
            jax.ShapeDtypeStruct(values.shape, BF),
        ],
        grid=(heads // HEADS_STEP,),
        in_specs=[head_spec, key_spec, key_spec, head_spec],
        out_specs=[head_spec, head_spec, key_spec, key_spec],
        scratch_shapes=[pltpu.VMEM((length, HD), F32)] * 2,
        compiler_params=params(dimension_semantics=("arbitrary",)),
        cost_estimate=cost(14 * heads * length * length * HD, 10 * 1024 * 1024),
        name="attention",
    )(queries, keys, values, cotangent)


def on_device(
    layer_input,
    out_grad,
    expert_ids,
    gate_level,
    w_gate,
    w_up,
    w_down,
    attn_queries,
    attn_keys,
    attn_values,
    attn_grad,
):
    tokens, d = layer_input.shape
    where = jnp.stack([lax.axis_index("dp") // 16, lax.axis_index("tensor") // 2]).astype(jnp.int32)
    ids_row = expert_ids.reshape(1, tokens)
    level_row = gate_level.reshape(1, tokens)
    tie = lax.optimization_barrier

    gate, up, down = w_gate[0], w_up[0], w_down[0]
    down_other = send(down, INNER)
    mates = [send(w, CORES) for w in (gate, up, down)]

    x_sent = dispatch(where, ids_row, level_row, layer_input, False)
    g_sent = dispatch(where, ids_row, level_row, out_grad, True)
    x_rows = plane_exchange(parted(x_sent))
    attended = attention(attn_queries, attn_keys, attn_values, attn_grad)
    x_rows, g_sent, attended, mates = tie((x_rows, g_sent, attended, mates))
    g_rows = plane_exchange(parted(g_sent))
    x_own, x_one, x_two, x_three = shuffle(x_rows)
    x_two_near = send(x_two, NEAR[1])
    x_own_far = send(x_own, INNER)
    x_one, x_three, x_two_near, x_own_far, down_other = tie(
        (x_one, x_three, x_two_near, x_own_far, down_other)
    )
    x_one_near = send(x_one, NEAR[0])
    x_three_near = send(x_three, NEAR[2])
    x_two_far = send(x_two_near, INNER)
    wg, wu = (gate, mates[0]), (up, mates[1])
    g_blocks, x_one_near, x_three_near = tie((shuffle(g_rows), x_one_near, x_three_near))
    down_other_mate = send(down_other, CORES)
    wd = (down, mates[2], down_other, down_other_mate)
    x_one_far = send(x_one_near, INNER)
    x_three_far = send(x_three_near, INNER)
    g_near = [g_blocks[0]] + [send(block, perm) for block, perm in zip(g_blocks[1:], NEAR)]
    hidden_near, acts_near = hidden_call([x_own, x_one_near, x_two_near, x_three_near], wg, wu)
    hidden_far, acts_far = hidden_call([x_own_far, x_one_far, x_two_far, x_three_far], wg, wu)
    hidden_other = send(hidden_far, INNER)

    g_near, hidden_other, hidden_near = tie((g_near, hidden_other, hidden_near))
    dh_near, dh_far = d_hidden_call(g_near, wd)
    dh_other = send(dh_far, INNER)
    terms = grad_call(acts_far, dh_other, wg, wu)

    arrived = [send(term, INNER) for term in terms[1:]]
    near_terms = grad_call(acts_near, dh_near, wg, wu)
    near_terms, hidden_other = tie((near_terms, hidden_other))
    out_sent = out_call(hidden_near, hidden_other, wd)
    out_rows = plane_exchange(out_sent)
    near_terms, own_term, arrived, _ = tie((near_terms, terms[0], arrived, out_sent))
    own_arrived = send(own_term, INNER)
    totals = [(a.astype(F32) + b.astype(F32)).astype(BF) for a, b in zip(near_terms[1:], arrived)]
    backs = [send(total, perm) for total, perm in zip(totals, BACK)]
    (out_own, out_one, out_two, out_three), *backs[1:] = tie((shuffle(out_rows), *backs[1:]))
    grad_rows = plane_exchange(unshuffle([near_terms[0]] + backs + [own_arrived]))
    out_back = [out_own] + [send(b, perm) for b, perm in zip((out_one, out_two, out_three), BACK)]

    moe_out = combine(where, ids_row, level_row, out_back, True, d)
    grad_rows, moe_out = tie((grad_rows, moe_out))
    grad_back = [grad_rows.reshape(TEAM * BLK, d // QUARTERS)]
    grad_x = combine(where, ids_row, level_row, grad_back, False, d)
    attn_out, grad_q, grad_k, grad_v = attended
    return (moe_out, grad_x, attn_out, grad_q, grad_k, grad_v)


def solution(mesh):
    in_specs = (
        P(("dp", "tensor"), None),
        P(("dp", "tensor"), None),
        P(("dp", "tensor"), None),
        P(("dp", "tensor"), None),
        P("dp", None, "tensor"),
        P("dp", None, "tensor"),
        P("dp", "tensor", None),
        P("dp", "tensor"),
        P("dp", "tensor"),
        P("dp", "tensor"),
        P("dp", "tensor"),
    )
    out_specs = (
        P(("dp", "tensor"), None),
        P(("dp", "tensor"), None),
        P("dp", "tensor"),
        P("dp", "tensor"),
        P("dp", "tensor"),
        P("dp", "tensor"),
    )
    return jax.shard_map(
        on_device, mesh=mesh, in_specs=in_specs, out_specs=out_specs, check_vma=False
    )
```
